32 devices in a mesh: group: 4 (over z), ctx: 2 (over x), tensor: 4 (over y, core).
Axes of the slice: x: 2, y: 2, z: 4, core: 2. Of those that a mesh axis runs over, the one named last changes fastest.
Arguments:
- tokens: bfloat16 [4, 3, 1024, 1280], P('group', None, 'ctx'), may hold values from -0.16992188 to 0.16992188
- cotangent: bfloat16 [4, 3, 1024, 1280], P('group', None, 'ctx'), may hold values from -6 to 6
- segments: int32 [4, 3, 1024], P('group'), may hold values from 0 to 7, never falling along the last dimension, each value on 1 to 512 neighbouring positions
- shard_order: int32 [2], replicated, may hold values from 0 to 1, each once
- attention_weights: float32 [4, 1280, 1280], P(None, ('tensor', 'ctx')), may hold values from -0.15625 to 0.15625
- feedforward_weights: float32 [3, 5120, 1280], P(None, ('tensor', 'ctx')), may hold values from -0.15625 to 0.15625
- head_scales: float32 [1280], P(('tensor', 'ctx')), may hold values from 0.8 to 1.6
- hidden_scales: float32 [2, 5120], P(None, ('tensor', 'ctx')), may hold values from 0.5 to 2
- residual_rates: float32 [2, 1280], P(None, 'ctx'), may hold values from 0.1 to 0.8
- attention_first: float32 [4, 4, 1280, 1280], P('group', None, ('tensor', 'ctx')), may hold values from -1.8 to 1.8
- feedforward_first: float32 [4, 3, 5120, 1280], P('group', None, ('tensor', 'ctx')), may hold values from -0.75 to 0.75
- heads_first: float32 [4, 1280], P('group', ('tensor', 'ctx')), may hold values from -24 to 24
- hidden_first: float32 [4, 2, 5120], P('group', None, ('tensor', 'ctx')), may hold values from -0.72 to 0.72
- rates_first: float32 [4, 2, 1280], P('group', None, 'ctx'), may hold values from -4.2 to 4.2
- attention_second: float32 [4, 4, 1280, 1280], P('group', None, ('tensor', 'ctx')), may hold values from 0.12 to 0.48
- feedforward_second: float32 [4, 3, 5120, 1280], P('group', None, ('tensor', 'ctx')), may hold values from 0.02 to 0.08
- heads_second: float32 [4, 1280], P('group', ('tensor', 'ctx')), may hold values from 3 to 12
- hidden_second: float32 [4, 2, 5120], P('group', None, ('tensor', 'ctx')), may hold values from 0.02 to 0.08
- rates_second: float32 [4, 2, 1280], P('group', None, 'ctx'), may hold values from 0.6 to 2.4
- attention_outer: float32 [4, 1280, 1280], P(None, ('tensor', 'ctx')), may hold values from -0.024 to 0.024
- feedforward_outer: float32 [3, 5120, 1280], P(None, ('tensor', 'ctx')), may hold values from -0.024 to 0.024
- heads_outer: float32 [1280], P(('tensor', 'ctx')), may hold values from -0.18 to 0.18
- hidden_outer: float32 [2, 5120], P(None, ('tensor', 'ctx')), may hold values from -0.18 to 0.18
- rates_outer: float32 [2, 1280], P(None, 'ctx'), may hold values from -0.18 to 0.18
Outputs:
- block_output: float32 [4, 3, 1024, 1280], P('group', None, 'ctx')
- input_gradient: float32 [4, 3, 1024, 1280], P('group', None, 'ctx')
- attention_gradient: float32 [4, 4, 1280, 1280], P('group', None, ('tensor', 'ctx'))
- feedforward_gradient: float32 [4, 3, 5120, 1280], P('group', None, ('tensor', 'ctx'))
- heads_gradient: float32 [4, 1280], P('group', ('tensor', 'ctx'))
- hidden_gradient: float32 [4, 2, 5120], P('group', None, ('tensor', 'ctx'))
- rates_gradient: float32 [4, 2, 1280], P('group', None, 'ctx')
- attention_moment: float32 [4, 4, 1280, 1280], P('group', None, ('tensor', 'ctx'))
- feedforward_moment: float32 [4, 3, 5120, 1280], P('group', None, ('tensor', 'ctx'))
- heads_moment: float32 [4, 1280], P('group', ('tensor', 'ctx'))
- hidden_moment: float32 [4, 2, 5120], P('group', None, ('tensor', 'ctx'))
- rates_moment: float32 [4, 2, 1280], P('group', None, 'ctx')
- attention_variance: float32 [4, 4, 1280, 1280], P('group', None, ('tensor', 'ctx'))
- feedforward_variance: float32 [4, 3, 5120, 1280], P('group', None, ('tensor', 'ctx'))
- heads_variance: float32 [4, 1280], P('group', ('tensor', 'ctx'))
- hidden_variance: float32 [4, 2, 5120], P('group', None, ('tensor', 'ctx'))
- rates_variance: float32 [4, 2, 1280], P('group', None, 'ctx')
- attention_momentum: float32 [4, 1280, 1280], P(None, ('tensor', 'ctx'))
- feedforward_momentum: float32 [3, 5120, 1280], P(None, ('tensor', 'ctx'))
- heads_momentum: float32 [1280], P(('tensor', 'ctx'))
- hidden_momentum: float32 [2, 5120], P(None, ('tensor', 'ctx'))
- rates_momentum: float32 [2, 1280], P(None, 'ctx')
- attention_master: float32 [4, 1280, 1280], P(None, ('tensor', 'ctx'))
- feedforward_master: float32 [3, 5120, 1280], P(None, ('tensor', 'ctx'))
- heads_master: float32 [1280], P(('tensor', 'ctx'))
- hidden_master: float32 [2, 5120], P(None, ('tensor', 'ctx'))
- rates_master: float32 [2, 1280], P(None, 'ctx')
The draws below stay inside these ranges and needn't reach their ends.
Inputs may be any that keep to these rules, and one draw needn't show every extreme that they name: `segments`: along each sequence the document number never falls; each document covers 1 to 512 positions and one covers exactly 512. `shard_order`: A permutation: every ctx index appears once.
All inputs are finite; a program needn't handle non-finite values.
Results may differ from the reference program's by a relative error of at most 0.015.
The reference program's roundings to bfloat16 on the way count: a program that leaves them out, or rounds other values in their place, can miss the bound.
Values may be sent and summed in bfloat16 or wider, within the bound.
A program may use at most 384 MiB of HBM per device.

```python
import math
from functools import partial
import jax
import jax.numpy as jnp
import numpy as np
from jax import lax

D = 1280
HEADS = 20
HEAD_DIM = 64
FF = 5120
MB = 3
NDOC = 8
SEQ = 1024
GROUPS = 4
DOC_MOST = 512
N_CTX = 2


def shard_levels(key, extent, cuts, least, top_value):
    def one(dim, blocks):
        heights = jax.random.uniform(jax.random.fold_in(jax.random.fold_in(key, 6), dim), (blocks,), jnp.float32, least / len(cuts), top_value / len(cuts))
        return jnp.repeat(jnp.exp(heights), extent[dim] // blocks).reshape((-1,) + (1,) * (len(extent) - dim - 1))

    level = one(*cuts[0])
    for cut in cuts[1:]:
        level = level * one(*cut)
    return level


def profile(count, total, limit, skew):
    portions = [(1 << 20) // math.isqrt(rank ** skew) + 1 for rank in range(2, count + 1)]
    surplus, given = total - limit - (count - 1), [1] * (count - 1)
    while surplus > 0:
        free = [i for i in range(count - 1) if given[i] < limit]
        whole, left = sum([portions[i] for i in free]), surplus
        for i in free:
            addition = min(limit - given[i], max(1, left * portions[i] // whole), surplus)
            given[i] = given[i] + addition
            surplus = surplus - addition
    return np.array([limit] + given)


def ragged(rng, amount, total, limit, skew):
    if amount == 2:
        one = jax.random.randint(rng, (), max(1, total - limit), min(limit, total - 1) + 1)
        return jnp.stack([one, total - one])
    lengths = jnp.asarray(profile(amount, total, limit, skew), jnp.int32)
    pairs = (amount - 1) // 2
    donor, taker = lengths[1:1 + 2 * pairs:2], lengths[2:2 + 2 * pairs:2]
    room = jnp.minimum(donor - 1, limit - taker)
    passed = jax.random.randint(jax.random.fold_in(rng, 1), (pairs,), 0, 1 << 20) % (room + 1)
    lengths = lengths.at[1:1 + 2 * pairs:2].set(donor - passed).at[2:2 + 2 * pairs:2].set(taker + passed)
    return lengths[jax.random.permutation(jax.random.fold_in(rng, 2), amount)]


def scatter_about(key, extent, spread, most, cuts=(), held_as=jnp.bfloat16):
    loudness = shard_levels(key, extent, cuts, -0.22, 0.18) if cuts else 1.0
    array = jax.random.normal(key, extent, jnp.float32) * spread * loudness
    return jnp.minimum(jnp.maximum(array, -most), most).astype(held_as)


def setup_inputs(seed: int = 0) -> dict:
    streams_of = jax.random.split(jax.random.key(seed), 25)
    return {
        "tokens": scatter_about(streams_of[0], (GROUPS, MB, SEQ, D), 0.028, 0.16992188, ((0, 4), (2, 2))),
        "cotangent": scatter_about(streams_of[1], (GROUPS, MB, SEQ, D), 1.0, 6.0, ((0, 4), (2, 2))),
        "segments": jax.vmap(lambda own: jnp.searchsorted(jnp.cumsum(ragged(own, NDOC, SEQ, DOC_MOST, 2)), jnp.arange(SEQ), side="right"))(jax.random.split(streams_of[2], GROUPS * MB)).reshape((GROUPS, MB, SEQ)).astype(jnp.int32),
        "shard_order": jax.random.permutation(streams_of[3], N_CTX).astype(jnp.int32),
        "attention_weights": scatter_about(streams_of[4], (4, D, D), D ** -0.5, 0.15625, ((1, 8),), jnp.float32),
        "feedforward_weights": scatter_about(streams_of[5], (3, FF, D), D ** -0.5, 0.15625, ((1, 8),), jnp.float32),
        "head_scales": jnp.clip(jnp.exp(math.log(1.6) - 0.6931472 * jax.random.uniform(streams_of[6], (D,), jnp.float32) ** shard_levels(streams_of[6], (D,), ((0, 8),), -0.2, 0.2)), 0.8, 1.6),
        "hidden_scales": jnp.clip(jnp.exp(math.log(2.0) - 1.3862944 * jax.random.uniform(streams_of[7], (2, FF), jnp.float32) ** shard_levels(streams_of[7], (2, FF), ((1, 8),), -0.2, 0.2)), 0.5, 2.0),
        "residual_rates": jnp.clip(jnp.exp(math.log(0.8) - 2.0794415 * jax.random.uniform(streams_of[8], (2, D), jnp.float32) ** shard_levels(streams_of[8], (2, D), ((1, 2),), -0.2, 0.2)), 0.1, 0.8),
        "attention_first": scatter_about(streams_of[9], (GROUPS, 4, D, D), 0.3, 1.8, ((0, 4), (2, 8)), jnp.float32),
        "feedforward_first": scatter_about(streams_of[10], (GROUPS, 3, FF, D), 0.125, 0.75, ((0, 4), (2, 8)), jnp.float32),
        "heads_first": scatter_about(streams_of[11], (GROUPS, D), 4.0, 24.0, ((0, 4), (1, 8)), jnp.float32),
        "hidden_first": scatter_about(streams_of[12], (GROUPS, 2, FF), 0.12, 0.72, ((0, 4), (2, 8)), jnp.float32),
        "rates_first": scatter_about(streams_of[13], (GROUPS, 2, D), 0.7, 4.2, ((0, 4), (2, 2)), jnp.float32),
        "attention_second": jnp.clip(jnp.exp(math.log(0.48) - 1.3862944 * jax.random.uniform(streams_of[14], (GROUPS, 4, D, D), jnp.float32) ** shard_levels(streams_of[14], (GROUPS, 4, D, D), ((0, 4), (2, 8)), -0.2, 0.2)), 0.12, 0.48),
        "feedforward_second": jnp.clip(jnp.exp(math.log(0.08) - 1.3862944 * jax.random.uniform(streams_of[15], (GROUPS, 3, FF, D), jnp.float32) ** shard_levels(streams_of[15], (GROUPS, 3, FF, D), ((0, 4), (2, 8)), -0.2, 0.2)), 0.02, 0.08),
        "heads_second": jnp.clip(jnp.exp(math.log(12.0) - 1.3862944 * jax.random.uniform(streams_of[16], (GROUPS, D), jnp.float32) ** shard_levels(streams_of[16], (GROUPS, D), ((0, 4), (1, 8)), -0.2, 0.2)), 3.0, 12.0),
        "hidden_second": jnp.clip(jnp.exp(math.log(0.08) - 1.3862944 * jax.random.uniform(streams_of[17], (GROUPS, 2, FF), jnp.float32) ** shard_levels(streams_of[17], (GROUPS, 2, FF), ((0, 4), (2, 8)), -0.2, 0.2)), 0.02, 0.08),
        "rates_second": jnp.clip(jnp.exp(math.log(2.4) - 1.3862944 * jax.random.uniform(streams_of[18], (GROUPS, 2, D), jnp.float32) ** shard_levels(streams_of[18], (GROUPS, 2, D), ((0, 4), (2, 2)), -0.2, 0.2)), 0.6, 2.4),
        "attention_outer": scatter_about(streams_of[19], (4, D, D), 0.004, 0.024, ((1, 8),), jnp.float32),
        "feedforward_outer": scatter_about(streams_of[20], (3, FF, D), 0.004, 0.024, ((1, 8),), jnp.float32),
        "heads_outer": scatter_about(streams_of[21], (D,), 0.03, 0.18, ((0, 8),), jnp.float32),
        "hidden_outer": scatter_about(streams_of[22], (2, FF), 0.03, 0.18, ((1, 8),), jnp.float32),
        "rates_outer": scatter_about(streams_of[23], (2, D), 0.03, 0.18, ((1, 2),), jnp.float32),
    }


@jax.custom_vjp
def low(v):
    return lax.optimization_barrier(v.astype(jnp.bfloat16)).astype(jnp.float32)

@jax.custom_vjp
def low_back(v):
    return v

def low_keep(v):
    return (low(v), None)

def low_pass(kept, grad):
    return (grad,)

def back_keep(v):
    return (v, None)

def back_low(kept, grad):
    return (low(grad),)
low.defvjp(low_keep, low_pass)
low_back.defvjp(back_keep, back_low)
EPSILON = 1e-06
BETA_ONE = 0.9
BETA_TWO = 0.95
CORR_ONE = 1.0 - 0.9 ** 4
CORR_TWO = 1.0 - 0.95 ** 4
ADAM_EPS = 1e-08
DECAY = 0.1
MATRIX_RATE = 0.02
SCALE_RATE = 0.3
OUTER_RATE = 0.7
OUTER_MOMENTUM = 0.9
PRECISE = lax.Precision.HIGHEST

def unit_rows(values):
    return values * lax.rsqrt(lax.optimization_barrier(jnp.sum(values * values, axis=-1, keepdims=True)) + EPSILON)

def layer_forward(params, token_row, positions, token_segments):
    attention_weights, feedforward_weights, head_scales, hidden_scales, residual_rates = tuple((low(member) for member in params))
    seq_length = token_row.shape[0]
    model_width = token_row.shape[1]
    projected = jnp.einsum('rd,khd->krh', token_row, attention_weights[:3], precision=PRECISE)
    queries = low_back(projected[0]).reshape(seq_length, HEADS, HEAD_DIM)
    keys_raw = low_back(projected[1]).reshape(seq_length, HEADS, HEAD_DIM)
    values_low = low(low_back(projected[2])).reshape(seq_length, HEADS, HEAD_DIM)
    scale_heads = head_scales.reshape(HEADS, HEAD_DIM)
    query_low = low(unit_rows(queries) * scale_heads * math.sqrt(HEAD_DIM))
    key_low = low(unit_rows(keys_raw) * scale_heads)
    block_rows = min(512, seq_length)

    def attend(block_index):
        row_start = block_index * block_rows
        query_block = lax.dynamic_slice_in_dim(query_low, row_start, block_rows, 0)
        query_place = lax.dynamic_slice_in_dim(positions, row_start, block_rows, 0)
        query_segment = lax.dynamic_slice_in_dim(token_segments, row_start, block_rows, 0)
        scores = low_back(jnp.einsum('qhd,khd->hqk', query_block, key_low, precision=PRECISE))
        allowed = (query_segment[:, None] == token_segments[None, :]) & (positions[None, :] <= query_place[:, None])
        raised = jnp.where(allowed[None], jnp.exp(scores), 0.0)
        row_total = lax.optimization_barrier(jnp.sum(raised, axis=-1))
        summed = low_back(jnp.einsum('hqk,khd->hqd', low(raised), values_low, precision=PRECISE))
        return jnp.transpose(summed / row_total[:, :, None], (1, 0, 2)).reshape(block_rows, model_width)
    mixed = lax.map(jax.checkpoint(attend), jnp.arange(seq_length // block_rows, dtype=jnp.int32))
    heads_low = low(low_back(mixed.reshape(seq_length, model_width)))
    attention_out = low_back(jnp.dot(heads_low, attention_weights[3], precision=PRECISE))
    attention_unit = unit_rows(attention_out)
    after_attention = unit_rows(token_row + residual_rates[0] * (attention_unit - token_row))
    normed_low = low(after_attention)
    gate_up = low_back(jnp.einsum('rd,khd->krh', normed_low, feedforward_weights[:2], precision=PRECISE))
    up_scaled = gate_up[0] * hidden_scales[0]
    gate_scaled = gate_up[1] * hidden_scales[1] * math.sqrt(model_width)
    hidden_low = low(jax.nn.silu(gate_scaled) * up_scaled)
    feed_out = low_back(jnp.dot(hidden_low, feedforward_weights[2], precision=PRECISE))
    feed_unit = unit_rows(feed_out)
    return unit_rows(after_attention + residual_rates[1] * (feed_unit - after_attention))

def adam_step(master, gradient, first_state, second_state, step_rate, is_matrix):
    moment = BETA_ONE * first_state + (1.0 - BETA_ONE) * gradient
    variance = BETA_TWO * second_state + (1.0 - BETA_TWO) * gradient * gradient
    update = moment / CORR_ONE / (jnp.sqrt(variance / CORR_TWO) + ADAM_EPS)
    updated = master - step_rate * (update + DECAY * master)
    if is_matrix:
        updated = unit_rows(updated)
    return (moment, variance, updated)

def outer_step(master, shift, outer_state, is_matrix):
    momentum = OUTER_MOMENTUM * outer_state + shift
    result = master - OUTER_RATE * (shift + OUTER_MOMENTUM * momentum)
    if is_matrix:
        result = unit_rows(result)
    return (momentum, result)

def reference(tokens, cotangent, segments, shard_order, attention_weights, feedforward_weights, head_scales, hidden_scales, residual_rates, attention_first, feedforward_first, heads_first, hidden_first, rates_first, attention_second, feedforward_second, heads_second, hidden_second, rates_second, attention_outer, feedforward_outer, heads_outer, hidden_outer, rates_outer):
    params = (attention_weights, feedforward_weights, head_scales, hidden_scales, residual_rates)
    firsts = (attention_first, feedforward_first, heads_first, hidden_first, rates_first)
    seconds = (attention_second, feedforward_second, heads_second, hidden_second, rates_second)
    outers = (attention_outer, feedforward_outer, heads_outer, hidden_outer, rates_outer)
    matrix_flags = (True, True, False, False, False)
    step_rates = (MATRIX_RATE, MATRIX_RATE, SCALE_RATE, SCALE_RATE, SCALE_RATE)
    rows_local = SEQ // N_CTX
    index_row = jnp.arange(SEQ, dtype=jnp.int32)
    positions = (shard_order[index_row // rows_local] * rows_local + index_row % rows_local).astype(jnp.int32)

    def one_sequence(running, inputs):
        token_row, cotangent_row, segment_row = inputs
        token_segments = segment_row[positions]
        forward = partial(layer_forward, positions=positions, token_segments=token_segments)
        output_row, pullback = jax.vjp(forward, params, token_row)
        param_grads, input_row = pullback(cotangent_row)
        running = tuple((summed_grad + part for summed_grad, part in zip(running, param_grads)))
        return (running, (output_row, input_row))
    output_list = []
    input_list = []
    grad_lists = [[], [], [], [], []]
    moment_lists = [[], [], [], [], []]
    variance_lists = [[], [], [], [], []]
    shift_totals = [jnp.zeros_like(member) for member in params]
    for group_index in range(GROUPS):
        zero_grads = tuple((jnp.zeros_like(member) for member in params))
        group_grads, (output_rows, input_rows) = lax.scan(one_sequence, zero_grads, (tokens[group_index].astype(jnp.float32), cotangent[group_index].astype(jnp.float32), segments[group_index]))
        output_list.append(output_rows)
        input_list.append(input_rows)
        for which in range(5):
            moment, variance, updated = adam_step(params[which], group_grads[which], firsts[which][group_index], seconds[which][group_index], step_rates[which], matrix_flags[which])
            grad_lists[which].append(group_grads[which])
            moment_lists[which].append(moment)
            variance_lists[which].append(variance)
            shift_totals[which] = shift_totals[which] + (params[which] - updated)
    shifts = [total_shift / GROUPS for total_shift in shift_totals]
    momenta = []
    masters = []
    for which in range(5):
        momentum, result = outer_step(params[which], shifts[which], outers[which], matrix_flags[which])
        momenta.append(momentum)
        masters.append(result)
    grads = [jnp.stack(entry) for entry in grad_lists]
    moments = [jnp.stack(entry) for entry in moment_lists]
    variances = [jnp.stack(entry) for entry in variance_lists]
    return (jnp.stack(output_list), jnp.stack(input_list), grads[0], grads[1], grads[2], grads[3], grads[4], moments[0], moments[1], moments[2], moments[3], moments[4], variances[0], variances[1], variances[2], variances[3], variances[4], momenta[0], momenta[1], momenta[2], momenta[3], momenta[4], masters[0], masters[1], masters[2], masters[3], masters[4])
```

```python
from functools import partial
import math

import jax
import jax.numpy as jnp
from jax import lax
from jax.experimental import pallas as pl
from jax.experimental.pallas import tpu as pltpu
from jax.sharding import PartitionSpec as P

HEAD_DIM = 64


EPSILON = 1e-06
BETA_ONE = 0.9
BETA_TWO = 0.95
CORR_ONE = 1.0 - 0.9**4
CORR_TWO = 1.0 - 0.95**4
ADAM_EPS = 1e-08
DECAY = 0.1
MATRIX_RATE = 0.02
SCALE_RATE = 0.3
OUTER_RATE = 0.7
OUTER_MOMENTUM = 0.9
MASKED = -1e30
VMEM_BYTES = 40 * 1024 * 1024
F32 = jnp.float32
LOW = jnp.bfloat16


def unit_rows(values, axis=-1):
    scale = lax.rsqrt(jnp.sum(values * values, axis=axis, keepdims=True) + EPSILON)
    return (values * scale, scale)


def unit_only(values):
    return values * lax.rsqrt(jnp.sum(values * values, axis=-1, keepdims=True) + EPSILON)


def unit_back(unit, scale, upstream, axis=-1):
    return scale * (upstream - unit * jnp.sum(upstream * unit, axis=axis, keepdims=True))


def dot(left, right, contract, out=F32):
    return lax.dot_general(
        left, right, (((contract[0],), (contract[1],)), ((), ())), preferred_element_type=F32
    ).astype(out)


def trade(values, axis, bit):
    count = lax.axis_size(axis)
    return lax.ppermute(values, axis, [(i, i ^ bit) for i in range(count)])


def ordered(first, own, other, axis):
    return jnp.where(
        first,
        jnp.concatenate([own, other], axis=axis),
        jnp.concatenate([other, own], axis=axis),
    )


def split_low(values):
    return lax.optimization_barrier(values.astype(LOW))


def add_low(left, right):
    return left.astype(F32) + right.astype(F32)


def tensor_sum(own_part, other_part):
    from_core = trade(other_part, "tensor", 1)
    pair = split_low(own_part + from_core.astype(F32))
    return add_low(pair, trade(pair, "tensor", 2))


def group_sum(values):
    dtype = values.dtype
    here = lax.axis_index("group")
    last = lax.axis_size("group") - 1
    pair = lax.optimization_barrier(
        add_low(values, lax.ppermute(values, "group", [(0, 1), (3, 2)])).astype(dtype)
    )
    whole = lax.optimization_barrier(
        add_low(pair, lax.ppermute(pair, "group", [(1, 2), (2, 1)])).astype(dtype)
    )
    back = lax.ppermute(whole, "group", [(1, 0), (2, 3)])
    return jnp.where((here == 0) | (here == last), back, whole).astype(F32)


def mask_bias(seg_q, place_q, seg_k, place_k):
    allowed = (seg_k == seg_q) & (place_k <= place_q)
    return jnp.where(allowed, 0.0, MASKED).astype(F32)


def attend_kernel(
    head_count, seg_q, place_q, seg_k, place_k, query, key_value, summed, total, heads, bias
):
    blocks, _, rows = key_value.shape
    width = head_count * HEAD_DIM
    for j in range(blocks):
        part = pl.ds(j * rows, rows)
        bias[part, :] = mask_bias(seg_q[...], place_q[...], seg_k[part, :], place_k[part, :])
    for head in range(head_count):
        cols = pl.ds(head * HEAD_DIM, HEAD_DIM)
        value_cols = pl.ds(width + head * HEAD_DIM, HEAD_DIM)
        block_query = query[cols, :]
        row_total = jnp.zeros((1, query.shape[1]), F32)
        acc = jnp.zeros((HEAD_DIM, query.shape[1]), F32)
        for j in range(blocks):
            scores = dot(key_value[j, cols, :], block_query, (0, 0))
            raised = jnp.exp(scores + bias[pl.ds(j * rows, rows), :])
            row_total = row_total + jnp.sum(raised, axis=0, keepdims=True)
            acc = acc + dot(key_value[j, value_cols, :], raised.astype(LOW), (1, 0))
        summed[cols, :] = acc
        total[pl.ds(head, 1), :] = row_total
        heads[cols, :] = (acc / row_total).astype(LOW)


def attend(head_count, places, query, key_value):
    blocks, _, rows = key_value.shape
    width, count = query.shape
    work = head_count * blocks * rows * count * HEAD_DIM * 4
    return pl.pallas_call(
        partial(attend_kernel, head_count),
        out_shape=(
            jax.ShapeDtypeStruct((width, count), F32),
            jax.ShapeDtypeStruct((head_count, count), F32),
            jax.ShapeDtypeStruct((width, count), LOW),
        ),
        scratch_shapes=[pltpu.VMEM((blocks * rows, count), F32)],
        compiler_params=pltpu.CompilerParams(vmem_limit_bytes=VMEM_BYTES),
        cost_estimate=pl.CostEstimate(
            flops=4 * work, bytes_accessed=6 * width * count, transcendentals=work // 256
        ),
    )(*places, query, key_value)


def attend_back_kernel(
    head_count,
    seg_q,
    place_q,
    seg_k,
    place_k,
    query,
    key_value,
    heads_back,
    summed,
    total,
    query_grad,
    own_grad,
    other_grad,
    bias,
):
    blocks, _, rows = key_value.shape
    width = head_count * HEAD_DIM
    for j in range(blocks):
        part = pl.ds(j * rows, rows)
        bias[part, :] = mask_bias(seg_q[...], place_q[...], seg_k[part, :], place_k[part, :])
    for head in range(head_count):
        cols = pl.ds(head * HEAD_DIM, HEAD_DIM)
        value_cols = pl.ds(width + head * HEAD_DIM, HEAD_DIM)
        block_query = query[cols, :]
        output_back = heads_back[cols, :].astype(F32)
        row_total = total[pl.ds(head, 1), :]
        summed_back = (output_back / row_total).astype(LOW)
        total_back = -jnp.sum(output_back * summed[cols, :], axis=0, keepdims=True) / (
            row_total * row_total
        )
        acc = jnp.zeros((HEAD_DIM, query.shape[1]), F32)
        for j in range(blocks):
            key_part = key_value[j, cols, :]
            scores = dot(key_part, block_query, (0, 0))
            raised = jnp.exp(scores + bias[pl.ds(j * rows, rows), :])
            raised_back = dot(key_value[j, value_cols, :], summed_back, (0, 0))
            score_back = (raised * (raised_back + total_back)).astype(LOW)
            acc = acc + dot(key_part, score_back, (1, 0))
            key_grad = dot(block_query, score_back, (1, 1))
            value_grad = dot(summed_back, raised.astype(LOW), (1, 1))
            if j == 0:
                own_grad[cols, :] = key_grad
                own_grad[value_cols, :] = value_grad
            else:
                other_grad[j - 1, cols, :] = key_grad.astype(other_grad.dtype)
                other_grad[j - 1, value_cols, :] = value_grad.astype(other_grad.dtype)
        query_grad[cols, :] = acc


def attend_back(head_count, places, query, key_value, heads_back, summed, total):
    blocks, both, rows = key_value.shape
    width, count = query.shape
    work = head_count * blocks * rows * count * HEAD_DIM * 2
    return pl.pallas_call(
        partial(attend_back_kernel, head_count),
        out_shape=(
            jax.ShapeDtypeStruct((width, count), F32),
            jax.ShapeDtypeStruct((both, rows), F32),
            jax.ShapeDtypeStruct((blocks - 1, both, rows), LOW if blocks == 2 else F32),
        ),
        scratch_shapes=[pltpu.VMEM((blocks * rows, count), F32)],
        compiler_params=pltpu.CompilerParams(vmem_limit_bytes=VMEM_BYTES),
        cost_estimate=pl.CostEstimate(
            flops=5 * 4 * work, bytes_accessed=16 * width * count, transcendentals=work // 128
        ),
    )(*places, query, key_value, heads_back, summed, total)


def adam_step(master, gradient, first_state, second_state, step_rate, is_matrix):
    moment = BETA_ONE * first_state + (1.0 - BETA_ONE) * gradient
    variance = BETA_TWO * second_state + (1.0 - BETA_TWO) * gradient * gradient
    update = moment / CORR_ONE / (jnp.sqrt(variance / CORR_TWO) + ADAM_EPS)
    updated = master - step_rate * (update + DECAY * master)
    if is_matrix:
        updated = unit_only(updated)
    return (moment, variance, updated)


def outer_step(master, shift, outer_state, is_matrix):
    momentum = OUTER_MOMENTUM * outer_state + shift
    result = master - OUTER_RATE * (shift + OUTER_MOMENTUM * momentum)
    if is_matrix:
        result = unit_only(result)
    return (momentum, result)


def on_device(
    tokens,
    cotangent,
    segments,
    shard_order,
    attention_weights,
    feedforward_weights,
    head_scales,
    hidden_scales,
    residual_rates,
    attention_first,
    feedforward_first,
    heads_first,
    hidden_first,
    rates_first,
    attention_second,
    feedforward_second,
    heads_second,
    hidden_second,
    rates_second,
    attention_outer,
    feedforward_outer,
    heads_outer,
    hidden_outer,
    rates_outer,
):
    micro_count, rows, model_width = tokens.shape[1:]
    half = rows // 2
    ctx_count = lax.axis_size("ctx")
    pair = ctx_count == 2
    group_count = lax.axis_size("group")
    own_rows = attention_weights.shape[1]
    own_units = feedforward_weights.shape[1]
    head_width = own_rows * ctx_count
    head_count = head_width // HEAD_DIM
    units = own_units * ctx_count
    root_head = math.sqrt(HEAD_DIM)
    root_width = math.sqrt(model_width)
    me = lax.axis_index("ctx")
    ctx_first = me == 0
    core_first = lax.rem(lax.axis_index("tensor"), 2) == 0
    even_group = lax.rem(lax.axis_index("group"), 2) == 0
    micros = range(micro_count)

    attention_low = attention_weights.astype(LOW)
    feed_low = feedforward_weights.astype(LOW)
    small_low = jnp.concatenate(
        [head_scales, hidden_scales[0], hidden_scales[1], residual_rates[0], residual_rates[1]]
    ).astype(LOW)
    own_cols = residual_rates.shape[1]
    if pair:
        triple_other = trade(attention_low[:3], "ctx", 1)
        triple_weights = ordered(ctx_first, attention_low[:3], triple_other, 1)
        small_other = trade(small_low, "ctx", 1)
        cuts = [own_rows, own_units, own_units, own_cols, own_cols]
        small_pieces = []
        start = 0
        for which, size in enumerate(cuts):
            mine = small_low[start : start + size].astype(F32)
            theirs = small_other[start : start + size].astype(F32)
            start += size
            if which in (1, 2):
                small_pieces.append(jnp.concatenate([mine, theirs]))
            else:
                small_pieces.append(ordered(ctx_first, mine, theirs, 0))
        scale_heads, scale_up, scale_gate, rate_attention, rate_feed = small_pieces
    else:
        triple_weights = lax.all_gather(attention_low[:3], "ctx", axis=1, tiled=True)
        scale_heads = lax.all_gather(head_scales.astype(LOW), "ctx", axis=0, tiled=True).astype(F32)
        scale_up, scale_gate = lax.all_gather(
            hidden_scales.astype(LOW), "ctx", axis=1, tiled=True
        ).astype(F32)
        rate_attention, rate_feed = lax.all_gather(
            residual_rates.astype(LOW), "ctx", axis=1, tiled=True
        ).astype(F32)
    triple_weights = triple_weights.reshape(3 * head_width, model_width)
    scale_column = scale_heads.reshape(head_count, HEAD_DIM, 1)

    token_halves = tokens[0].reshape(micro_count, 2, half, model_width)
    token_own = jnp.where(core_first, token_halves[:, 0], token_halves[:, 1])
    token_other = jnp.where(core_first, token_halves[:, 1], token_halves[:, 0])
    token_rows = jnp.concatenate([token_own, token_other], axis=1)
    cotangent_halves = cotangent[0].reshape(micro_count, 2, half, model_width)
    cotangent_own = jnp.where(core_first, cotangent_halves[:, 0], cotangent_halves[:, 1])

    if pair:
        block_ids = jnp.stack([me, 1 - me])
    else:
        block_ids = lax.rem(me + jnp.arange(ctx_count, dtype=jnp.int32), ctx_count)
    table = jnp.arange(ctx_count, dtype=jnp.int32)
    order_of = jnp.sum(
        jnp.where(block_ids[:, None] == table[None, :], shard_order[None, :], 0), axis=1
    )
    local = jnp.arange(rows, dtype=jnp.int32)
    local = jnp.where(core_first, local, lax.rem(local + half, rows))
    place_blocks = order_of[:, None] * rows + local[None, :]
    segment_blocks = segments[0].reshape(micro_count, ctx_count, rows)
    segment_blocks = jnp.sum(
        jnp.where(
            (order_of[:, None] == table[None, :])[None, :, :, None], segment_blocks[:, None], 0
        ),
        axis=2,
    )
    segment_blocks = jnp.where(
        core_first,
        segment_blocks,
        jnp.concatenate([segment_blocks[:, :, half:], segment_blocks[:, :, :half]], axis=2),
    )
    places = [
        (
            segment_blocks[b, 0][None, :],
            place_blocks[0][None, :],
            segment_blocks[b].reshape(ctx_count * rows, 1),
            place_blocks.reshape(ctx_count * rows, 1),
        )
        for b in micros
    ]

    queries, key_values = [], []
    query_low = []
    query_units, query_norms, key_units, key_norms = [], [], [], []
    for b in micros:
        projected = dot(triple_weights, token_rows[b], (1, 1)).reshape(
            3, head_count, HEAD_DIM, rows
        )
        query_unit, query_norm = unit_rows(projected[0], axis=1)
        key_unit, key_norm = unit_rows(projected[1], axis=1)
        query_units.append(query_unit)
        query_norms.append(query_norm)
        key_units.append(key_unit)
        key_norms.append(key_norm)
        query_low.append(
            (query_unit * scale_column * root_head).astype(LOW).reshape(head_width, rows)
        )
        key_value = jnp.concatenate(
            [
                (key_unit * scale_column).astype(LOW).reshape(head_width, rows),
                projected[2].astype(LOW).reshape(head_width, rows),
            ],
            axis=0,
        )
        if pair:
            key_values.append(jnp.stack([key_value, trade(key_value, "ctx", 1)]))
        else:
            gathered = lax.all_gather(key_value, "ctx", axis=0)
            key_values.append(jnp.take(gathered, block_ids, axis=0))

    if pair:
        output_source, feed_source, _ = lax.optimization_barrier(
            (attention_low[3], feed_low, key_values[-1])
        )
        output_weights = ordered(ctx_first, output_source, trade(output_source, "ctx", 1), 0)
        part = own_units // 2
        feed_full = []
        for which in (0, 1, 2):
            source = feed_source[which]
            piece = jnp.where(even_group, source[:part], source[part:])
            across = trade(piece, "ctx", 1)
            along = trade(across, "group", 1)
            feed_full.append(
                jnp.concatenate([source, ordered(even_group, across, along, 0)], axis=0)
            )
    else:
        output_weights = lax.all_gather(attention_low[3], "ctx", axis=0, tiled=True)
        feed_full = list(lax.all_gather(feed_low, "ctx", axis=1, tiled=True))
    up_weights, gate_weights, down_weights = feed_full

    summeds, totals, heads_lows = [], [], []
    attention_units, attention_norms, afters, after_norms, normed_rows = [], [], [], [], []
    for b in micros:
        summed, total, heads_low = attend(head_count, places[b], query_low[b], key_values[b])
        summeds.append(summed)
        totals.append(total)
        heads_lows.append(heads_low)
        other_part = dot(heads_low[:, half:], output_weights, (0, 0), LOW)
        own_part = dot(heads_low[:, :half], output_weights, (0, 0))
        attention_unit, attention_norm = unit_rows(tensor_sum(own_part, other_part))
        token_float = token_own[b].astype(F32)
        after, after_norm = unit_rows(
            token_float + rate_attention * (attention_unit - token_float)
        )
        attention_units.append(attention_unit)
        attention_norms.append(attention_norm)
        afters.append(after)
        after_norms.append(after_norm)
        normed_low = split_low(after)
        normed_rows.append(
            jnp.concatenate([normed_low, trade(normed_low, "tensor", 1)], axis=0)
        )

    ups, gates, hidden_rows = [], [], []
    output_pieces, second_backs, feed_back_rows = [], [], []
    feed_rate_term = jnp.zeros((model_width,), F32)
    for b in micros:
        up = dot(normed_rows[b], up_weights, (1, 1))
        gate = dot(normed_rows[b], gate_weights, (1, 1))
        ups.append(up)
        gates.append(gate)
        gate_scaled = gate * scale_gate * root_width
        hidden = (gate_scaled * jax.nn.sigmoid(gate_scaled) * (up * scale_up)).astype(LOW)
        hidden_rows.append(hidden)
        other_part = dot(hidden[half:], down_weights, (1, 0), LOW)
        own_part = dot(hidden[:half], down_weights, (1, 0))
        feed_unit, feed_norm = unit_rows(tensor_sum(own_part, other_part))
        output, output_norm = unit_rows(afters[b] + rate_feed * (feed_unit - afters[b]))
        second_back = unit_back(output, output_norm, cotangent_own[b].astype(F32))
        feed_rate_term = feed_rate_term + jnp.sum(second_back * (feed_unit - afters[b]), axis=0)
        feed_back = split_low(unit_back(feed_unit, feed_norm, second_back * rate_feed))
        second_backs.append(second_back)
        feed_back_rows.append(jnp.concatenate([feed_back, trade(feed_back, "tensor", 1)], axis=0))
        output_pieces.append(ordered(core_first, output, trade(output, "tensor", 1), 0))

    up_back_rows, gate_back_rows = [], []
    first_backs, attention_back_rows = [], []
    up_terms = jnp.zeros((units,), F32)
    gate_terms = jnp.zeros((units,), F32)
    attention_rate_term = jnp.zeros((model_width,), F32)
    for b in micros:
        hidden_back = dot(feed_back_rows[b], down_weights, (1, 1))
        gate_scaled = gates[b] * scale_gate * root_width
        sigmoid_gate = jax.nn.sigmoid(gate_scaled)
        up_back = hidden_back * gate_scaled * sigmoid_gate
        gate_back = (
            hidden_back
            * (ups[b] * scale_up)
            * sigmoid_gate
            * (1.0 + gate_scaled * (1.0 - sigmoid_gate))
        )
        up_terms = up_terms + jnp.sum(up_back * ups[b], axis=0)
        gate_terms = gate_terms + jnp.sum(gate_back * gates[b] * root_width, axis=0)
        up_low = (up_back * scale_up).astype(LOW)
        gate_low = (gate_back * scale_gate * root_width).astype(LOW)
        up_back_rows.append(up_low)
        gate_back_rows.append(gate_low)
        other_part = (
            dot(up_low[half:], up_weights, (1, 0)) + dot(gate_low[half:], gate_weights, (1, 0))
        ).astype(LOW)
        own_part = dot(up_low[:half], up_weights, (1, 0)) + dot(
            gate_low[:half], gate_weights, (1, 0)
        )
        after_grad = second_backs[b] * (1.0 - rate_feed) + tensor_sum(own_part, other_part)
        first_back = unit_back(afters[b], after_norms[b], after_grad)
        first_backs.append(first_back)
        attention_rate_term = attention_rate_term + jnp.sum(
            first_back * (attention_units[b] - token_own[b].astype(F32)), axis=0
        )
        attention_back = split_low(
            unit_back(attention_units[b], attention_norms[b], first_back * rate_attention)
        )
        attention_back_rows.append(
            jnp.concatenate([attention_back, trade(attention_back, "tensor", 1)], axis=0)
        )

    def to_owner(gradient):
        if not pair:
            return lax.psum_scatter(gradient, "ctx", scatter_dimension=0, tiled=True)
        size = gradient.shape[0] // 2
        return gradient[:size] + trade(gradient[size:].astype(LOW), "ctx", 1).astype(F32)

    def to_owner_ordered(gradient):
        if not pair:
            return lax.psum_scatter(gradient, "ctx", scatter_dimension=0, tiled=True)
        size = gradient.shape[0] // 2
        own = jnp.where(ctx_first, gradient[:size], gradient[size:])
        other = jnp.where(ctx_first, gradient[size:], gradient[:size])
        return own + trade(other.astype(LOW), "ctx", 1).astype(F32)

    normed_all = jnp.concatenate(normed_rows, axis=0)
    down_grad = to_owner(
        dot(
            jnp.concatenate(hidden_rows, axis=0), jnp.concatenate(feed_back_rows, axis=0), (0, 0)
        )
    )
    up_grad = to_owner(dot(jnp.concatenate(up_back_rows, axis=0), normed_all, (0, 0)))
    gate_grad = to_owner(dot(jnp.concatenate(gate_back_rows, axis=0), normed_all, (0, 0)))
    output_grad = to_owner_ordered(
        dot(
            jnp.concatenate(heads_lows, axis=1), jnp.concatenate(attention_back_rows, axis=0), (1, 0)
        )
    )

    input_pieces, triples = [], []
    head_terms = jnp.zeros((head_count, HEAD_DIM), F32)
    for b in micros:
        heads_back = dot(output_weights, attention_back_rows[b], (1, 1), LOW)
        query_grad, own_grad, other_grad = attend_back(
            head_count, places[b], query_low[b], key_values[b], heads_back, summeds[b], totals[b]
        )
        if pair:
            side_grad = own_grad + trade(other_grad[0], "ctx", 1).astype(F32)
        else:
            sides = jnp.concatenate([own_grad[None], other_grad], axis=0)
            sides = jnp.take(sides, lax.rem(table - me + ctx_count, ctx_count), axis=0)
            side_grad = lax.psum_scatter(sides, "ctx", scatter_dimension=0)
        query_grad = query_grad.reshape(head_count, HEAD_DIM, rows)
        key_grad = side_grad[:head_width].reshape(head_count, HEAD_DIM, rows)
        head_terms = head_terms + jnp.sum(
            query_grad * query_units[b] * root_head + key_grad * key_units[b], axis=2
        )
        triple = jnp.concatenate(
            [
                unit_back(
                    query_units[b], query_norms[b], query_grad * scale_column * root_head, axis=1
                ).reshape(head_width, rows),
                unit_back(key_units[b], key_norms[b], key_grad * scale_column, axis=1).reshape(
                    head_width, rows
                ),
                side_grad[head_width:],
            ],
            axis=0,
        ).astype(LOW)
        triples.append(triple)
        other_part = dot(triple[:, half:], triple_weights, (0, 0), LOW)
        own_part = dot(triple[:, :half], triple_weights, (0, 0))
        input_own = first_backs[b] * (1.0 - rate_attention) + tensor_sum(own_part, other_part)
        input_pieces.append(ordered(core_first, input_own, trade(input_own, "tensor", 1), 0))

    triple_grad = dot(
        jnp.concatenate(triples, axis=1),
        token_rows.reshape(micro_count * rows, model_width),
        (1, 0),
    ).reshape(3, head_width, model_width)
    attention_grads = [to_owner_ordered(triple_grad[which]) for which in range(3)] + [output_grad]
    feed_grads = [up_grad, gate_grad, down_grad]

    rate_terms = jnp.concatenate([attention_rate_term, feed_rate_term])
    rate_terms = rate_terms + trade(rate_terms, "tensor", 1)
    rate_terms = rate_terms.reshape(2, model_width)
    head_terms = head_terms.reshape(head_width)
    hidden_terms = jnp.stack([up_terms, gate_terms])
    if pair:
        heads_own = jnp.where(ctx_first, head_terms[:own_rows], head_terms[own_rows:])
        heads_other = jnp.where(ctx_first, head_terms[own_rows:], head_terms[:own_rows])
        rates_own = jnp.where(ctx_first, rate_terms[:, :own_cols], rate_terms[:, own_cols:])
        rates_other = jnp.where(ctx_first, rate_terms[:, own_cols:], rate_terms[:, :own_cols])
        flat = jnp.concatenate(
            [heads_other, hidden_terms[:, own_units:].reshape(-1), rates_other.reshape(-1)]
        )
        flat = trade(flat, "ctx", 1)
        heads_grad = heads_own + flat[:own_rows]
        hidden_grad = hidden_terms[:, :own_units] + flat[
            own_rows : own_rows + 2 * own_units
        ].reshape(2, own_units)
        rates_grad = rates_own + flat[own_rows + 2 * own_units :].reshape(2, own_cols)
    else:
        heads_grad = lax.psum_scatter(head_terms, "ctx", scatter_dimension=0, tiled=True)
        hidden_grad = lax.psum_scatter(hidden_terms, "ctx", scatter_dimension=1, tiled=True)
        rates_grad = lax.psum_scatter(rate_terms, "ctx", scatter_dimension=1, tiled=True)

    def matrix_steps(gradients, masters, firsts, seconds, outers):
        moments, variances, momenta, results = [], [], [], []
        for which, gradient in enumerate(gradients):
            master = masters[which]
            moment, variance, updated = adam_step(
                master, gradient, firsts[0, which], seconds[0, which], MATRIX_RATE, True
            )
            shift = group_sum(split_low(master - updated)) / group_count
            momentum, result = outer_step(master, shift, outers[which], True)
            moments.append(moment)
            variances.append(variance)
            momenta.append(momentum)
            results.append(result)
        return (
            jnp.stack(gradients)[None],
            jnp.stack(moments)[None],
            jnp.stack(variances)[None],
            jnp.stack(momenta),
            jnp.stack(results),
        )

    feed_outs = matrix_steps(
        feed_grads, feedforward_weights, feedforward_first, feedforward_second, feedforward_outer
    )
    attention_outs = matrix_steps(
        attention_grads, attention_weights, attention_first, attention_second, attention_outer
    )

    masters = (head_scales, hidden_scales, residual_rates)
    firsts = (heads_first[0], hidden_first[0], rates_first[0])
    seconds = (heads_second[0], hidden_second[0], rates_second[0])
    outers = (heads_outer, hidden_outer, rates_outer)
    small_grads = (heads_grad, hidden_grad, rates_grad)
    small_moments, small_variances, small_shifts = [], [], []
    for which in range(3):
        moment, variance, updated = adam_step(
            masters[which],
            small_grads[which],
            firsts[which],
            seconds[which],
            SCALE_RATE,
            False,
        )
        small_moments.append(moment)
        small_variances.append(variance)
        small_shifts.append((masters[which] - updated).reshape(-1))
    shift_flat = group_sum(jnp.concatenate(small_shifts)) / group_count
    small_momenta, small_results = [], []
    start = 0
    for which in range(3):
        size = masters[which].size
        shift = shift_flat[start : start + size].reshape(masters[which].shape)
        start += size
        momentum, result = outer_step(masters[which], shift, outers[which], False)
        small_momenta.append(momentum)
        small_results.append(result)

    return (
        jnp.stack(output_pieces)[None],
        jnp.stack(input_pieces)[None],
        attention_outs[0],
        feed_outs[0],
        *[entry[None] for entry in small_grads],
        attention_outs[1],
        feed_outs[1],
        *[entry[None] for entry in small_moments],
        attention_outs[2],
        feed_outs[2],
        *[entry[None] for entry in small_variances],
        attention_outs[3],
        feed_outs[3],
        *small_momenta,
        attention_outs[4],
        feed_outs[4],
        *small_results,
    )


def solution(mesh):
    placed = (
        P("group", None, "ctx", None),
        P("group", None, "ctx", None),
        P("group", None, None),
        P(),
        P(None, ("tensor", "ctx"), None),
        P(None, ("tensor", "ctx"), None),
        P(("tensor", "ctx")),
        P(None, ("tensor", "ctx")),
        P(None, "ctx"),
        P("group", None, ("tensor", "ctx"), None),
        P("group", None, ("tensor", "ctx"), None),
        P("group", ("tensor", "ctx")),
        P("group", None, ("tensor", "ctx")),
        P("group", None, "ctx"),
        P("group", None, ("tensor", "ctx"), None),
        P("group", None, ("tensor", "ctx"), None),
        P("group", ("tensor", "ctx")),
        P("group", None, ("tensor", "ctx")),
        P("group", None, "ctx"),
        P(None, ("tensor", "ctx"), None),
        P(None, ("tensor", "ctx"), None),
        P(("tensor", "ctx")),
        P(None, ("tensor", "ctx")),
        P(None, "ctx"),
    )
    return jax.shard_map(
        on_device,
        mesh=mesh,
        in_specs=placed,
        out_specs=(
            P("group", None, "ctx", None),
            P("group", None, "ctx", None),
            P("group", None, ("tensor", "ctx"), None),
            P("group", None, ("tensor", "ctx"), None),
            P("group", ("tensor", "ctx")),
            P("group", None, ("tensor", "ctx")),
            P("group", None, "ctx"),
            P("group", None, ("tensor", "ctx"), None),
            P("group", None, ("tensor", "ctx"), None),
            P("group", ("tensor", "ctx")),
            P("group", None, ("tensor", "ctx")),
            P("group", None, "ctx"),
            P("group", None, ("tensor", "ctx"), None),
            P("group", None, ("tensor", "ctx"), None),
            P("group", ("tensor", "ctx")),
            P("group", None, ("tensor", "ctx")),
            P("group", None, "ctx"),
            P(None, ("tensor", "ctx"), None),
            P(None, ("tensor", "ctx"), None),
            P(("tensor", "ctx")),
            P(None, ("tensor", "ctx")),
            P(None, "ctx"),
            P(None, ("tensor", "ctx"), None),
            P(None, ("tensor", "ctx"), None),
            P(("tensor", "ctx")),
            P(None, ("tensor", "ctx")),
            P(None, "ctx"),
        ),
        check_vma=False,
    )
```

```python
from functools import partial
import math

import jax
import jax.numpy as jnp
from jax import lax
from jax.experimental import pallas as pl
from jax.experimental.pallas import tpu as pltpu
from jax.sharding import PartitionSpec as P

HEAD_DIM = 64


EPSILON = 1e-06
BETA_ONE = 0.9
BETA_TWO = 0.95
CORR_ONE = 1.0 - 0.9**4
CORR_TWO = 1.0 - 0.95**4
ADAM_EPS = 1e-08
DECAY = 0.1
MATRIX_RATE = 0.02
SCALE_RATE = 0.3
OUTER_RATE = 0.7
OUTER_MOMENTUM = 0.9
MASKED = -1e30
VMEM_BYTES = 40 * 1024 * 1024
F32 = jnp.float32
LOW = jnp.bfloat16


def unit_rows(values, axis=-1):
    scale = lax.rsqrt(jnp.sum(values * values, axis=axis, keepdims=True) + EPSILON)
    return (values * scale, scale)


def unit_only(values):
    return values * lax.rsqrt(jnp.sum(values * values, axis=-1, keepdims=True) + EPSILON)


def unit_back(unit, scale, upstream, axis=-1):
    return scale * (upstream - unit * jnp.sum(upstream * unit, axis=axis, keepdims=True))


def dot(left, right, contract, out=F32):
    return lax.dot_general(
        left, right, (((contract[0],), (contract[1],)), ((), ())), preferred_element_type=F32
    ).astype(out)


def trade(values, axis, bit):
    count = lax.axis_size(axis)
    return lax.ppermute(values, axis, [(i, i ^ bit) for i in range(count)])


def ordered(first, own, other, axis):
    return jnp.where(
        first,
        jnp.concatenate([own, other], axis=axis),
        jnp.concatenate([other, own], axis=axis),
    )


def split_low(values):
    return lax.optimization_barrier(values.astype(LOW))


def add_low(left, right):
    return left.astype(F32) + right.astype(F32)


def tensor_sum(own_part, other_part):
    from_core = trade(other_part, "tensor", 1)
    pair = split_low(own_part + from_core.astype(F32))
    return add_low(pair, trade(pair, "tensor", 2))


def group_sum(values):
    dtype = values.dtype
    pair = lax.optimization_barrier(
        add_low(values, lax.ppermute(values, "group", [(0, 1), (3, 2)])).astype(dtype)
    )
    whole = lax.optimization_barrier(
        add_low(pair, lax.ppermute(pair, "group", [(1, 2), (2, 1)])).astype(dtype)
    )
    back = lax.ppermute(whole, "group", [(1, 0), (2, 3)])
    return (whole, back)


def mask_bias(seg_q, place_q, seg_k, place_k):
    allowed = (seg_k == seg_q) & (place_k <= place_q)
    return jnp.where(allowed, 0.0, MASKED).astype(F32)


def attend_kernel(
    head_count, seg_q, place_q, seg_k, place_k, query, key_value, summed, total, heads, bias
):
    blocks, _, rows = key_value.shape
    width = head_count * HEAD_DIM
    for j in range(blocks):
        part = pl.ds(j * rows, rows)
        bias[part, :] = mask_bias(seg_q[...], place_q[...], seg_k[part, :], place_k[part, :])
    for head in range(head_count):
        cols = pl.ds(head * HEAD_DIM, HEAD_DIM)
        value_cols = pl.ds(width + head * HEAD_DIM, HEAD_DIM)
        block_query = query[cols, :]
        row_total = jnp.zeros((1, query.shape[1]), F32)
        acc = jnp.zeros((HEAD_DIM, query.shape[1]), F32)
        for j in range(blocks):
            scores = dot(key_value[j, cols, :], block_query, (0, 0))
            raised = jnp.exp(scores + bias[pl.ds(j * rows, rows), :])
            row_total = row_total + jnp.sum(raised, axis=0, keepdims=True)
            acc = acc + dot(key_value[j, value_cols, :], raised.astype(LOW), (1, 0))
        summed[cols, :] = acc
        total[pl.ds(head, 1), :] = row_total
        heads[cols, :] = (acc / row_total).astype(LOW)


def attend(head_count, places, query, key_value):
    blocks, _, rows = key_value.shape
    width, count = query.shape
    work = head_count * blocks * rows * count * HEAD_DIM * 4
    return pl.pallas_call(
        partial(attend_kernel, head_count),
        out_shape=(
            jax.ShapeDtypeStruct((width, count), F32),
            jax.ShapeDtypeStruct((head_count, count), F32),
            jax.ShapeDtypeStruct((width, count), LOW),
        ),
        scratch_shapes=[pltpu.VMEM((blocks * rows, count), F32)],
        compiler_params=pltpu.CompilerParams(vmem_limit_bytes=VMEM_BYTES),
        cost_estimate=pl.CostEstimate(
            flops=4 * work, bytes_accessed=6 * width * count, transcendentals=work // 256
        ),
    )(*places, query, key_value)


def attend_back_kernel(
    head_count,
    seg_q,
    place_q,
    seg_k,
    place_k,
    query,
    key_value,
    heads_back,
    summed,
    total,
    query_grad,
    own_grad,
    other_grad,
    bias,
):
    blocks, _, rows = key_value.shape
    width = head_count * HEAD_DIM
    for j in range(blocks):
        part = pl.ds(j * rows, rows)
        bias[part, :] = mask_bias(seg_q[...], place_q[...], seg_k[part, :], place_k[part, :])
    for head in range(head_count):
        cols = pl.ds(head * HEAD_DIM, HEAD_DIM)
        value_cols = pl.ds(width + head * HEAD_DIM, HEAD_DIM)
        block_query = query[cols, :]
        output_back = heads_back[cols, :].astype(F32)
        row_total = total[pl.ds(head, 1), :]
        summed_back = (output_back / row_total).astype(LOW)
        total_back = -jnp.sum(output_back * summed[cols, :], axis=0, keepdims=True) / (
            row_total * row_total
        )
        acc = jnp.zeros((HEAD_DIM, query.shape[1]), F32)
        for j in range(blocks):
            key_part = key_value[j, cols, :]
            scores = dot(key_part, block_query, (0, 0))
            raised = jnp.exp(scores + bias[pl.ds(j * rows, rows), :])
            raised_back = dot(key_value[j, value_cols, :], summed_back, (0, 0))
            score_back = (raised * (raised_back + total_back)).astype(LOW)
            acc = acc + dot(key_part, score_back, (1, 0))
            key_grad = dot(block_query, score_back, (1, 1))
            value_grad = dot(summed_back, raised.astype(LOW), (1, 1))
            if j == 0:
                own_grad[cols, :] = key_grad
                own_grad[value_cols, :] = value_grad
            else:
                other_grad[j - 1, cols, :] = key_grad.astype(other_grad.dtype)
                other_grad[j - 1, value_cols, :] = value_grad.astype(other_grad.dtype)
        query_grad[cols, :] = acc


def attend_back(head_count, places, query, key_value, heads_back, summed, total):
    blocks, both, rows = key_value.shape
    width, count = query.shape
    work = head_count * blocks * rows * count * HEAD_DIM * 2
    return pl.pallas_call(
        partial(attend_back_kernel, head_count),
        out_shape=(
            jax.ShapeDtypeStruct((width, count), F32),
            jax.ShapeDtypeStruct((both, rows), F32),
            jax.ShapeDtypeStruct((blocks - 1, both, rows), LOW if blocks == 2 else F32),
        ),
        scratch_shapes=[pltpu.VMEM((blocks * rows, count), F32)],
        compiler_params=pltpu.CompilerParams(vmem_limit_bytes=VMEM_BYTES),
        cost_estimate=pl.CostEstimate(
            flops=5 * 4 * work, bytes_accessed=16 * width * count, transcendentals=work // 128
        ),
    )(*places, query, key_value, heads_back, summed, total)


def adam_step(master, gradient, first_state, second_state, step_rate, is_matrix):
    moment = BETA_ONE * first_state + (1.0 - BETA_ONE) * gradient
    variance = BETA_TWO * second_state + (1.0 - BETA_TWO) * gradient * gradient
    update = moment / CORR_ONE / (jnp.sqrt(variance / CORR_TWO) + ADAM_EPS)
    updated = master - step_rate * (update + DECAY * master)
    if is_matrix:
        updated = unit_only(updated)
    return (moment, variance, updated)


def outer_step(master, shift, outer_state, is_matrix):
    momentum = OUTER_MOMENTUM * outer_state + shift
    result = master - OUTER_RATE * (shift + OUTER_MOMENTUM * momentum)
    if is_matrix:
        result = unit_only(result)
    return (momentum, result)


def row_tile(rows):
    for size in (160, 128):
        if rows % size == 0:
            return size
    return rows


def adam_kernel(has_partner, offset, own, partner, master, first, second, *rest):
    del offset
    gradient_out, moment_out, variance_out, shift_out = rest[-4:]
    gradient = own[...]
    if has_partner:
        gradient = gradient + partner[...].astype(F32)
    moment, variance, updated = adam_step(
        master[0], gradient, first[0, 0], second[0, 0], MATRIX_RATE, True
    )
    gradient_out[0, 0] = gradient
    moment_out[0, 0] = moment
    variance_out[0, 0] = variance
    shift_out[...] = (master[0] - updated).astype(LOW)


def adam_slab(which, own_block, gradient, partner, master, first, second, earlier):
    slabs, rows, width = master.shape
    tile = row_tile(rows)
    steps = rows // tile
    has_partner = partner is not None
    if not has_partner:
        partner = jnp.zeros((tile, width), LOW)
    flat = pl.BlockSpec((tile, width), lambda i, at: (i, 0))
    held = pl.BlockSpec((tile, width), lambda i, at: (at[0] * steps + i, 0))
    once = pl.BlockSpec((tile, width), lambda i, at: (0, 0))
    slab = pl.BlockSpec((1, tile, width), lambda i, at: (which, i, 0))
    grouped = pl.BlockSpec((1, 1, tile, width), lambda i, at: (0, which, i, 0))
    whole = jax.ShapeDtypeStruct((1, slabs, rows, width), F32)
    earlier = () if earlier is None else earlier
    return pl.pallas_call(
        partial(adam_kernel, has_partner),
        grid_spec=pltpu.PrefetchScalarGridSpec(
            num_scalar_prefetch=1,
            grid=(steps,),
            in_specs=[held, flat if has_partner else once, slab, grouped, grouped]
            + [pl.BlockSpec(memory_space=pl.ANY)] * len(earlier),
            out_specs=[grouped, grouped, grouped, flat],
        ),
        out_shape=[whole, whole, whole, jax.ShapeDtypeStruct((rows, width), LOW)],
        input_output_aliases={6 + n: n for n in range(len(earlier))},
        compiler_params=pltpu.CompilerParams(vmem_limit_bytes=VMEM_BYTES),
        cost_estimate=pl.CostEstimate(
            flops=30 * rows * width, bytes_accessed=32 * rows * width, transcendentals=rows * width
        ),
    )(own_block, gradient, partner, master, first, second, *earlier)


def outer_kernel(group_count, at_end, whole, back, master, outer, *rest):
    momentum_out, result_out = rest[-2:]
    shift = jnp.where(at_end[0] == 1, back[...].astype(F32), whole[...].astype(F32)) / group_count
    momentum, result = outer_step(master[0], shift, outer[0], True)
    momentum_out[0] = momentum
    result_out[0] = result


def outer_slab(which, group_count, at_end, whole, back, master, outer, earlier):
    slabs, rows, width = master.shape
    tile = row_tile(rows)
    flat = pl.BlockSpec((tile, width), lambda i, at: (i, 0))
    slab = pl.BlockSpec((1, tile, width), lambda i, at: (which, i, 0))
    result = jax.ShapeDtypeStruct((slabs, rows, width), F32)
    earlier = () if earlier is None else earlier
    return pl.pallas_call(
        partial(outer_kernel, group_count),
        grid_spec=pltpu.PrefetchScalarGridSpec(
            num_scalar_prefetch=1,
            grid=(rows // tile,),
            in_specs=[flat, flat, slab, slab]
            + [pl.BlockSpec(memory_space=pl.ANY)] * len(earlier),
            out_specs=[slab, slab],
        ),
        out_shape=[result, result],
        input_output_aliases={5 + n: n for n in range(len(earlier))},
        compiler_params=pltpu.CompilerParams(vmem_limit_bytes=VMEM_BYTES),
        cost_estimate=pl.CostEstimate(
            flops=20 * rows * width, bytes_accessed=20 * rows * width, transcendentals=rows
        ),
    )(at_end, whole, back, master, outer, *earlier)


def place_kernel(core, own, other, *rest):
    out = rest[-1]

    @pl.when(pl.program_id(0) == 0)
    def _():
        out[0, 0] = own[...]

    @pl.when(pl.program_id(0) == 1)
    def _():
        out[0, 0] = other[...]


def place_rows(which, count, core, own, other, earlier):
    half, width = own.shape
    held = pl.BlockSpec((half, width), lambda i, at: (0, 0))
    earlier = () if earlier is None else (earlier,)
    return pl.pallas_call(
        place_kernel,
        grid_spec=pltpu.PrefetchScalarGridSpec(
            num_scalar_prefetch=1,
            grid=(2,),
            in_specs=[held, held] + [pl.BlockSpec(memory_space=pl.ANY)] * len(earlier),
            out_specs=pl.BlockSpec(
                (1, 1, half, width), lambda i, at: (0, which, lax.rem(at[0] + i, 2), 0)
            ),
        ),
        out_shape=jax.ShapeDtypeStruct((1, count, 2 * half, width), F32),
        input_output_aliases={3: 0} if earlier else {},
        compiler_params=pltpu.CompilerParams(vmem_limit_bytes=VMEM_BYTES),
        cost_estimate=pl.CostEstimate(
            flops=0, bytes_accessed=16 * half * width, transcendentals=0
        ),
    )(core, own, other, *earlier)


def on_device(
    tokens,
    cotangent,
    segments,
    shard_order,
    attention_weights,
    feedforward_weights,
    head_scales,
    hidden_scales,
    residual_rates,
    attention_first,
    feedforward_first,
    heads_first,
    hidden_first,
    rates_first,
    attention_second,
    feedforward_second,
    heads_second,
    hidden_second,
    rates_second,
    attention_outer,
    feedforward_outer,
    heads_outer,
    hidden_outer,
    rates_outer,
):
    micro_count, rows, model_width = tokens.shape[1:]
    half = rows // 2
    ctx_count = lax.axis_size("ctx")
    pair = ctx_count == 2
    group_count = lax.axis_size("group")
    own_rows = attention_weights.shape[1]
    own_units = feedforward_weights.shape[1]
    head_width = own_rows * ctx_count
    head_count = head_width // HEAD_DIM
    units = own_units * ctx_count
    root_head = math.sqrt(HEAD_DIM)
    root_width = math.sqrt(model_width)
    me = lax.axis_index("ctx")
    ctx_first = me == 0
    core_index = lax.rem(lax.axis_index("tensor"), 2).reshape(1)
    core_first = core_index[0] == 0
    even_group = lax.rem(lax.axis_index("group"), 2) == 0
    micros = range(micro_count)

    attention_low = attention_weights.astype(LOW)
    feed_low = feedforward_weights.astype(LOW)
    small_low = jnp.concatenate(
        [head_scales, hidden_scales[0], hidden_scales[1], residual_rates[0], residual_rates[1]]
    ).astype(LOW)
    own_cols = residual_rates.shape[1]
    if pair:
        triple_other = trade(attention_low[:3], "ctx", 1)
        triple_weights = ordered(ctx_first, attention_low[:3], triple_other, 1)
        small_other = trade(small_low, "ctx", 1)
        cuts = [own_rows, own_units, own_units, own_cols, own_cols]
        small_pieces = []
        start = 0
        for which, size in enumerate(cuts):
            mine = small_low[start : start + size].astype(F32)
            theirs = small_other[start : start + size].astype(F32)
            start += size
            if which in (1, 2):
                small_pieces.append(jnp.concatenate([mine, theirs]))
            else:
                small_pieces.append(ordered(ctx_first, mine, theirs, 0))
        scale_heads, scale_up, scale_gate, rate_attention, rate_feed = small_pieces
    else:
        triple_weights = lax.all_gather(attention_low[:3], "ctx", axis=1, tiled=True)
        scale_heads = lax.all_gather(head_scales.astype(LOW), "ctx", axis=0, tiled=True).astype(F32)
        scale_up, scale_gate = lax.all_gather(
            hidden_scales.astype(LOW), "ctx", axis=1, tiled=True
        ).astype(F32)
        rate_attention, rate_feed = lax.all_gather(
            residual_rates.astype(LOW), "ctx", axis=1, tiled=True
        ).astype(F32)
    triple_weights = triple_weights.reshape(3 * head_width, model_width)
    scale_column = scale_heads.reshape(head_count, HEAD_DIM, 1)

    token_halves = tokens[0].reshape(micro_count, 2, half, model_width)
    token_own = jnp.where(core_first, token_halves[:, 0], token_halves[:, 1])
    token_other = jnp.where(core_first, token_halves[:, 1], token_halves[:, 0])
    token_rows = jnp.concatenate([token_own, token_other], axis=1)
    cotangent_halves = cotangent[0].reshape(micro_count, 2, half, model_width)
    cotangent_own = jnp.where(core_first, cotangent_halves[:, 0], cotangent_halves[:, 1])

    if pair:
        block_ids = jnp.stack([me, 1 - me])
    else:
        block_ids = lax.rem(me + jnp.arange(ctx_count, dtype=jnp.int32), ctx_count)
    table = jnp.arange(ctx_count, dtype=jnp.int32)
    order_of = jnp.sum(
        jnp.where(block_ids[:, None] == table[None, :], shard_order[None, :], 0), axis=1
    )
    local = jnp.arange(rows, dtype=jnp.int32)
    local = jnp.where(core_first, local, lax.rem(local + half, rows))
    place_blocks = order_of[:, None] * rows + local[None, :]
    segment_blocks = segments[0].reshape(micro_count, ctx_count, rows)
    segment_blocks = jnp.sum(
        jnp.where(
            (order_of[:, None] == table[None, :])[None, :, :, None], segment_blocks[:, None], 0
        ),
        axis=2,
    )
    segment_blocks = jnp.where(
        core_first,
        segment_blocks,
        jnp.concatenate([segment_blocks[:, :, half:], segment_blocks[:, :, :half]], axis=2),
    )
    places = [
        (
            segment_blocks[b, 0][None, :],
            place_blocks[0][None, :],
            segment_blocks[b].reshape(ctx_count * rows, 1),
            place_blocks.reshape(ctx_count * rows, 1),
        )
        for b in micros
    ]

    queries, key_values = [], []
    query_low = []
    query_units, query_norms, key_units, key_norms = [], [], [], []
    for b in micros:
        projected = dot(triple_weights, token_rows[b], (1, 1)).reshape(
            3, head_count, HEAD_DIM, rows
        )
        query_unit, query_norm = unit_rows(projected[0], axis=1)
        key_unit, key_norm = unit_rows(projected[1], axis=1)
        query_units.append(query_unit)
        query_norms.append(query_norm)
        key_units.append(key_unit)
        key_norms.append(key_norm)
        query_low.append(
            (query_unit * scale_column * root_head).astype(LOW).reshape(head_width, rows)
        )
        key_value = jnp.concatenate(
            [
                (key_unit * scale_column).astype(LOW).reshape(head_width, rows),
                projected[2].astype(LOW).reshape(head_width, rows),
            ],
            axis=0,
        )
        if pair:
            key_values.append(jnp.stack([key_value, trade(key_value, "ctx", 1)]))
        else:
            gathered = lax.all_gather(key_value, "ctx", axis=0)
            key_values.append(jnp.take(gathered, block_ids, axis=0))

    if pair:
        output_source, feed_source, _ = lax.optimization_barrier(
            (attention_low[3], feed_low, key_values[-1])
        )
        output_weights = ordered(ctx_first, output_source, trade(output_source, "ctx", 1), 0)
        part = own_units // 2
        feed_full = []
        for which in (0, 1, 2):
            source = feed_source[which]
            piece = jnp.where(even_group, source[:part], source[part:])
            across = trade(piece, "ctx", 1)
            along = trade(across, "group", 1)
            feed_full.append(
                jnp.concatenate([source, ordered(even_group, across, along, 0)], axis=0)
            )
    else:
        output_weights = lax.all_gather(attention_low[3], "ctx", axis=0, tiled=True)
        feed_full = list(lax.all_gather(feed_low, "ctx", axis=1, tiled=True))
    up_weights, gate_weights, down_weights = feed_full

    summeds, totals, heads_lows = [], [], []
    attention_units, attention_norms, afters, after_norms, normed_rows = [], [], [], [], []
    for b in micros:
        summed, total, heads_low = attend(head_count, places[b], query_low[b], key_values[b])
        summeds.append(summed)
        totals.append(total)
        heads_lows.append(heads_low)
        other_part = dot(heads_low[:, half:], output_weights, (0, 0), LOW)
        own_part = dot(heads_low[:, :half], output_weights, (0, 0))
        attention_unit, attention_norm = unit_rows(tensor_sum(own_part, other_part))
        token_float = token_own[b].astype(F32)
        after, after_norm = unit_rows(
            token_float + rate_attention * (attention_unit - token_float)
        )
        attention_units.append(attention_unit)
        attention_norms.append(attention_norm)
        afters.append(after)
        after_norms.append(after_norm)
        normed_low = split_low(after)
        normed_rows.append(
            jnp.concatenate([normed_low, trade(normed_low, "tensor", 1)], axis=0)
        )

    ups, gates, hidden_rows = [], [], []
    second_backs, feed_back_rows = [], []
    block_output = None
    feed_rate_term = jnp.zeros((model_width,), F32)
    for b in micros:
        up = dot(normed_rows[b], up_weights, (1, 1))
        gate = dot(normed_rows[b], gate_weights, (1, 1))
        ups.append(up)
        gates.append(gate)
        gate_scaled = gate * scale_gate * root_width
        hidden = (gate_scaled * jax.nn.sigmoid(gate_scaled) * (up * scale_up)).astype(LOW)
        hidden_rows.append(hidden)
        other_part = dot(hidden[half:], down_weights, (1, 0), LOW)
        own_part = dot(hidden[:half], down_weights, (1, 0))
        feed_unit, feed_norm = unit_rows(tensor_sum(own_part, other_part))
        output, output_norm = unit_rows(afters[b] + rate_feed * (feed_unit - afters[b]))
        second_back = unit_back(output, output_norm, cotangent_own[b].astype(F32))
        feed_rate_term = feed_rate_term + jnp.sum(second_back * (feed_unit - afters[b]), axis=0)
        feed_back = split_low(unit_back(feed_unit, feed_norm, second_back * rate_feed))
        second_backs.append(second_back)
        feed_back_rows.append(jnp.concatenate([feed_back, trade(feed_back, "tensor", 1)], axis=0))
        block_output = place_rows(
            b, micro_count, core_index, output, trade(output, "tensor", 1), block_output
        )

    up_back_rows, gate_back_rows = [], []
    first_backs, attention_back_rows = [], []
    up_terms = jnp.zeros((units,), F32)
    gate_terms = jnp.zeros((units,), F32)
    attention_rate_term = jnp.zeros((model_width,), F32)
    for b in micros:
        hidden_back = dot(feed_back_rows[b], down_weights, (1, 1))
        gate_scaled = gates[b] * scale_gate * root_width
        sigmoid_gate = jax.nn.sigmoid(gate_scaled)
        up_back = hidden_back * gate_scaled * sigmoid_gate
        gate_back = (
            hidden_back
            * (ups[b] * scale_up)
            * sigmoid_gate
            * (1.0 + gate_scaled * (1.0 - sigmoid_gate))
        )
        up_terms = up_terms + jnp.sum(up_back * ups[b], axis=0)
        gate_terms = gate_terms + jnp.sum(gate_back * gates[b] * root_width, axis=0)
        up_low = (up_back * scale_up).astype(LOW)
        gate_low = (gate_back * scale_gate * root_width).astype(LOW)
        up_back_rows.append(up_low)
        gate_back_rows.append(gate_low)
        other_part = (
            dot(up_low[half:], up_weights, (1, 0)) + dot(gate_low[half:], gate_weights, (1, 0))
        ).astype(LOW)
        own_part = dot(up_low[:half], up_weights, (1, 0)) + dot(
            gate_low[:half], gate_weights, (1, 0)
        )
        after_grad = second_backs[b] * (1.0 - rate_feed) + tensor_sum(own_part, other_part)
        first_back = unit_back(afters[b], after_norms[b], after_grad)
        first_backs.append(first_back)
        attention_rate_term = attention_rate_term + jnp.sum(
            first_back * (attention_units[b] - token_own[b].astype(F32)), axis=0
        )
        attention_back = split_low(
            unit_back(attention_units[b], attention_norms[b], first_back * rate_attention)
        )
        attention_back_rows.append(
            jnp.concatenate([attention_back, trade(attention_back, "tensor", 1)], axis=0)
        )

    def to_owner(gradient, in_order):
        if not pair:
            summed_rows = lax.psum_scatter(gradient, "ctx", scatter_dimension=0, tiled=True)
            return (summed_rows, None, jnp.zeros((1,), jnp.int32))
        size = gradient.shape[0] // 2
        other = gradient[size:]
        block = jnp.zeros((1,), jnp.int32)
        if in_order:
            other = jnp.where(ctx_first, gradient[size:], gradient[:size])
            block = me.reshape(1)
        return (gradient, trade(other.astype(LOW), "ctx", 1), block)

    normed_all = jnp.concatenate(normed_rows, axis=0)
    down_grad = to_owner(
        dot(
            jnp.concatenate(hidden_rows, axis=0), jnp.concatenate(feed_back_rows, axis=0), (0, 0)
        ),
        False,
    )
    up_grad = to_owner(dot(jnp.concatenate(up_back_rows, axis=0), normed_all, (0, 0)), False)
    gate_grad = to_owner(dot(jnp.concatenate(gate_back_rows, axis=0), normed_all, (0, 0)), False)
    output_grad = to_owner(
        dot(
            jnp.concatenate(heads_lows, axis=1), jnp.concatenate(attention_back_rows, axis=0), (1, 0)
        ),
        True,
    )

    triples = []
    input_gradient = None
    head_terms = jnp.zeros((head_count, HEAD_DIM), F32)
    for b in micros:
        heads_back = dot(output_weights, attention_back_rows[b], (1, 1), LOW)
        query_grad, own_grad, other_grad = attend_back(
            head_count, places[b], query_low[b], key_values[b], heads_back, summeds[b], totals[b]
        )
        if pair:
            side_grad = own_grad + trade(other_grad[0], "ctx", 1).astype(F32)
        else:
            sides = jnp.concatenate([own_grad[None], other_grad], axis=0)
            sides = jnp.take(sides, lax.rem(table - me + ctx_count, ctx_count), axis=0)
            side_grad = lax.psum_scatter(sides, "ctx", scatter_dimension=0)
        query_grad = query_grad.reshape(head_count, HEAD_DIM, rows)
        key_grad = side_grad[:head_width].reshape(head_count, HEAD_DIM, rows)
        head_terms = head_terms + jnp.sum(
            query_grad * query_units[b] * root_head + key_grad * key_units[b], axis=2
        )
        triple = jnp.concatenate(
            [
                unit_back(
                    query_units[b], query_norms[b], query_grad * scale_column * root_head, axis=1
                ).reshape(head_width, rows),
                unit_back(key_units[b], key_norms[b], key_grad * scale_column, axis=1).reshape(
                    head_width, rows
                ),
                side_grad[head_width:],
            ],
            axis=0,
        ).astype(LOW)
        triples.append(triple)
        other_part = dot(triple[:, half:], triple_weights, (0, 0), LOW)
        own_part = dot(triple[:, :half], triple_weights, (0, 0))
        input_own = first_backs[b] * (1.0 - rate_attention) + tensor_sum(own_part, other_part)
        input_gradient = place_rows(
            b, micro_count, core_index, input_own, trade(input_own, "tensor", 1), input_gradient
        )

    triple_grad = dot(
        jnp.concatenate(triples, axis=1),
        token_rows.reshape(micro_count * rows, model_width),
        (1, 0),
    ).reshape(3, head_width, model_width)
    attention_grads = [to_owner(triple_grad[which], True) for which in range(3)] + [output_grad]
    feed_grads = [up_grad, gate_grad, down_grad]

    rate_terms = jnp.concatenate([attention_rate_term, feed_rate_term])
    rate_terms = rate_terms + trade(rate_terms, "tensor", 1)
    rate_terms = rate_terms.reshape(2, model_width)
    head_terms = head_terms.reshape(head_width)
    hidden_terms = jnp.stack([up_terms, gate_terms])
    if pair:
        heads_own = jnp.where(ctx_first, head_terms[:own_rows], head_terms[own_rows:])
        heads_other = jnp.where(ctx_first, head_terms[own_rows:], head_terms[:own_rows])
        rates_own = jnp.where(ctx_first, rate_terms[:, :own_cols], rate_terms[:, own_cols:])
        rates_other = jnp.where(ctx_first, rate_terms[:, own_cols:], rate_terms[:, :own_cols])
        flat = jnp.concatenate(
            [heads_other, hidden_terms[:, own_units:].reshape(-1), rates_other.reshape(-1)]
        )
        flat = trade(flat, "ctx", 1)
        heads_grad = heads_own + flat[:own_rows]
        hidden_grad = hidden_terms[:, :own_units] + flat[
            own_rows : own_rows + 2 * own_units
        ].reshape(2, own_units)
        rates_grad = rates_own + flat[own_rows + 2 * own_units :].reshape(2, own_cols)
    else:
        heads_grad = lax.psum_scatter(head_terms, "ctx", scatter_dimension=0, tiled=True)
        hidden_grad = lax.psum_scatter(hidden_terms, "ctx", scatter_dimension=1, tiled=True)
        rates_grad = lax.psum_scatter(rate_terms, "ctx", scatter_dimension=1, tiled=True)

    at_end = lax.axis_index("group")
    at_end = ((at_end == 0) | (at_end == group_count - 1)).astype(jnp.int32)

    def matrix_steps(order, gradients, masters, firsts, seconds, outers):
        adam_outs, outer_outs = None, None
        for which in order:
            gradient, partner, block = gradients[which]
            *adam_outs, shift = adam_slab(
                which, block, gradient, partner, masters, firsts, seconds, adam_outs
            )
            whole, back = group_sum(shift)
            outer_outs = outer_slab(
                which, group_count, at_end.reshape(1), whole, back, masters, outers, outer_outs
            )
        return (*adam_outs, *outer_outs)

    feed_outs = matrix_steps(
        (2, 0, 1), feed_grads, feedforward_weights, feedforward_first, feedforward_second, feedforward_outer
    )
    attention_outs = matrix_steps(
        (3, 0, 1, 2), attention_grads, attention_weights, attention_first, attention_second, attention_outer
    )

    masters = (head_scales, hidden_scales, residual_rates)
    firsts = (heads_first[0], hidden_first[0], rates_first[0])
    seconds = (heads_second[0], hidden_second[0], rates_second[0])
    outers = (heads_outer, hidden_outer, rates_outer)
    small_grads = (heads_grad, hidden_grad, rates_grad)
    small_moments, small_variances, small_shifts = [], [], []
    for which in range(3):
        moment, variance, updated = adam_step(
            masters[which],
            small_grads[which],
            firsts[which],
            seconds[which],
            SCALE_RATE,
            False,
        )
        small_moments.append(moment)
        small_variances.append(variance)
        small_shifts.append((masters[which] - updated).reshape(-1))
    whole, back = group_sum(jnp.concatenate(small_shifts))
    shift_flat = jnp.where(at_end == 1, back, whole) / group_count
    small_momenta, small_results = [], []
    start = 0
    for which in range(3):
        size = masters[which].size
        shift = shift_flat[start : start + size].reshape(masters[which].shape)
        start += size
        momentum, result = outer_step(masters[which], shift, outers[which], False)
        small_momenta.append(momentum)
        small_results.append(result)

    return (
        block_output,
        input_gradient,
        attention_outs[0],
        feed_outs[0],
        *[entry[None] for entry in small_grads],
        attention_outs[1],
        feed_outs[1],
        *[entry[None] for entry in small_moments],
        attention_outs[2],
        feed_outs[2],
        *[entry[None] for entry in small_variances],
        attention_outs[3],
        feed_outs[3],
        *small_momenta,
        attention_outs[4],
        feed_outs[4],
        *small_results,
    )


def solution(mesh):
    placed = (
        P("group", None, "ctx", None),
        P("group", None, "ctx", None),
        P("group", None, None),
        P(),
        P(None, ("tensor", "ctx"), None),
        P(None, ("tensor", "ctx"), None),
        P(("tensor", "ctx")),
        P(None, ("tensor", "ctx")),
        P(None, "ctx"),
        P("group", None, ("tensor", "ctx"), None),
        P("group", None, ("tensor", "ctx"), None),
        P("group", ("tensor", "ctx")),
        P("group", None, ("tensor", "ctx")),
        P("group", None, "ctx"),
        P("group", None, ("tensor", "ctx"), None),
        P("group", None, ("tensor", "ctx"), None),
        P("group", ("tensor", "ctx")),
        P("group", None, ("tensor", "ctx")),
        P("group", None, "ctx"),
        P(None, ("tensor", "ctx"), None),
        P(None, ("tensor", "ctx"), None),
        P(("tensor", "ctx")),
        P(None, ("tensor", "ctx")),
        P(None, "ctx"),
    )
    return jax.shard_map(
        on_device,
        mesh=mesh,
        in_specs=placed,
        out_specs=(
            P("group", None, "ctx", None),
            P("group", None, "ctx", None),
            P("group", None, ("tensor", "ctx"), None),
            P("group", None, ("tensor", "ctx"), None),
            P("group", ("tensor", "ctx")),
            P("group", None, ("tensor", "ctx")),
            P("group", None, "ctx"),
            P("group", None, ("tensor", "ctx"), None),
            P("group", None, ("tensor", "ctx"), None),
            P("group", ("tensor", "ctx")),
            P("group", None, ("tensor", "ctx")),
            P("group", None, "ctx"),
            P("group", None, ("tensor", "ctx"), None),
            P("group", None, ("tensor", "ctx"), None),
            P("group", ("tensor", "ctx")),
            P("group", None, ("tensor", "ctx")),
            P("group", None, "ctx"),
            P(None, ("tensor", "ctx"), None),
            P(None, ("tensor", "ctx"), None),
            P(("tensor", "ctx")),
            P(None, ("tensor", "ctx")),
            P(None, "ctx"),
            P(None, ("tensor", "ctx"), None),
            P(None, ("tensor", "ctx"), None),
            P(("tensor", "ctx")),
            P(None, ("tensor", "ctx")),
            P(None, "ctx"),
        ),
        check_vma=False,
    )
```

```python
from functools import partial
import math

import jax
import jax.numpy as jnp
from jax import lax
from jax.experimental import pallas as pl
from jax.experimental.pallas import tpu as pltpu
from jax.sharding import PartitionSpec as P

HEAD_DIM = 64


EPSILON = 1e-06
BETA_ONE = 0.9
BETA_TWO = 0.95
CORR_ONE = 1.0 - 0.9**4
CORR_TWO = 1.0 - 0.95**4
ADAM_EPS = 1e-08
DECAY = 0.1
MATRIX_RATE = 0.02
SCALE_RATE = 0.3
OUTER_RATE = 0.7
OUTER_MOMENTUM = 0.9
MASKED = -1e30
VMEM_BYTES = 40 * 1024 * 1024
LARGE_VMEM_BYTES = 56 * 1024 * 1024
F32 = jnp.float32
LOW = jnp.bfloat16


def unit_rows(values, axis=-1):
    scale = lax.rsqrt(jnp.sum(values * values, axis=axis, keepdims=True) + EPSILON)
    return (values * scale, scale)


def unit_only(values):
    return values * lax.rsqrt(jnp.sum(values * values, axis=-1, keepdims=True) + EPSILON)


def unit_back(unit, scale, upstream, axis=-1):
    return scale * (upstream - unit * jnp.sum(upstream * unit, axis=axis, keepdims=True))


def dot(left, right, contract, out=F32):
    return lax.dot_general(
        left, right, (((contract[0],), (contract[1],)), ((), ())), preferred_element_type=F32
    ).astype(out)


def trade(values, axis, bit):
    count = lax.axis_size(axis)
    return lax.ppermute(values, axis, [(i, i ^ bit) for i in range(count)])


def ordered(first, own, other, axis):
    return jnp.where(
        first,
        jnp.concatenate([own, other], axis=axis),
        jnp.concatenate([other, own], axis=axis),
    )


def split_low(values):
    return lax.optimization_barrier(values.astype(LOW))


def add_low(left, right):
    return left.astype(F32) + right.astype(F32)


def ordered_after(body, count, deps):
    def wrapped(*refs):
        return body(*refs[:count], *refs[count + len(deps) :])

    return wrapped


UNREAD = pl.BlockSpec(memory_space=pl.ANY)
IN_VMEM = pl.BlockSpec(memory_space=pltpu.VMEM)


def tie_kernel(*refs):
    del refs


def tie(values, *deps):
    return pl.pallas_call(
        tie_kernel,
        in_specs=[UNREAD] * (1 + len(deps)),
        out_specs=UNREAD,
        out_shape=jax.ShapeDtypeStruct(values.shape, values.dtype),
        input_output_aliases={0: 0},
    )(values, *deps)


def tensor_sum(own_part, other_part):
    from_core = trade(other_part, "tensor", 1)
    pair = split_low(own_part + from_core.astype(F32))
    return (pair, trade(pair, "tensor", 2))


def group_sum(values):
    dtype = values.dtype
    pair = lax.optimization_barrier(
        add_low(values, lax.ppermute(values, "group", [(0, 1), (3, 2)])).astype(dtype)
    )
    whole = lax.optimization_barrier(
        add_low(pair, lax.ppermute(pair, "group", [(1, 2), (2, 1)])).astype(dtype)
    )
    back = lax.ppermute(whole, "group", [(1, 0), (2, 3)])
    return (pair, whole, back)


def mask_bias(seg_q, place_q, seg_k, place_k):
    allowed = (seg_k == seg_q) & (place_k <= place_q)
    return jnp.where(allowed, 0.0, MASKED).astype(F32)


def project_kernel(head_count, weights, own, other, scale, projected, query_low, key_value):
    width = head_count * HEAD_DIM
    rows = jnp.concatenate([own[...], other[...]], axis=0)
    projected[...] = dot(weights[...], rows, (1, 1))
    for head in range(head_count):
        cols = pl.ds(head * HEAD_DIM, HEAD_DIM)
        key_cols = pl.ds(width + head * HEAD_DIM, HEAD_DIM)
        head_scale = scale[cols, :]
        query_unit, _ = unit_rows(projected[cols, :], axis=0)
        key_unit, _ = unit_rows(projected[key_cols, :], axis=0)
        query_low[cols, :] = (query_unit * head_scale * math.sqrt(HEAD_DIM)).astype(LOW)
        key_value[cols, :] = (key_unit * head_scale).astype(LOW)
    key_value[width : 2 * width, :] = projected[2 * width : 3 * width, :].astype(LOW)


def project(head_count, weights, own, other, scale, deps=()):
    total, model_width = weights.shape
    width = head_count * HEAD_DIM
    rows = own.shape[0] + other.shape[0]
    return pl.pallas_call(
        ordered_after(partial(project_kernel, head_count), 4, deps),
        in_specs=[IN_VMEM] * 4 + [UNREAD] * len(deps),
        out_shape=[
            jax.ShapeDtypeStruct((total, rows), F32),
            jax.ShapeDtypeStruct((width, rows), LOW),
            jax.ShapeDtypeStruct((2 * width, rows), LOW),
        ],
        compiler_params=pltpu.CompilerParams(vmem_limit_bytes=VMEM_BYTES),
        cost_estimate=pl.CostEstimate(
            flops=2 * total * rows * model_width,
            bytes_accessed=2 * total * model_width + 6 * total * rows,
            transcendentals=0,
        ),
    )(weights, own, other, scale, *deps)


def sides_kernel(head_count, has_partner, own, arrived, query_grad, projected, scale, triple, terms):
    width = head_count * HEAD_DIM
    root_head = math.sqrt(HEAD_DIM)

    def side(cols):
        gradient = own[cols, :]
        if has_partner:
            gradient = gradient + arrived[cols, :].astype(F32)
        return gradient

    for head in range(head_count):
        cols = pl.ds(head * HEAD_DIM, HEAD_DIM)
        key_cols = pl.ds(width + head * HEAD_DIM, HEAD_DIM)
        head_scale = scale[cols, :]
        query_unit, query_norm = unit_rows(projected[cols, :], axis=0)
        key_unit, key_norm = unit_rows(projected[key_cols, :], axis=0)
        query_scaled = query_grad[cols, :] * root_head
        key_scaled = side(cols)
        terms[cols, :] = jnp.sum(
            query_scaled * query_unit + key_scaled * key_unit, axis=1, keepdims=True
        )
        triple[cols, :] = unit_back(
            query_unit, query_norm, query_scaled * head_scale, axis=0
        ).astype(LOW)
        triple[key_cols, :] = unit_back(
            key_unit, key_norm, key_scaled * head_scale, axis=0
        ).astype(LOW)
    triple[2 * width : 3 * width, :] = side(pl.ds(width, width)).astype(LOW)


def sides_back(head_count, own, arrived, query_grad, projected, scale, deps=()):
    total, rows = projected.shape
    width = head_count * HEAD_DIM
    has_partner = arrived is not None
    if not has_partner:
        arrived = jnp.zeros((16, rows), LOW)
    return pl.pallas_call(
        ordered_after(partial(sides_kernel, head_count, has_partner), 5, deps),
        in_specs=[IN_VMEM] * 5 + [UNREAD] * len(deps),
        out_shape=[
            jax.ShapeDtypeStruct((total, rows), LOW),
            jax.ShapeDtypeStruct((width, 1), F32),
        ],
        compiler_params=pltpu.CompilerParams(vmem_limit_bytes=VMEM_BYTES),
        cost_estimate=pl.CostEstimate(
            flops=40 * total * rows, bytes_accessed=14 * total * rows, transcendentals=rows
        ),
    )(own, arrived, query_grad, projected, scale, *deps)


def triple_grad_kernel(count, parts, own_part, me, *refs):
    lefts, rights = refs[:count], refs[count : 3 * count]
    own_out, other_outs = refs[3 * count], refs[3 * count + 1 :]
    right = jnp.concatenate([ref[...] for ref in rights], axis=0)
    rows = lefts[0].shape[0] // parts
    for side in range(2):
        place = me[0] if side == 0 else 1 - me[0]
        left = jnp.concatenate(
            [
                jnp.concatenate(
                    [
                        ref[pl.ds(pl.multiple_of(n * rows + place * own_part, 16), own_part), :]
                        for n in range(parts)
                    ],
                    axis=0,
                )
                for ref in lefts
            ],
            axis=1,
        )
        total = dot(left, right, (1, 0))
        if side == 0:
            own_out[...] = total
        else:
            for n in range(parts):
                other_outs[n][...] = total[n * own_part : (n + 1) * own_part, :].astype(LOW)


def triple_grad(me, parts, lefts, rights, deps=()):
    count = len(lefts)
    total, rows = lefts[0].shape
    own_part = total // parts // 2
    width = rights[0][0].shape[1]
    return pl.pallas_call(
        ordered_after(partial(triple_grad_kernel, count, parts, own_part), 1 + 3 * count, deps),
        in_specs=[pl.BlockSpec(memory_space=pltpu.SMEM)]
        + [IN_VMEM] * (3 * count)
        + [UNREAD] * len(deps),
        out_shape=[jax.ShapeDtypeStruct((parts * own_part, width), F32)]
        + [jax.ShapeDtypeStruct((own_part, width), LOW)] * parts,
        compiler_params=pltpu.CompilerParams(vmem_limit_bytes=VMEM_BYTES),
        cost_estimate=pl.CostEstimate(
            flops=2 * count * rows * total * width,
            bytes_accessed=2 * count * rows * (total + width) + 3 * total * width,
            transcendentals=0,
        ),
    )(me, *lefts, *[side for right in rights for side in right], *deps)


def attend_kernel(
    head_count, seg_q, place_q, seg_k, place_k, query, key_value, summed, total, heads, bias
):
    blocks, _, rows = key_value.shape
    width = head_count * HEAD_DIM
    for j in range(blocks):
        part = pl.ds(j * rows, rows)
        bias[part, :] = mask_bias(seg_q[...], place_q[...], seg_k[part, :], place_k[part, :])
    for head in range(head_count):
        cols = pl.ds(head * HEAD_DIM, HEAD_DIM)
        value_cols = pl.ds(width + head * HEAD_DIM, HEAD_DIM)
        block_query = query[cols, :]
        row_total = jnp.zeros((1, query.shape[1]), F32)
        acc = jnp.zeros((HEAD_DIM, query.shape[1]), F32)
        for j in range(blocks):
            scores = dot(key_value[j, cols, :], block_query, (0, 0))
            raised = jnp.exp(scores + bias[pl.ds(j * rows, rows), :])
            row_total = row_total + jnp.sum(raised, axis=0, keepdims=True)
            acc = acc + dot(key_value[j, value_cols, :], raised.astype(LOW), (1, 0))
        summed[cols, :] = acc
        total[pl.ds(head, 1), :] = row_total
        heads[cols, :] = (acc / row_total).astype(LOW)


def attend(head_count, places, query, key_value, deps=()):
    blocks, _, rows = key_value.shape
    width, count = query.shape
    work = head_count * blocks * rows * count * HEAD_DIM * 4
    return pl.pallas_call(
        ordered_after(partial(attend_kernel, head_count), 6, deps),
        in_specs=[IN_VMEM] * 6 + [UNREAD] * len(deps),
        out_shape=(
            jax.ShapeDtypeStruct((width, count), F32),
            jax.ShapeDtypeStruct((head_count, count), F32),
            jax.ShapeDtypeStruct((width, count), LOW),
        ),
        scratch_shapes=[pltpu.VMEM((blocks * rows, count), F32)],
        compiler_params=pltpu.CompilerParams(vmem_limit_bytes=VMEM_BYTES),
        cost_estimate=pl.CostEstimate(
            flops=4 * work, bytes_accessed=6 * width * count, transcendentals=work // 256
        ),
    )(*places, query, key_value, *deps)


def attend_back_kernel(
    head_count,
    seg_q,
    place_q,
    seg_k,
    place_k,
    query,
    key_value,
    heads_back,
    summed,
    total,
    query_grad,
    own_grad,
    other_grad,
    bias,
):
    blocks, _, rows = key_value.shape
    width = head_count * HEAD_DIM
    for j in range(blocks):
        part = pl.ds(j * rows, rows)
        bias[part, :] = mask_bias(seg_q[...], place_q[...], seg_k[part, :], place_k[part, :])
    for head in range(head_count):
        cols = pl.ds(head * HEAD_DIM, HEAD_DIM)
        value_cols = pl.ds(width + head * HEAD_DIM, HEAD_DIM)
        block_query = query[cols, :]
        output_back = heads_back[cols, :].astype(F32)
        row_total = total[pl.ds(head, 1), :]
        summed_back = (output_back / row_total).astype(LOW)
        total_back = -jnp.sum(output_back * summed[cols, :], axis=0, keepdims=True) / (
            row_total * row_total
        )
        acc = jnp.zeros((HEAD_DIM, query.shape[1]), F32)
        for j in range(blocks):
            key_part = key_value[j, cols, :]
            scores = dot(key_part, block_query, (0, 0))
            raised = jnp.exp(scores + bias[pl.ds(j * rows, rows), :])
            raised_back = dot(key_value[j, value_cols, :], summed_back, (0, 0))
            score_back = (raised * (raised_back + total_back)).astype(LOW)
            acc = acc + dot(key_part, score_back, (1, 0))
            key_grad = dot(block_query, score_back, (1, 1))
            value_grad = dot(summed_back, raised.astype(LOW), (1, 1))
            if j == 0:
                own_grad[cols, :] = key_grad
                own_grad[value_cols, :] = value_grad
            else:
                other_grad[j - 1, cols, :] = key_grad.astype(other_grad.dtype)
                other_grad[j - 1, value_cols, :] = value_grad.astype(other_grad.dtype)
        query_grad[cols, :] = acc


def attend_back(head_count, places, query, key_value, heads_back, summed, total, deps=()):
    blocks, both, rows = key_value.shape
    width, count = query.shape
    work = head_count * blocks * rows * count * HEAD_DIM * 2
    return pl.pallas_call(
        ordered_after(partial(attend_back_kernel, head_count), 9, deps),
        in_specs=[IN_VMEM] * 9 + [UNREAD] * len(deps),
        out_shape=(
            jax.ShapeDtypeStruct((width, count), F32),
            jax.ShapeDtypeStruct((both, rows), F32),
            jax.ShapeDtypeStruct((blocks - 1, both, rows), LOW if blocks == 2 else F32),
        ),
        scratch_shapes=[pltpu.VMEM((blocks * rows, count), F32)],
        compiler_params=pltpu.CompilerParams(vmem_limit_bytes=VMEM_BYTES),
        cost_estimate=pl.CostEstimate(
            flops=5 * 4 * work, bytes_accessed=16 * width * count, transcendentals=work // 128
        ),
    )(*places, query, key_value, heads_back, summed, total, *deps)


def sigmoid(values):
    return 1.0 / (1.0 + jnp.exp(-values))


def feed_kernel(
    root_width,
    own,
    other,
    up_weights,
    gate_weights,
    down_weights,
    scale_up,
    scale_gate,
    up_out,
    gate_out,
    hidden_out,
    own_out,
    other_out,
    total,
):
    half = own.shape[0]
    rows = jnp.concatenate([own[...], other[...]], axis=0)
    up = dot(rows, up_weights[...], (1, 1))
    gate = dot(rows, gate_weights[...], (1, 1))
    up_out[...] = up
    gate_out[...] = gate
    gate_scaled = gate * scale_gate[...] * root_width
    hidden = (gate_scaled * sigmoid(gate_scaled) * (up * scale_up[...])).astype(LOW)
    hidden_out[...] = hidden
    part = dot(hidden, down_weights[...], (1, 0))
    step = pl.program_id(0)

    @pl.when(step == 0)
    def _():
        total[...] = part

    @pl.when(step > 0)
    def _():
        total[...] += part

    @pl.when(step == pl.num_programs(0) - 1)
    def _():
        own_out[...] = total[:half, :]
        other_out[...] = total[half:, :].astype(LOW)


def feed_forward(own, other, feed_full, scale_up, scale_gate, deps=()):
    half, width = own.shape
    units = feed_full[0].shape[0]
    tile = units
    held = pl.BlockSpec((half, width), lambda i: (0, 0))
    weight = pl.BlockSpec((tile, width), lambda i: (i, 0))
    scale = pl.BlockSpec((1, tile), lambda i: (0, i))
    piece = pl.BlockSpec((2 * half, tile), lambda i: (0, i))
    kept = jax.ShapeDtypeStruct((2 * half, units), F32)
    return pl.pallas_call(
        ordered_after(partial(feed_kernel, math.sqrt(width)), 7, deps),
        grid=(units // tile,),
        in_specs=[held, held, weight, weight, weight, scale, scale] + [UNREAD] * len(deps),
        out_specs=[piece, piece, piece, held, held],
        out_shape=[
            kept,
            kept,
            jax.ShapeDtypeStruct((2 * half, units), LOW),
            jax.ShapeDtypeStruct((half, width), F32),
            jax.ShapeDtypeStruct((half, width), LOW),
        ],
        scratch_shapes=[pltpu.VMEM((2 * half, width), F32)],
        compiler_params=pltpu.CompilerParams(vmem_limit_bytes=LARGE_VMEM_BYTES),
        cost_estimate=pl.CostEstimate(
            flops=12 * half * width * units,
            bytes_accessed=6 * width * units + 20 * half * units + 10 * half * width,
            transcendentals=2 * half * units,
        ),
    )(own, other, *feed_full, scale_up, scale_gate, *deps)


def feed_back_kernel(
    root_width,
    own,
    other,
    up_ref,
    gate_ref,
    up_weights,
    gate_weights,
    down_weights,
    scale_up,
    scale_gate,
    up_out,
    gate_out,
    terms_out,
    own_out,
    other_out,
    total,
):
    half = own.shape[0]
    rows = jnp.concatenate([own[...], other[...]], axis=0)
    hidden_back = dot(rows, down_weights[...], (1, 1))
    up = up_ref[...]
    gate = gate_ref[...]
    gate_scaled = gate * scale_gate[...] * root_width
    sigmoid_gate = sigmoid(gate_scaled)
    up_back = hidden_back * (gate_scaled * sigmoid_gate)
    gate_back = (
        hidden_back
        * (up * scale_up[...])
        * (sigmoid_gate * (1.0 + gate_scaled * (1.0 - sigmoid_gate)))
    )
    terms_out[...] = jnp.concatenate(
        [
            jnp.sum(up_back * up, axis=0, keepdims=True),
            jnp.sum(gate_back * gate, axis=0, keepdims=True) * root_width,
        ],
        axis=0,
    )
    up_low = (up_back * scale_up[...]).astype(LOW)
    gate_low = (gate_back * scale_gate[...] * root_width).astype(LOW)
    up_out[...] = up_low
    gate_out[...] = gate_low
    part = dot(up_low, up_weights[...], (1, 0)) + dot(gate_low, gate_weights[...], (1, 0))
    step = pl.program_id(0)

    @pl.when(step == 0)
    def _():
        total[...] = part

    @pl.when(step > 0)
    def _():
        total[...] += part

    @pl.when(step == pl.num_programs(0) - 1)
    def _():
        own_out[...] = total[:half, :]
        other_out[...] = total[half:, :].astype(LOW)


def feed_backward(own, other, up, gate, feed_full, scale_up, scale_gate, deps=()):
    half, width = own.shape
    units = feed_full[0].shape[0]
    tile = units
    held = pl.BlockSpec((half, width), lambda i: (0, 0))
    weight = pl.BlockSpec((tile, width), lambda i: (i, 0))
    scale = pl.BlockSpec((1, tile), lambda i: (0, i))
    piece = pl.BlockSpec((2 * half, tile), lambda i: (0, i))
    return pl.pallas_call(
        ordered_after(partial(feed_back_kernel, math.sqrt(width)), 9, deps),
        grid=(units // tile,),
        in_specs=[held, held, piece, piece, weight, weight, weight, scale, scale]
        + [UNREAD] * len(deps),
        out_specs=[piece, piece, pl.BlockSpec((2, tile), lambda i: (0, i)), held, held],
        out_shape=[
            jax.ShapeDtypeStruct((2 * half, units), LOW),
            jax.ShapeDtypeStruct((2 * half, units), LOW),
            jax.ShapeDtypeStruct((2, units), F32),
            jax.ShapeDtypeStruct((half, width), F32),
            jax.ShapeDtypeStruct((half, width), LOW),
        ],
        scratch_shapes=[pltpu.VMEM((2 * half, width), F32)],
        compiler_params=pltpu.CompilerParams(vmem_limit_bytes=LARGE_VMEM_BYTES),
        cost_estimate=pl.CostEstimate(
            flops=12 * half * width * units,
            bytes_accessed=6 * width * units + 24 * half * units + 10 * half * width,
            transcendentals=2 * half * units,
        ),
    )(own, other, up, gate, *feed_full, scale_up, scale_gate, *deps)


def weight_grad_kernel(count, *refs):
    lefts, rights = refs[:count], refs[count : 3 * count]
    own_out, other_out = refs[3 * count :]
    part = own_out.shape[0]
    right = jnp.concatenate([ref[...] for ref in rights], axis=0)
    for side in range(2):
        left = jnp.concatenate([ref[:, side * part : (side + 1) * part] for ref in lefts], axis=0)
        total = dot(left, right, (0, 0))
        if side == 0:
            own_out[...] = total
        else:
            other_out[...] = total.astype(LOW)


def weight_grad(lefts, rights, deps=()):
    count = len(lefts)
    rows, units = lefts[0].shape
    half, width = rights[0][0].shape
    part = units // 2
    return pl.pallas_call(
        ordered_after(partial(weight_grad_kernel, count), 3 * count, deps),
        in_specs=[IN_VMEM] * (3 * count) + [UNREAD] * len(deps),
        out_shape=[
            jax.ShapeDtypeStruct((part, width), F32),
            jax.ShapeDtypeStruct((part, width), LOW),
        ],
        compiler_params=pltpu.CompilerParams(vmem_limit_bytes=LARGE_VMEM_BYTES),
        cost_estimate=pl.CostEstimate(
            flops=2 * count * rows * units * width,
            bytes_accessed=2 * count * rows * (units + width) + 3 * units * width,
            transcendentals=0,
        ),
    )(*lefts, *[side for right in rights for side in right], *deps)


def first_part(pair, partner, token, rate):
    attention_unit, attention_norm = unit_rows(add_low(pair[...], partner[...]))
    token_float = token[...].astype(F32)
    after, after_norm = unit_rows(token_float + rate * (attention_unit - token_float))
    return (attention_unit, attention_norm, token_float, after, after_norm)


def normed_kernel(pair, partner, token, rates, normed_out):
    normed_out[...] = first_part(pair, partner, token, rates[0:1, :])[3].astype(LOW)


def output_kernel(
    pair, partner, token, feed_pair, feed_partner, cotangent, rates, output_out, second_out, back_out, term_out
):
    after = first_part(pair, partner, token, rates[0:1, :])[3]
    rate = rates[1:2, :]
    feed_unit, feed_norm = unit_rows(add_low(feed_pair[...], feed_partner[...]))
    output, output_norm = unit_rows(after + rate * (feed_unit - after))
    output_out[...] = output
    second_back = unit_back(output, output_norm, cotangent[...].astype(F32))
    second_out[...] = second_back
    back_out[...] = unit_back(feed_unit, feed_norm, second_back * rate).astype(LOW)
    term = jnp.sum(second_back * (feed_unit - after), axis=0, keepdims=True)

    @pl.when(pl.program_id(0) == 0)
    def _():
        term_out[...] = term

    @pl.when(pl.program_id(0) > 0)
    def _():
        term_out[...] += term


def first_back_kernel(
    pair, partner, token, second, grad_pair, grad_partner, rates, skip_out, back_out, term_out
):
    rate = rates[0:1, :]
    attention_unit, attention_norm, token_float, after, after_norm = first_part(
        pair, partner, token, rate
    )
    after_grad = second[...] * (1.0 - rates[1:2, :]) + add_low(grad_pair[...], grad_partner[...])
    first_back = unit_back(after, after_norm, after_grad)
    skip_out[...] = first_back * (1.0 - rate)
    back_out[...] = unit_back(attention_unit, attention_norm, first_back * rate).astype(LOW)
    term = jnp.sum(first_back * (attention_unit - token_float), axis=0, keepdims=True)

    @pl.when(pl.program_id(0) == 0)
    def _():
        term_out[...] = term

    @pl.when(pl.program_id(0) > 0)
    def _():
        term_out[...] += term


def rowwise(body, arrays, rates, outs, has_term, deps=()):
    half, width = arrays[0].shape
    tile = 128 if half % 128 == 0 else half
    flat = pl.BlockSpec((tile, width), lambda i: (i, 0))
    term = [pl.BlockSpec((1, width), lambda i: (0, 0))] if has_term else []
    term_shape = [jax.ShapeDtypeStruct((1, width), F32)] if has_term else []
    return pl.pallas_call(
        ordered_after(body, len(arrays) + 1, deps),
        grid=(half // tile,),
        in_specs=[flat] * len(arrays)
        + [pl.BlockSpec((2, width), lambda i: (0, 0))]
        + [UNREAD] * len(deps),
        out_specs=[flat] * len(outs) + term,
        out_shape=[jax.ShapeDtypeStruct((half, width), kind) for kind in outs] + term_shape,
        compiler_params=pltpu.CompilerParams(vmem_limit_bytes=VMEM_BYTES),
        cost_estimate=pl.CostEstimate(
            flops=40 * half * width,
            bytes_accessed=(2 * len(arrays) + 4 * len(outs)) * half * width,
            transcendentals=4 * half,
        ),
    )(*arrays, rates, *deps)


def adam_step(master, gradient, first_state, second_state, step_rate, is_matrix):
    moment = BETA_ONE * first_state + (1.0 - BETA_ONE) * gradient
    variance = BETA_TWO * second_state + (1.0 - BETA_TWO) * gradient * gradient
    update = moment / CORR_ONE / (jnp.sqrt(variance / CORR_TWO) + ADAM_EPS)
    updated = master - step_rate * (update + DECAY * master)
    if is_matrix:
        updated = unit_only(updated)
    return (moment, variance, updated)


def outer_step(master, shift, outer_state, is_matrix):
    momentum = OUTER_MOMENTUM * outer_state + shift
    result = master - OUTER_RATE * (shift + OUTER_MOMENTUM * momentum)
    if is_matrix:
        result = unit_only(result)
    return (momentum, result)


def row_tile(rows):
    for size in (160, 128):
        if rows % size == 0:
            return size
    return rows


def adam_kernel(has_partner, chunks, offset, own, partner, master, first, second, *rest):
    del offset
    gradient_out, moment_out, variance_out = rest[-3 - chunks : -chunks]
    gradient = own[...]
    if has_partner:
        gradient = gradient + partner[...].astype(F32)
    moment, variance, updated = adam_step(
        master[0], gradient, first[0, 0], second[0, 0], MATRIX_RATE, True
    )
    gradient_out[0, 0] = gradient
    moment_out[0, 0] = moment
    variance_out[0, 0] = variance
    shift = (master[0] - updated).astype(LOW)
    each = pl.num_programs(0) // chunks
    for n in range(chunks):

        @pl.when(pl.program_id(0) // each == n)
        def _(n=n):
            rest[n - chunks][...] = shift


def adam_slab(which, chunks, own_block, gradient, partner, master, first, second, earlier, deps=()):
    slabs, rows, width = master.shape
    tile = row_tile(rows)
    steps = rows // tile
    each = steps // chunks
    has_partner = partner is not None
    if not has_partner:
        partner = jnp.zeros((tile, width), LOW)
    flat = pl.BlockSpec((tile, width), lambda i, at: (i, 0))
    held = pl.BlockSpec((tile, width), lambda i, at: (at[0] * steps + i, 0))
    once = pl.BlockSpec((tile, width), lambda i, at: (0, 0))
    slab = pl.BlockSpec((1, tile, width), lambda i, at: (which, i, 0))
    grouped = pl.BlockSpec((1, 1, tile, width), lambda i, at: (0, which, i, 0))
    whole = jax.ShapeDtypeStruct((1, slabs, rows, width), F32)
    earlier = () if earlier is None else earlier
    pieces = [
        pl.BlockSpec((tile, width), lambda i, at, n=n: (jnp.clip(i - n * each, 0, each - 1), 0))
        for n in range(chunks)
    ]
    return pl.pallas_call(
        partial(adam_kernel, has_partner, chunks),
        grid_spec=pltpu.PrefetchScalarGridSpec(
            num_scalar_prefetch=1,
            grid=(steps,),
            in_specs=[held, flat if has_partner else once, slab, grouped, grouped]
            + [UNREAD] * (len(earlier) + len(deps)),
            out_specs=[grouped, grouped, grouped] + pieces,
        ),
        out_shape=[whole, whole, whole]
        + [jax.ShapeDtypeStruct((rows // chunks, width), LOW)] * chunks,
        input_output_aliases={6 + n: n for n in range(len(earlier))},
        compiler_params=pltpu.CompilerParams(vmem_limit_bytes=VMEM_BYTES),
        cost_estimate=pl.CostEstimate(
            flops=30 * rows * width, bytes_accessed=32 * rows * width, transcendentals=rows * width
        ),
    )(own_block, gradient, partner, master, first, second, *earlier, *deps)


def outer_kernel(group_count, at_end, whole, back, master, outer, *rest):
    momentum_out, result_out = rest[-2:]
    shift = jnp.where(at_end[0] == 1, back[...].astype(F32), whole[...].astype(F32)) / group_count
    momentum, result = outer_step(master[0], shift, outer[0], True)
    momentum_out[0] = momentum
    result_out[0] = result


def outer_slab(which, chunk, group_count, at_end, whole, back, master, outer, earlier, deps=()):
    slabs, rows, width = master.shape
    part = whole.shape[0]
    tile = row_tile(part)
    steps = part // tile
    flat = pl.BlockSpec((tile, width), lambda i, at: (i, 0))
    slab = pl.BlockSpec((1, tile, width), lambda i, at: (which, chunk * steps + i, 0))
    result = jax.ShapeDtypeStruct((slabs, rows, width), F32)
    earlier = () if earlier is None else earlier
    return pl.pallas_call(
        partial(outer_kernel, group_count),
        grid_spec=pltpu.PrefetchScalarGridSpec(
            num_scalar_prefetch=1,
            grid=(steps,),
            in_specs=[flat, flat, slab, slab] + [UNREAD] * (len(earlier) + len(deps)),
            out_specs=[slab, slab],
        ),
        out_shape=[result, result],
        input_output_aliases={5 + n: n for n in range(len(earlier))},
        compiler_params=pltpu.CompilerParams(vmem_limit_bytes=VMEM_BYTES),
        cost_estimate=pl.CostEstimate(
            flops=20 * part * width, bytes_accessed=20 * part * width, transcendentals=part
        ),
    )(at_end, whole, back, master, outer, *earlier, *deps)


class MatrixSteps:
    def __init__(self, chunks, at_end, master, first, second, outer):
        self.chunks = chunks
        self.at_end = at_end.reshape(1)
        self.arrays = (master, first, second)
        self.outer_state = outer
        self.inner_outs = None
        self.sums = {}

    def inner(self, which, gradient, deps):
        own, partner, block = gradient
        outs = adam_slab(
            which, self.chunks, block, own, partner, *self.arrays, self.inner_outs, deps
        )
        self.inner_outs = outs[:3]
        self.sums[which] = [group_sum(shift) for shift in outs[3:]]
        return outs[3]

    def pairs(self, which):
        return [step[0] for step in self.sums[which]]

    def wholes(self, which):
        return [step[1] for step in self.sums[which]]

    def outer(self):
        outs = None
        for which, chunk_sums in self.sums.items():
            for chunk, (_, whole, back) in enumerate(chunk_sums):
                outs = outer_slab(
                    which,
                    chunk,
                    lax.axis_size("group"),
                    self.at_end,
                    whole,
                    back,
                    self.arrays[0],
                    self.outer_state,
                    outs,
                )
        return (*self.inner_outs, *outs)


def place_kernel(core, own, other, *rest):
    out = rest[-1]

    @pl.when(pl.program_id(0) == 0)
    def _():
        out[0, 0] = own[...]

    @pl.when(pl.program_id(0) == 1)
    def _():
        out[0, 0] = other[...]


def place_rows(which, count, core, own, other, earlier, deps=()):
    half, width = own.shape
    held = pl.BlockSpec((half, width), lambda i, at: (0, 0))
    earlier = () if earlier is None else (earlier,)
    return pl.pallas_call(
        place_kernel,
        grid_spec=pltpu.PrefetchScalarGridSpec(
            num_scalar_prefetch=1,
            grid=(2,),
            in_specs=[held, held] + [UNREAD] * (len(earlier) + len(deps)),
            out_specs=pl.BlockSpec(
                (1, 1, half, width), lambda i, at: (0, which, lax.rem(at[0] + i, 2), 0)
            ),
        ),
        out_shape=jax.ShapeDtypeStruct((1, count, 2 * half, width), F32),
        input_output_aliases={3: 0} if earlier else {},
        compiler_params=pltpu.CompilerParams(vmem_limit_bytes=VMEM_BYTES),
        cost_estimate=pl.CostEstimate(
            flops=0, bytes_accessed=16 * half * width, transcendentals=0
        ),
    )(core, own, other, *earlier, *deps)


def on_device(
    tokens,
    cotangent,
    segments,
    shard_order,
    attention_weights,
    feedforward_weights,
    head_scales,
    hidden_scales,
    residual_rates,
    attention_first,
    feedforward_first,
    heads_first,
    hidden_first,
    rates_first,
    attention_second,
    feedforward_second,
    heads_second,
    hidden_second,
    rates_second,
    attention_outer,
    feedforward_outer,
    heads_outer,
    hidden_outer,
    rates_outer,
):
    micro_count, rows, model_width = tokens.shape[1:]
    half = rows // 2
    ctx_count = lax.axis_size("ctx")
    pair = ctx_count == 2
    group_count = lax.axis_size("group")
    own_rows = attention_weights.shape[1]
    own_units = feedforward_weights.shape[1]
    head_width = own_rows * ctx_count
    head_count = head_width // HEAD_DIM
    units = own_units * ctx_count
    root_head = math.sqrt(HEAD_DIM)
    root_width = math.sqrt(model_width)
    me = lax.axis_index("ctx")
    ctx_first = me == 0
    core_index = lax.rem(lax.axis_index("tensor"), 2).reshape(1)
    core_first = core_index[0] == 0
    even_group = lax.rem(lax.axis_index("group"), 2) == 0
    micros = range(micro_count)
    at_end = lax.axis_index("group")
    at_end = ((at_end == 0) | (at_end == group_count - 1)).astype(jnp.int32)

    attention_low = attention_weights.astype(LOW)
    feed_low = feedforward_weights.astype(LOW)
    small_low = jnp.concatenate(
        [head_scales, hidden_scales[0], hidden_scales[1], residual_rates[0], residual_rates[1]]
    ).astype(LOW)
    own_cols = residual_rates.shape[1]
    if pair:
        part = own_rows // 2
        piece = jnp.where(even_group, attention_low[:3, :part], attention_low[:3, part:])
        triple_across = trade(piece, "ctx", 1)
        triple_other = ordered(even_group, triple_across, trade(triple_across, "group", 1), 1)
        triple_weights = ordered(ctx_first, attention_low[:3], triple_other, 1)
        small_other = trade(small_low, "ctx", 1)
        cuts = [own_rows, own_units, own_units, own_cols, own_cols]
        small_pieces = []
        start = 0
        for which, size in enumerate(cuts):
            mine = small_low[start : start + size].astype(F32)
            theirs = small_other[start : start + size].astype(F32)
            start += size
            if which in (1, 2):
                small_pieces.append(jnp.concatenate([mine, theirs]))
            else:
                small_pieces.append(ordered(ctx_first, mine, theirs, 0))
        scale_heads, scale_up, scale_gate, rate_attention, rate_feed = small_pieces
    else:
        triple_weights = lax.all_gather(attention_low[:3], "ctx", axis=1, tiled=True)
        scale_heads = lax.all_gather(head_scales.astype(LOW), "ctx", axis=0, tiled=True).astype(F32)
        scale_up, scale_gate = lax.all_gather(
            hidden_scales.astype(LOW), "ctx", axis=1, tiled=True
        ).astype(F32)
        rate_attention, rate_feed = lax.all_gather(
            residual_rates.astype(LOW), "ctx", axis=1, tiled=True
        ).astype(F32)
    triple_weights = triple_weights.reshape(3 * head_width, model_width)
    scale_column = scale_heads.reshape(head_width, 1)

    token_halves = tokens[0].reshape(micro_count, 2, half, model_width)
    token_own = jnp.where(core_first, token_halves[:, 0], token_halves[:, 1])
    token_other = jnp.where(core_first, token_halves[:, 1], token_halves[:, 0])
    cotangent_halves = cotangent[0].reshape(micro_count, 2, half, model_width)
    cotangent_own = jnp.where(core_first, cotangent_halves[:, 0], cotangent_halves[:, 1])

    if pair:
        block_ids = jnp.stack([me, 1 - me])
    else:
        block_ids = lax.rem(me + jnp.arange(ctx_count, dtype=jnp.int32), ctx_count)
    table = jnp.arange(ctx_count, dtype=jnp.int32)
    order_of = jnp.sum(
        jnp.where(block_ids[:, None] == table[None, :], shard_order[None, :], 0), axis=1
    )
    local = jnp.arange(rows, dtype=jnp.int32)
    local = jnp.where(core_first, local, lax.rem(local + half, rows))
    place_blocks = order_of[:, None] * rows + local[None, :]
    segment_blocks = segments[0].reshape(micro_count, ctx_count, rows)
    segment_blocks = jnp.sum(
        jnp.where(
            (order_of[:, None] == table[None, :])[None, :, :, None], segment_blocks[:, None], 0
        ),
        axis=2,
    )
    segment_blocks = jnp.where(
        core_first,
        segment_blocks,
        jnp.concatenate([segment_blocks[:, :, half:], segment_blocks[:, :, :half]], axis=2),
    )
    places = [
        (
            segment_blocks[b, 0][None, :],
            place_blocks[0][None, :],
            segment_blocks[b].reshape(ctx_count * rows, 1),
            place_blocks.reshape(ctx_count * rows, 1),
        )
        for b in micros
    ]

    if pair:
        arrivals = []
        before = triple_across
        feed_full = []
        for which in range(3):
            source = feed_low[which]
            part = own_units // 2
            piece = tie(jnp.where(even_group, source[:part], source[part:]), before)
            across = trade(piece, "ctx", 1)
            before = across
            arrivals.append(across)
            along = trade(across, "group", 1)
            feed_full.append(
                jnp.concatenate([source, ordered(even_group, across, along, 0)], axis=0)
            )
        part = own_rows // 2
        piece = tie(
            jnp.where(even_group, attention_low[3, :part], attention_low[3, part:]), triple_across
        )
        across = trade(piece, "ctx", 1)
        output_other = ordered(even_group, across, trade(across, "group", 1), 0)
        output_weights = ordered(ctx_first, attention_low[3], output_other, 0)
    else:
        output_weights = lax.all_gather(attention_low[3], "ctx", axis=0, tiled=True)
        feed_full = list(lax.all_gather(feed_low, "ctx", axis=1, tiled=True))
        arrivals = []
    up_weights, gate_weights, down_weights = feed_full

    projections, query_low, key_values = [], [], []
    for b in micros:
        projected, query, key_value = project(
            head_count,
            triple_weights,
            token_own[b],
            token_other[b],
            scale_column,
            projections[-1:],
        )
        projections.append(projected)
        query_low.append(query)
        if pair:
            sent = tie(key_value, arrivals[0]) if b == 0 else key_value
            key_values.append(jnp.stack([key_value, trade(sent, "ctx", 1)]))
        else:
            gathered = lax.all_gather(key_value, "ctx", axis=0)
            key_values.append(jnp.take(gathered, block_ids, axis=0))

    rates_both = jnp.stack([rate_attention, rate_feed])
    scale_up = scale_up.reshape(1, units)
    scale_gate = scale_gate.reshape(1, units)
    summeds, totals, heads_lows, attention_sums, normed_rows = [], [], [], [], []

    def normed_part(b, deps):
        (normed_low,) = rowwise(
            normed_kernel, attention_sums[b], rates_both, [LOW], False, deps
        )
        normed_rows.append((normed_low, trade(normed_low, "tensor", 1)))

    for b in micros:
        deps = totals[-1:] + arrivals[1:2] * (b == 0)
        if b == micro_count - 1 and b > 1:
            normed_part(0, totals[-1:])
            deps = [normed_rows[0][0]] + arrivals[2:]
        summed, total, heads_low = attend(
            head_count, places[b], query_low[b], key_values[b], deps
        )
        summeds.append(summed)
        totals.append(total)
        heads_lows.append(heads_low)
        other_part = dot(heads_low[:, half:], output_weights, (0, 0), LOW)
        own_part = dot(heads_low[:, :half], output_weights, (0, 0))
        attention_sums.append((*tensor_sum(own_part, other_part), token_own[b]))
    for b in micros[len(normed_rows) :]:
        normed_part(b, [rows_of[0] for rows_of in normed_rows[-1:]] + totals[-1:])

    ups, gates, hidden_rows, feed_parts = [], [], [], []
    for b in micros:
        up, gate, hidden, own_part, other_part = feed_forward(
            *normed_rows[b],
            feed_full,
            scale_up,
            scale_gate,
            [normed_rows[-1][0] if b == 0 else feed_parts[-1][1]],
        )
        ups.append(up)
        gates.append(gate)
        hidden_rows.append(hidden)
        feed_parts.append((own_part, other_part))

    outputs, second_backs, feed_back_rows, feed_rate_terms = [], [], [], []
    up_back_rows, gate_back_rows, hidden_terms, grad_sums = [], [], [], []
    skips, attention_back_rows, attention_rate_terms = [], [], []
    attention_grads = []
    down_grad = None

    def output_part(b, deps):
        output, second_back, feed_back, term = rowwise(
            output_kernel,
            (*attention_sums[b], *tensor_sum(*feed_parts[b]), cotangent_own[b]),
            rates_both,
            [F32, F32, LOW],
            True,
            deps,
        )
        outputs.append(output)
        second_backs.append(second_back)
        feed_rate_terms.append(term)
        feed_back_rows.append((feed_back, trade(feed_back, "tensor", 1)))

    def feed_part_back(b, deps):
        up_low, gate_low, terms, own_part, other_part = feed_backward(
            *feed_back_rows[b], ups[b], gates[b], feed_full, scale_up, scale_gate, deps
        )
        up_back_rows.append(up_low)
        gate_back_rows.append(gate_low)
        hidden_terms.append(terms)
        grad_sums.append(tensor_sum(own_part, other_part))

    def first_part_back(b, deps):
        skip, attention_back, term = rowwise(
            first_back_kernel,
            (*attention_sums[b], second_backs[b], *grad_sums[b]),
            rates_both,
            [F32, LOW],
            True,
            deps,
        )
        skips.append(skip)
        attention_rate_terms.append(term)
        attention_back_rows.append(
            jnp.concatenate([attention_back, trade(attention_back, "tensor", 1)], axis=0)
        )

    def attention_part_back(b, deps):
        heads_back = dot(output_weights, attention_back_rows[b], (1, 1), LOW)
        attention_grads.append(
            attend_back(
                head_count,
                places[b],
                query_low[b],
                key_values[b],
                heads_back,
                summeds[b],
                totals[b],
                deps,
            )
        )

    def to_owner(gradient, in_order):
        if not pair:
            summed_rows = lax.psum_scatter(gradient, "ctx", scatter_dimension=0, tiled=True)
            return (summed_rows, None, jnp.zeros((1,), jnp.int32))
        size = gradient.shape[0] // 2
        other = gradient[size:]
        block = jnp.zeros((1,), jnp.int32)
        if in_order:
            other = jnp.where(ctx_first, gradient[size:], gradient[:size])
            block = me.reshape(1)
        return (gradient, trade(other.astype(LOW), "ctx", 1), block)

    def feed_gradient(lefts, rights, deps, hold=()):
        if not pair:
            right = jnp.concatenate([side for entry in rights for side in entry], axis=0)
            grad = to_owner(dot(jnp.concatenate(lefts, axis=0), right, (0, 0)), False)
            return (grad, grad[0])
        own, other = weight_grad(lefts, rights, deps)
        sent = tie(other, *hold) if hold else other
        return ((own, trade(sent, "ctx", 1), jnp.zeros((1,), jnp.int32)), own)

    triples, head_terms, input_sums = [], [], []

    def sides_part_back(b, deps):
        query_grad, own_grad, other_grad = attention_grads[b]
        arrived = None
        if pair:
            arrived = side_arrivals[b]
        else:
            sides = jnp.concatenate([own_grad[None], other_grad], axis=0)
            sides = jnp.take(sides, lax.rem(table - me + ctx_count, ctx_count), axis=0)
            own_grad = lax.psum_scatter(sides, "ctx", scatter_dimension=0)
        triple, terms = sides_back(
            head_count, own_grad, arrived, query_grad, projections[b], scale_column, deps
        )
        triples.append(triple)
        head_terms.append(terms)
        other_part = dot(triple[:, half:], triple_weights, (0, 0), LOW)
        own_part = dot(triple[:, :half], triple_weights, (0, 0))
        input_sums.append(tensor_sum(own_part, other_part))

    last = micro_count - 1
    tag = feed_parts[-1][1]
    for b in micros:
        output_part(b, [tag])
        if b == last:
            down_grad, tag = feed_gradient(hidden_rows, feed_back_rows, [])
            first_part_back(0, [tag])
            tag = attention_rate_terms[0]
        feed_part_back(b, [tag])
        tag = hidden_terms[b]
    up_grad, tag = feed_gradient(up_back_rows, normed_rows, [tag])
    feed_steps = MatrixSteps(
        2 if own_units % 320 == 0 else 1,
        at_end,
        feedforward_weights,
        feedforward_first,
        feedforward_second,
        feedforward_outer,
    )
    side_arrivals = []

    def send_sides(b):
        if pair:
            side_arrivals.append(trade(attention_grads[b][2][0], "ctx", 1))

    token_halves_of = [(token_own[b], token_other[b]) for b in micros]
    arrived_down = [down_grad[1]] if pair else []
    attention_part_back(0, [tag] + arrived_down)
    send_sides(0)
    first_part_back(1, [attention_grads[0][0]])
    attention_part_back(1, [attention_rate_terms[1]])
    send_sides(1)
    tag = feed_steps.inner(2, down_grad, [attention_grads[1][0]])
    sides_part_back(0, [tag])
    for b in micros[2:]:
        first_part_back(b, [head_terms[-1]])
        attention_part_back(b, [attention_rate_terms[b]])
        send_sides(b)
        sides_part_back(b - 1, [attention_grads[b][0]])
    output_grad = to_owner(
        dot(
            jnp.concatenate(heads_lows, axis=1), jnp.concatenate(attention_back_rows, axis=0), (1, 0)
        ),
        True,
    )
    gate_grad, gate_tag = feed_gradient(
        gate_back_rows,
        normed_rows,
        [head_terms[-1]] + feed_steps.pairs(2)[:1],
        side_arrivals[-1:],
    )
    tag = feed_steps.inner(0, up_grad, [gate_tag] + feed_steps.pairs(2))
    sides_part_back(last, [tag])
    if pair:
        own, *others = triple_grad(
            me.reshape(1), 3, triples, token_halves_of, feed_steps.wholes(2)[:1]
        )
        tag = own
        projection_grads = [
            (own, trade(others[which], "ctx", 1), jnp.full((1,), which, jnp.int32))
            for which in range(3)
        ]
    else:
        triple_all = dot(
            jnp.concatenate(triples, axis=1),
            jnp.concatenate([side for sides in token_halves_of for side in sides], axis=0),
            (1, 0),
        ).reshape(3, head_width, model_width)
        projection_grads = [to_owner(triple_all[which], True) for which in range(3)]

    block_output = None
    for b in micros:
        block_output = place_rows(
            b,
            micro_count,
            core_index,
            outputs[b],
            trade(outputs[b], "tensor", 1),
            block_output,
            [tag],
        )

    rate_terms = jnp.concatenate([sum(attention_rate_terms), sum(feed_rate_terms)], axis=0)
    rate_terms = rate_terms + trade(rate_terms, "tensor", 1)
    head_terms = sum(head_terms).reshape(head_width)
    hidden_terms = sum(hidden_terms)
    if pair:
        heads_own = jnp.where(ctx_first, head_terms[:own_rows], head_terms[own_rows:])
        heads_other = jnp.where(ctx_first, head_terms[own_rows:], head_terms[:own_rows])
        rates_own = jnp.where(ctx_first, rate_terms[:, :own_cols], rate_terms[:, own_cols:])
        rates_other = jnp.where(ctx_first, rate_terms[:, own_cols:], rate_terms[:, :own_cols])
        flat = jnp.concatenate(
            [heads_other, hidden_terms[:, own_units:].reshape(-1), rates_other.reshape(-1)]
        )
        flat = trade(flat, "ctx", 1)
        heads_grad = heads_own + flat[:own_rows]
        hidden_grad = hidden_terms[:, :own_units] + flat[
            own_rows : own_rows + 2 * own_units
        ].reshape(2, own_units)
        rates_grad = rates_own + flat[own_rows + 2 * own_units :].reshape(2, own_cols)
    else:
        heads_grad = lax.psum_scatter(head_terms, "ctx", scatter_dimension=0, tiled=True)
        hidden_grad = lax.psum_scatter(hidden_terms, "ctx", scatter_dimension=1, tiled=True)
        rates_grad = lax.psum_scatter(rate_terms, "ctx", scatter_dimension=1, tiled=True)

    attention_steps = MatrixSteps(
        1,
        at_end,
        attention_weights,
        attention_first,
        attention_second,
        attention_outer,
    )
    attention_steps.inner(3, output_grad, [tag])
    input_gradient = None
    arrived_inputs = [sums[1] for sums in input_sums]
    feed_steps.inner(1, gate_grad, feed_steps.pairs(0) + arrived_inputs[:2])
    for which in range(3):
        attention_steps.inner(
            which,
            projection_grads[which],
            feed_steps.wholes(0) + arrived_inputs[2:] if which == 0 else [],
        )
    for b in micros:
        input_own = skips[b] + add_low(*input_sums[b])
        input_gradient = place_rows(
            b, micro_count, core_index, input_own, trade(input_own, "tensor", 1), input_gradient
        )
    feed_outs = feed_steps.outer()
    attention_outs = attention_steps.outer()

    masters = (head_scales, hidden_scales, residual_rates)
    firsts = (heads_first[0], hidden_first[0], rates_first[0])
    seconds = (heads_second[0], hidden_second[0], rates_second[0])
    outers = (heads_outer, hidden_outer, rates_outer)
    small_grads = (heads_grad, hidden_grad, rates_grad)
    small_moments, small_variances, small_shifts = [], [], []
    for which in range(3):
        moment, variance, updated = adam_step(
            masters[which],
            small_grads[which],
            firsts[which],
            seconds[which],
            SCALE_RATE,
            False,
        )
        small_moments.append(moment)
        small_variances.append(variance)
        small_shifts.append((masters[which] - updated).reshape(-1))
    _, whole, back = group_sum(jnp.concatenate(small_shifts))
    shift_flat = jnp.where(at_end == 1, back, whole) / group_count
    small_momenta, small_results = [], []
    start = 0
    for which in range(3):
        size = masters[which].size
        shift = shift_flat[start : start + size].reshape(masters[which].shape)
        start += size
        momentum, result = outer_step(masters[which], shift, outers[which], False)
        small_momenta.append(momentum)
        small_results.append(result)

    return (
        block_output,
        input_gradient,
        attention_outs[0],
        feed_outs[0],
        *[entry[None] for entry in small_grads],
        attention_outs[1],
        feed_outs[1],
        *[entry[None] for entry in small_moments],
        attention_outs[2],
        feed_outs[2],
        *[entry[None] for entry in small_variances],
        attention_outs[3],
        feed_outs[3],
        *small_momenta,
        attention_outs[4],
        feed_outs[4],
        *small_results,
    )


def solution(mesh):
    placed = (
        P("group", None, "ctx", None),
        P("group", None, "ctx", None),
        P("group", None, None),
        P(),
        P(None, ("tensor", "ctx"), None),
        P(None, ("tensor", "ctx"), None),
        P(("tensor", "ctx")),
        P(None, ("tensor", "ctx")),
        P(None, "ctx"),
        P("group", None, ("tensor", "ctx"), None),
        P("group", None, ("tensor", "ctx"), None),
        P("group", ("tensor", "ctx")),
        P("group", None, ("tensor", "ctx")),
        P("group", None, "ctx"),
        P("group", None, ("tensor", "ctx"), None),
        P("group", None, ("tensor", "ctx"), None),
        P("group", ("tensor", "ctx")),
        P("group", None, ("tensor", "ctx")),
        P("group", None, "ctx"),
        P(None, ("tensor", "ctx"), None),
        P(None, ("tensor", "ctx"), None),
        P(("tensor", "ctx")),
        P(None, ("tensor", "ctx")),
        P(None, "ctx"),
    )
    return jax.shard_map(
        on_device,
        mesh=mesh,
        in_specs=placed,
        out_specs=(
            P("group", None, "ctx", None),
            P("group", None, "ctx", None),
            P("group", None, ("tensor", "ctx"), None),
            P("group", None, ("tensor", "ctx"), None),
            P("group", ("tensor", "ctx")),
            P("group", None, ("tensor", "ctx")),
            P("group", None, "ctx"),
            P("group", None, ("tensor", "ctx"), None),
            P("group", None, ("tensor", "ctx"), None),
            P("group", ("tensor", "ctx")),
            P("group", None, ("tensor", "ctx")),
            P("group", None, "ctx"),
            P("group", None, ("tensor", "ctx"), None),
            P("group", None, ("tensor", "ctx"), None),
            P("group", ("tensor", "ctx")),
            P("group", None, ("tensor", "ctx")),
            P("group", None, "ctx"),
            P(None, ("tensor", "ctx"), None),
            P(None, ("tensor", "ctx"), None),
            P(("tensor", "ctx")),
            P(None, ("tensor", "ctx")),
            P(None, "ctx"),
            P(None, ("tensor", "ctx"), None),
            P(None, ("tensor", "ctx"), None),
            P(("tensor", "ctx")),
            P(None, ("tensor", "ctx")),
            P(None, "ctx"),
        ),
        check_vma=False,
    )
```

```python
from functools import partial
import math

import jax
import jax.numpy as jnp
from jax import lax
from jax.experimental import pallas as pl
from jax.experimental.pallas import tpu as pltpu
from jax.sharding import PartitionSpec as P

HEAD_DIM = 64


EPSILON = 1e-06
BETA_ONE = 0.9
BETA_TWO = 0.95
CORR_ONE = 1.0 - 0.9**4
CORR_TWO = 1.0 - 0.95**4
ADAM_EPS = 1e-08
DECAY = 0.1
MATRIX_RATE = 0.02
SCALE_RATE = 0.3
OUTER_RATE = 0.7
OUTER_MOMENTUM = 0.9
MASKED = -1e30
VMEM_BYTES = 40 * 1024 * 1024
LARGE_VMEM_BYTES = 56 * 1024 * 1024
SMALL_VMEM_BYTES = 16 * 1024 * 1024
F32 = jnp.float32
SMALL_COST = pl.CostEstimate(flops=1000, bytes_accessed=1000, transcendentals=0)
LOW = jnp.bfloat16


def unit_rows(values, axis=-1):
    scale = lax.rsqrt(jnp.sum(values * values, axis=axis, keepdims=True) + EPSILON)
    return (values * scale, scale)


def unit_only(values):
    return values * lax.rsqrt(jnp.sum(values * values, axis=-1, keepdims=True) + EPSILON)


def unit_back(unit, scale, upstream, axis=-1):
    return scale * (upstream - unit * jnp.sum(upstream * unit, axis=axis, keepdims=True))


def dot(left, right, contract, out=F32):
    return lax.dot_general(
        left, right, (((contract[0],), (contract[1],)), ((), ())), preferred_element_type=F32
    ).astype(out)


def trade(values, axis, bit):
    count = lax.axis_size(axis)
    return lax.ppermute(values, axis, [(i, i ^ bit) for i in range(count)])


def ordered(first, own, other, axis):
    return jnp.where(
        first,
        jnp.concatenate([own, other], axis=axis),
        jnp.concatenate([other, own], axis=axis),
    )


def split_low(values):
    return lax.optimization_barrier(values.astype(LOW))


def add_low(left, right):
    return left.astype(F32) + right.astype(F32)


def ordered_after(body, count, deps):
    def wrapped(*refs):
        return body(*refs[:count], *refs[count + len(deps) :])

    return wrapped


UNREAD = pl.BlockSpec(memory_space=pl.ANY)
IN_VMEM = pl.BlockSpec(memory_space=pltpu.VMEM)


def tie_kernel(*refs):
    del refs


def tie(values, *deps):
    return pl.pallas_call(
        tie_kernel,
        in_specs=[UNREAD] * (1 + len(deps)),
        out_specs=UNREAD,
        out_shape=jax.ShapeDtypeStruct(values.shape, values.dtype),
        input_output_aliases={0: 0},
    )(values, *deps)


def add_kernel(count, *refs):
    total = refs[0][...].astype(F32)
    for ref in refs[1:count]:
        total = total + ref[...].astype(F32)
    refs[-1][...] = total.astype(refs[-1].dtype)


def added(terms, out):
    if len(terms[0].shape) == 1:
        return lax.optimization_barrier(sum(term.astype(F32) for term in terms).astype(out))
    return pl.pallas_call(
        partial(add_kernel, len(terms)),
        in_specs=[IN_VMEM] * len(terms),
        out_shape=jax.ShapeDtypeStruct(terms[0].shape, out),
        compiler_params=pltpu.CompilerParams(vmem_limit_bytes=SMALL_VMEM_BYTES),
        cost_estimate=SMALL_COST,
    )(*terms)


def rows_kernel(features, weights, own_out, other_out):
    half = own_out.shape[0]
    other_out[...] = dot(features[:, half:], weights[...], (0, 0), LOW)
    own_out[...] = dot(features[:, :half], weights[...], (0, 0))


def to_rows(features, weights):
    half = features.shape[1] // 2
    width = weights.shape[1]
    return pl.pallas_call(
        rows_kernel,
        in_specs=[IN_VMEM] * 2,
        out_shape=[
            jax.ShapeDtypeStruct((half, width), F32),
            jax.ShapeDtypeStruct((half, width), LOW),
        ],
        compiler_params=pltpu.CompilerParams(vmem_limit_bytes=VMEM_BYTES),
        cost_estimate=SMALL_COST,
    )(features, weights)


def tensor_sum(own_part, other_part):
    pair = added([own_part, trade(other_part, "tensor", 1)], LOW)
    return (pair, trade(pair, "tensor", 2))


def group_sum(values):
    dtype = values.dtype
    pair = added([values, lax.ppermute(values, "group", [(0, 1), (3, 2)])], dtype)
    whole = added([pair, lax.ppermute(pair, "group", [(1, 2), (2, 1)])], dtype)
    back = lax.ppermute(whole, "group", [(1, 0), (2, 3)])
    return (pair, whole, back)


def chain_kernel(count, *refs):
    shifts, outs = refs[:count], refs[count : 2 * count]
    landed = refs[2 * count : 3 * count]
    crossed = refs[3 * count : 4 * count]
    pairs = refs[4 * count : 5 * count]
    sems = refs[5 * count]
    here = lax.axis_index("group")
    at_end = (here == 0) | (here == 3)
    middle = jnp.where(here < 2, 1, 2)
    end = jnp.where(here < 2, 0, 3)
    facing = 3 - middle
    barrier = pltpu.get_barrier_semaphore()

    def remote(source, target, k, step, to):
        return pltpu.make_async_remote_copy(
            src_ref=source,
            dst_ref=target,
            send_sem=sems.at[k, 2 * step],
            recv_sem=sems.at[k, 2 * step + 1],
            device_id={"group": to},
            device_id_type=pl.DeviceIdType.MESH,
        )

    inward = [remote(shifts[k], landed[k], k, 0, middle) for k in range(count)]
    across = [remote(pairs[k], crossed[k], k, 1, facing) for k in range(count)]
    outward = [remote(outs[k], landed[k], k, 2, end) for k in range(count)]

    @pl.when(at_end)
    def _():
        pl.semaphore_signal(
            barrier, inc=1, device_id={"group": middle}, device_id_type=pl.DeviceIdType.MESH
        )
        pl.semaphore_wait(barrier, 1)
        for copy in inward:
            copy.start()
        for k in range(count):
            outward[k].wait_recv()
            outs[k][...] = landed[k][...]
        for copy in inward:
            copy.wait_send()

    @pl.when(jnp.logical_not(at_end))
    def _():
        for to in (end, facing):
            pl.semaphore_signal(
                barrier, inc=1, device_id={"group": to}, device_id_type=pl.DeviceIdType.MESH
            )
        pl.semaphore_wait(barrier, 2)
        for k in range(count + 1):
            if k < count:
                inward[k].wait_recv()
                total = shifts[k][...].astype(F32) + landed[k][...].astype(F32)
                pairs[k][...] = total.astype(pairs[k].dtype)
                across[k].start()
            if k > 0:
                across[k - 1].wait_recv()
                total = pairs[k - 1][...].astype(F32) + crossed[k - 1][...].astype(F32)
                outs[k - 1][...] = total.astype(outs[k - 1].dtype)
                outward[k - 1].start()
        for k in range(count):
            across[k].wait_send()
            outward[k].wait_send()


def chain_sum(shifts, deps):
    count = len(shifts)
    shapes = [jax.ShapeDtypeStruct(shift.shape, shift.dtype) for shift in shifts]
    buffers = [pltpu.VMEM(shift.shape, shift.dtype) for shift in shifts]
    return pl.pallas_call(
        ordered_after(partial(chain_kernel, count), count, deps),
        in_specs=[IN_VMEM] * count + [UNREAD] * len(deps),
        out_specs=[IN_VMEM] * count,
        out_shape=shapes,
        scratch_shapes=buffers * 3 + [pltpu.SemaphoreType.DMA((count, 6))],
        compiler_params=pltpu.CompilerParams(
            collective_id=0, has_side_effects=True, vmem_limit_bytes=VMEM_BYTES
        ),
        cost_estimate=SMALL_COST,
    )(*shifts, *deps)


def mask_bias(seg_q, place_q, seg_k, place_k):
    allowed = (seg_k == seg_q) & (place_k <= place_q)
    return jnp.where(allowed, 0.0, MASKED).astype(F32)


def project_kernel(head_count, weights, own, other, scale, projected, query_low, key_value):
    width = head_count * HEAD_DIM
    rows = jnp.concatenate([own[...], other[...]], axis=0)
    projected[...] = dot(weights[...], rows, (1, 1))
    for head in range(head_count):
        cols = pl.ds(head * HEAD_DIM, HEAD_DIM)
        key_cols = pl.ds(width + head * HEAD_DIM, HEAD_DIM)
        head_scale = scale[cols, :]
        query_unit, _ = unit_rows(projected[cols, :], axis=0)
        key_unit, _ = unit_rows(projected[key_cols, :], axis=0)
        query_low[cols, :] = (query_unit * head_scale * math.sqrt(HEAD_DIM)).astype(LOW)
        key_value[cols, :] = (key_unit * head_scale).astype(LOW)
    key_value[width : 2 * width, :] = projected[2 * width : 3 * width, :].astype(LOW)


def project(head_count, weights, own, other, scale, deps=()):
    total, model_width = weights.shape
    width = head_count * HEAD_DIM
    rows = own.shape[0] + other.shape[0]
    return pl.pallas_call(
        ordered_after(partial(project_kernel, head_count), 4, deps),
        in_specs=[IN_VMEM] * 4 + [UNREAD] * len(deps),
        out_shape=[
            jax.ShapeDtypeStruct((total, rows), F32),
            jax.ShapeDtypeStruct((width, rows), LOW),
            jax.ShapeDtypeStruct((2 * width, rows), LOW),
        ],
        compiler_params=pltpu.CompilerParams(vmem_limit_bytes=VMEM_BYTES),
        cost_estimate=SMALL_COST,
    )(weights, own, other, scale, *deps)


def sides_kernel(head_count, has_partner, own, arrived, query_grad, projected, scale, triple, terms):
    width = head_count * HEAD_DIM
    root_head = math.sqrt(HEAD_DIM)

    def side(cols):
        gradient = own[cols, :]
        if has_partner:
            gradient = gradient + arrived[cols, :].astype(F32)
        return gradient

    for head in range(head_count):
        cols = pl.ds(head * HEAD_DIM, HEAD_DIM)
        key_cols = pl.ds(width + head * HEAD_DIM, HEAD_DIM)
        head_scale = scale[cols, :]
        query_unit, query_norm = unit_rows(projected[cols, :], axis=0)
        key_unit, key_norm = unit_rows(projected[key_cols, :], axis=0)
        query_scaled = query_grad[cols, :] * root_head
        key_scaled = side(cols)
        terms[cols, :] = jnp.sum(
            query_scaled * query_unit + key_scaled * key_unit, axis=1, keepdims=True
        )
        triple[cols, :] = unit_back(
            query_unit, query_norm, query_scaled * head_scale, axis=0
        ).astype(LOW)
        triple[key_cols, :] = unit_back(
            key_unit, key_norm, key_scaled * head_scale, axis=0
        ).astype(LOW)
    triple[2 * width : 3 * width, :] = side(pl.ds(width, width)).astype(LOW)


def sides_back(head_count, own, arrived, query_grad, projected, scale, deps=()):
    total, rows = projected.shape
    width = head_count * HEAD_DIM
    has_partner = arrived is not None
    if not has_partner:
        arrived = jnp.zeros((16, rows), LOW)
    return pl.pallas_call(
        ordered_after(partial(sides_kernel, head_count, has_partner), 5, deps),
        in_specs=[IN_VMEM] * 5 + [UNREAD] * len(deps),
        out_shape=[
            jax.ShapeDtypeStruct((total, rows), LOW),
            jax.ShapeDtypeStruct((width, 1), F32),
        ],
        compiler_params=pltpu.CompilerParams(vmem_limit_bytes=VMEM_BYTES),
        cost_estimate=SMALL_COST,
    )(own, arrived, query_grad, projected, scale, *deps)


def triple_grad_kernel(count, parts, own_part, me, *refs):
    lefts, rights = refs[:count], refs[count : 3 * count]
    own_out, other_outs = refs[3 * count], refs[3 * count + 1 :]
    right = jnp.concatenate([ref[...] for ref in rights], axis=0)
    rows = lefts[0].shape[0] // parts
    for side in range(2):
        place = me[0] if side == 0 else 1 - me[0]
        left = jnp.concatenate(
            [
                jnp.concatenate(
                    [
                        ref[pl.ds(pl.multiple_of(n * rows + place * own_part, 16), own_part), :]
                        for n in range(parts)
                    ],
                    axis=0,
                )
                for ref in lefts
            ],
            axis=1,
        )
        total = dot(left, right, (1, 0))
        if side == 0:
            own_out[...] = total
        else:
            for n in range(parts):
                other_outs[n][...] = total[n * own_part : (n + 1) * own_part, :].astype(LOW)


def triple_grad(me, parts, lefts, rights, deps=()):
    count = len(lefts)
    total, rows = lefts[0].shape
    own_part = total // parts // 2
    width = rights[0][0].shape[1]
    return pl.pallas_call(
        ordered_after(partial(triple_grad_kernel, count, parts, own_part), 1 + 3 * count, deps),
        in_specs=[pl.BlockSpec(memory_space=pltpu.SMEM)]
        + [IN_VMEM] * (3 * count)
        + [UNREAD] * len(deps),
        out_shape=[jax.ShapeDtypeStruct((parts * own_part, width), F32)]
        + [jax.ShapeDtypeStruct((own_part, width), LOW)] * parts,
        compiler_params=pltpu.CompilerParams(vmem_limit_bytes=VMEM_BYTES),
        cost_estimate=SMALL_COST,
    )(me, *lefts, *[side for right in rights for side in right], *deps)


def attend_kernel(
    head_count, seg_q, place_q, seg_k, place_k, query, key_value, summed, total, heads, bias
):
    blocks, _, rows = key_value.shape
    width = head_count * HEAD_DIM
    for j in range(blocks):
        part = pl.ds(j * rows, rows)
        bias[part, :] = mask_bias(seg_q[...], place_q[...], seg_k[part, :], place_k[part, :])
    for head in range(head_count):
        cols = pl.ds(head * HEAD_DIM, HEAD_DIM)
        value_cols = pl.ds(width + head * HEAD_DIM, HEAD_DIM)
        block_query = query[cols, :]
        row_total = jnp.zeros((1, query.shape[1]), F32)
        acc = jnp.zeros((HEAD_DIM, query.shape[1]), F32)
        for j in range(blocks):
            scores = dot(key_value[j, cols, :], block_query, (0, 0))
            raised = jnp.exp(scores + bias[pl.ds(j * rows, rows), :])
            row_total = row_total + jnp.sum(raised, axis=0, keepdims=True)
            acc = acc + dot(key_value[j, value_cols, :], raised.astype(LOW), (1, 0))
        summed[cols, :] = acc
        total[pl.ds(head, 1), :] = row_total
        heads[cols, :] = (acc / row_total).astype(LOW)


def attend(head_count, places, query, key_value, deps=()):
    blocks, _, rows = key_value.shape
    width, count = query.shape
    return pl.pallas_call(
        ordered_after(partial(attend_kernel, head_count), 6, deps),
        in_specs=[IN_VMEM] * 6 + [UNREAD] * len(deps),
        out_shape=(
            jax.ShapeDtypeStruct((width, count), F32),
            jax.ShapeDtypeStruct((head_count, count), F32),
            jax.ShapeDtypeStruct((width, count), LOW),
        ),
        scratch_shapes=[pltpu.VMEM((blocks * rows, count), F32)],
        compiler_params=pltpu.CompilerParams(vmem_limit_bytes=VMEM_BYTES),
        cost_estimate=SMALL_COST,
    )(*places, query, key_value, *deps)


def attend_back_kernel(
    head_count,
    seg_q,
    place_q,
    seg_k,
    place_k,
    query,
    key_value,
    rows_own,
    rows_other,
    weights,
    summed,
    total,
    query_grad,
    own_grad,
    other_grad,
    bias,
    heads_back,
):
    blocks, _, rows = key_value.shape
    rows_back = jnp.concatenate([rows_own[...], rows_other[...]], axis=0)
    heads_back[...] = dot(weights[...], rows_back, (1, 1), LOW)
    width = head_count * HEAD_DIM
    for j in range(blocks):
        part = pl.ds(j * rows, rows)
        bias[part, :] = mask_bias(seg_q[...], place_q[...], seg_k[part, :], place_k[part, :])
    for head in range(head_count):
        cols = pl.ds(head * HEAD_DIM, HEAD_DIM)
        value_cols = pl.ds(width + head * HEAD_DIM, HEAD_DIM)
        block_query = query[cols, :]
        output_back = heads_back[cols, :].astype(F32)
        row_total = total[pl.ds(head, 1), :]
        summed_back = (output_back / row_total).astype(LOW)
        total_back = -jnp.sum(output_back * summed[cols, :], axis=0, keepdims=True) / (
            row_total * row_total
        )
        acc = jnp.zeros((HEAD_DIM, query.shape[1]), F32)
        for j in range(blocks):
            key_part = key_value[j, cols, :]
            scores = dot(key_part, block_query, (0, 0))
            raised = jnp.exp(scores + bias[pl.ds(j * rows, rows), :])
            raised_back = dot(key_value[j, value_cols, :], summed_back, (0, 0))
            score_back = (raised * (raised_back + total_back)).astype(LOW)
            acc = acc + dot(key_part, score_back, (1, 0))
            key_grad = dot(block_query, score_back, (1, 1))
            value_grad = dot(summed_back, raised.astype(LOW), (1, 1))
            if j == 0:
                own_grad[cols, :] = key_grad
                own_grad[value_cols, :] = value_grad
            else:
                other_grad[j - 1, cols, :] = key_grad.astype(other_grad.dtype)
                other_grad[j - 1, value_cols, :] = value_grad.astype(other_grad.dtype)
        query_grad[cols, :] = acc


def attend_back(head_count, places, query, key_value, rows_back, weights, summed, total, deps=()):
    blocks, both, rows = key_value.shape
    width, count = query.shape
    return pl.pallas_call(
        ordered_after(partial(attend_back_kernel, head_count), 11, deps),
        in_specs=[IN_VMEM] * 11 + [UNREAD] * len(deps),
        out_shape=(
            jax.ShapeDtypeStruct((width, count), F32),
            jax.ShapeDtypeStruct((both, rows), F32),
            jax.ShapeDtypeStruct((blocks - 1, both, rows), LOW if blocks == 2 else F32),
        ),
        scratch_shapes=[pltpu.VMEM((blocks * rows, count), F32), pltpu.VMEM((width, count), LOW)],
        compiler_params=pltpu.CompilerParams(vmem_limit_bytes=VMEM_BYTES),
        cost_estimate=SMALL_COST,
    )(*places, query, key_value, *rows_back, weights, summed, total, *deps)


def sigmoid(values):
    return 1.0 / (1.0 + jnp.exp(-values))


def feed_kernel(
    root_width,
    own,
    other,
    up_weights,
    gate_weights,
    down_weights,
    scale_up,
    scale_gate,
    up_out,
    gate_out,
    hidden_out,
    own_out,
    other_out,
    total,
):
    half = own.shape[0]
    rows = jnp.concatenate([own[...], other[...]], axis=0)
    up = dot(rows, up_weights[...], (1, 1))
    gate = dot(rows, gate_weights[...], (1, 1))
    up_out[...] = up
    gate_out[...] = gate
    gate_scaled = gate * scale_gate[...] * root_width
    hidden = (gate_scaled * sigmoid(gate_scaled) * (up * scale_up[...])).astype(LOW)
    hidden_out[...] = hidden
    part = dot(hidden, down_weights[...], (1, 0))
    step = pl.program_id(0)

    @pl.when(step == 0)
    def _():
        total[...] = part

    @pl.when(step > 0)
    def _():
        total[...] += part

    @pl.when(step == pl.num_programs(0) - 1)
    def _():
        own_out[...] = total[:half, :]
        other_out[...] = total[half:, :].astype(LOW)


def feed_forward(own, other, feed_full, scale_up, scale_gate, deps=()):
    half, width = own.shape
    units = feed_full[0].shape[0]
    tile = units
    held = pl.BlockSpec((half, width), lambda i: (0, 0))
    weight = pl.BlockSpec((tile, width), lambda i: (i, 0))
    scale = pl.BlockSpec((1, tile), lambda i: (0, i))
    piece = pl.BlockSpec((2 * half, tile), lambda i: (0, i))
    kept = jax.ShapeDtypeStruct((2 * half, units), F32)
    return pl.pallas_call(
        ordered_after(partial(feed_kernel, math.sqrt(width)), 7, deps),
        grid=(units // tile,),
        in_specs=[held, held, weight, weight, weight, scale, scale] + [UNREAD] * len(deps),
        out_specs=[piece, piece, piece, held, held],
        out_shape=[
            kept,
            kept,
            jax.ShapeDtypeStruct((2 * half, units), LOW),
            jax.ShapeDtypeStruct((half, width), F32),
            jax.ShapeDtypeStruct((half, width), LOW),
        ],
        scratch_shapes=[pltpu.VMEM((2 * half, width), F32)],
        compiler_params=pltpu.CompilerParams(vmem_limit_bytes=LARGE_VMEM_BYTES),
        cost_estimate=SMALL_COST,
    )(own, other, *feed_full, scale_up, scale_gate, *deps)


def feed_back_kernel(
    root_width,
    own,
    other,
    up_ref,
    gate_ref,
    up_weights,
    gate_weights,
    down_weights,
    scale_up,
    scale_gate,
    up_out,
    gate_out,
    terms_out,
    own_out,
    other_out,
    total,
):
    half = own.shape[0]
    rows = jnp.concatenate([own[...], other[...]], axis=0)
    hidden_back = dot(rows, down_weights[...], (1, 1))
    up = up_ref[...]
    gate = gate_ref[...]
    gate_scaled = gate * scale_gate[...] * root_width
    sigmoid_gate = sigmoid(gate_scaled)
    up_back = hidden_back * (gate_scaled * sigmoid_gate)
    gate_back = (
        hidden_back
        * (up * scale_up[...])
        * (sigmoid_gate * (1.0 + gate_scaled * (1.0 - sigmoid_gate)))
    )
    terms_out[...] = jnp.concatenate(
        [
            jnp.sum(up_back * up, axis=0, keepdims=True),
            jnp.sum(gate_back * gate, axis=0, keepdims=True) * root_width,
        ],
        axis=0,
    )
    up_low = (up_back * scale_up[...]).astype(LOW)
    gate_low = (gate_back * scale_gate[...] * root_width).astype(LOW)
    up_out[...] = up_low
    gate_out[...] = gate_low
    part = dot(up_low, up_weights[...], (1, 0)) + dot(gate_low, gate_weights[...], (1, 0))
    step = pl.program_id(0)

    @pl.when(step == 0)
    def _():
        total[...] = part

    @pl.when(step > 0)
    def _():
        total[...] += part

    @pl.when(step == pl.num_programs(0) - 1)
    def _():
        own_out[...] = total[:half, :]
        other_out[...] = total[half:, :].astype(LOW)


def feed_backward(own, other, up, gate, feed_full, scale_up, scale_gate, deps=()):
    half, width = own.shape
    units = feed_full[0].shape[0]
    tile = units
    held = pl.BlockSpec((half, width), lambda i: (0, 0))
    weight = pl.BlockSpec((tile, width), lambda i: (i, 0))
    scale = pl.BlockSpec((1, tile), lambda i: (0, i))
    piece = pl.BlockSpec((2 * half, tile), lambda i: (0, i))
    return pl.pallas_call(
        ordered_after(partial(feed_back_kernel, math.sqrt(width)), 9, deps),
        grid=(units // tile,),
        in_specs=[held, held, piece, piece, weight, weight, weight, scale, scale]
        + [UNREAD] * len(deps),
        out_specs=[piece, piece, pl.BlockSpec((2, tile), lambda i: (0, i)), held, held],
        out_shape=[
            jax.ShapeDtypeStruct((2 * half, units), LOW),
            jax.ShapeDtypeStruct((2 * half, units), LOW),
            jax.ShapeDtypeStruct((2, units), F32),
            jax.ShapeDtypeStruct((half, width), F32),
            jax.ShapeDtypeStruct((half, width), LOW),
        ],
        scratch_shapes=[pltpu.VMEM((2 * half, width), F32)],
        compiler_params=pltpu.CompilerParams(vmem_limit_bytes=LARGE_VMEM_BYTES),
        cost_estimate=SMALL_COST,
    )(own, other, up, gate, *feed_full, scale_up, scale_gate, *deps)


def weight_grad_kernel(count, *refs):
    lefts, rights = refs[:count], refs[count : 3 * count]
    own_out, other_out = refs[3 * count :]
    part = own_out.shape[0]
    right = jnp.concatenate([ref[...] for ref in rights], axis=0)
    for side in range(2):
        left = jnp.concatenate([ref[:, side * part : (side + 1) * part] for ref in lefts], axis=0)
        total = dot(left, right, (0, 0))
        if side == 0:
            own_out[...] = total
        else:
            other_out[...] = total.astype(LOW)


def weight_grad(lefts, rights, deps=()):
    count = len(lefts)
    rows, units = lefts[0].shape
    half, width = rights[0][0].shape
    part = units // 2
    return pl.pallas_call(
        ordered_after(partial(weight_grad_kernel, count), 3 * count, deps),
        in_specs=[IN_VMEM] * (3 * count) + [UNREAD] * len(deps),
        out_shape=[
            jax.ShapeDtypeStruct((part, width), F32),
            jax.ShapeDtypeStruct((part, width), LOW),
        ],
        compiler_params=pltpu.CompilerParams(vmem_limit_bytes=LARGE_VMEM_BYTES),
        cost_estimate=SMALL_COST,
    )(*lefts, *[side for right in rights for side in right], *deps)


def first_part(pair, partner, token, rate):
    attention_unit, attention_norm = unit_rows(add_low(pair[...], partner[...]))
    token_float = token[...].astype(F32)
    after, after_norm = unit_rows(token_float + rate * (attention_unit - token_float))
    return (attention_unit, attention_norm, token_float, after, after_norm)


def normed_kernel(pair, partner, token, rates, normed_out):
    normed_out[...] = first_part(pair, partner, token, rates[0:1, :])[3].astype(LOW)


def output_kernel(
    pair, partner, token, feed_pair, feed_partner, cotangent, rates, output_out, second_out, back_out, term_out
):
    after = first_part(pair, partner, token, rates[0:1, :])[3]
    rate = rates[1:2, :]
    feed_unit, feed_norm = unit_rows(add_low(feed_pair[...], feed_partner[...]))
    output, output_norm = unit_rows(after + rate * (feed_unit - after))
    output_out[...] = output
    second_back = unit_back(output, output_norm, cotangent[...].astype(F32))
    second_out[...] = second_back
    back_out[...] = unit_back(feed_unit, feed_norm, second_back * rate).astype(LOW)
    term = jnp.sum(second_back * (feed_unit - after), axis=0, keepdims=True)

    @pl.when(pl.program_id(0) == 0)
    def _():
        term_out[...] = term

    @pl.when(pl.program_id(0) > 0)
    def _():
        term_out[...] += term


def first_back_kernel(
    pair, partner, token, second, grad_pair, grad_partner, rates, skip_out, back_out, term_out
):
    rate = rates[0:1, :]
    attention_unit, attention_norm, token_float, after, after_norm = first_part(
        pair, partner, token, rate
    )
    after_grad = second[...] * (1.0 - rates[1:2, :]) + add_low(grad_pair[...], grad_partner[...])
    first_back = unit_back(after, after_norm, after_grad)
    skip_out[...] = first_back * (1.0 - rate)
    back_out[...] = unit_back(attention_unit, attention_norm, first_back * rate).astype(LOW)
    term = jnp.sum(first_back * (attention_unit - token_float), axis=0, keepdims=True)

    @pl.when(pl.program_id(0) == 0)
    def _():
        term_out[...] = term

    @pl.when(pl.program_id(0) > 0)
    def _():
        term_out[...] += term


def rowwise(body, arrays, rates, outs, has_term, deps=()):
    half, width = arrays[0].shape
    tile = 128 if half % 128 == 0 else half
    flat = pl.BlockSpec((tile, width), lambda i: (i, 0))
    term = [pl.BlockSpec((1, width), lambda i: (0, 0))] if has_term else []
    term_shape = [jax.ShapeDtypeStruct((1, width), F32)] if has_term else []
    return pl.pallas_call(
        ordered_after(body, len(arrays) + 1, deps),
        grid=(half // tile,),
        in_specs=[flat] * len(arrays)
        + [pl.BlockSpec((2, width), lambda i: (0, 0))]
        + [UNREAD] * len(deps),
        out_specs=[flat] * len(outs) + term,
        out_shape=[jax.ShapeDtypeStruct((half, width), kind) for kind in outs] + term_shape,
        compiler_params=pltpu.CompilerParams(vmem_limit_bytes=VMEM_BYTES),
        cost_estimate=SMALL_COST,
    )(*arrays, rates, *deps)


def adam_step(master, gradient, first_state, second_state, step_rate, is_matrix):
    moment = BETA_ONE * first_state + (1.0 - BETA_ONE) * gradient
    variance = BETA_TWO * second_state + (1.0 - BETA_TWO) * gradient * gradient
    update = moment / CORR_ONE / (jnp.sqrt(variance / CORR_TWO) + ADAM_EPS)
    updated = master - step_rate * (update + DECAY * master)
    if is_matrix:
        updated = unit_only(updated)
    return (moment, variance, updated)


def outer_step(master, shift, outer_state, is_matrix):
    momentum = OUTER_MOMENTUM * outer_state + shift
    result = master - OUTER_RATE * (shift + OUTER_MOMENTUM * momentum)
    if is_matrix:
        result = unit_only(result)
    return (momentum, result)


def row_tile(rows):
    for size in (160, 128):
        if rows % size == 0:
            return size
    return rows


def adam_kernel(has_partner, chunks, offset, own, partner, master, first, second, *rest):
    del offset
    gradient_out, moment_out, variance_out = rest[-3 - chunks : -chunks]
    gradient = own[...]
    if has_partner:
        gradient = gradient + partner[...].astype(F32)
    moment, variance, updated = adam_step(
        master[0], gradient, first[0, 0], second[0, 0], MATRIX_RATE, True
    )
    gradient_out[0, 0] = gradient
    moment_out[0, 0] = moment
    variance_out[0, 0] = variance
    shift = (master[0] - updated).astype(LOW)
    each = pl.num_programs(0) // chunks
    for n in range(chunks):

        @pl.when(pl.program_id(0) // each == n)
        def _(n=n):
            rest[n - chunks][...] = shift


def adam_slab(which, chunks, own_block, gradient, partner, master, first, second, earlier, deps=()):
    slabs, rows, width = master.shape
    tile = row_tile(rows)
    steps = rows // tile
    each = steps // chunks
    has_partner = partner is not None
    if not has_partner:
        partner = jnp.zeros((tile, width), LOW)
    flat = pl.BlockSpec((tile, width), lambda i, at: (i, 0))
    held = pl.BlockSpec((tile, width), lambda i, at: (at[0] * steps + i, 0))
    once = pl.BlockSpec((tile, width), lambda i, at: (0, 0))
    slab = pl.BlockSpec((1, tile, width), lambda i, at: (which, i, 0))
    grouped = pl.BlockSpec((1, 1, tile, width), lambda i, at: (0, which, i, 0))
    whole = jax.ShapeDtypeStruct((1, slabs, rows, width), F32)
    earlier = () if earlier is None else earlier
    pieces = [
        pl.BlockSpec((tile, width), lambda i, at, n=n: (jnp.clip(i - n * each, 0, each - 1), 0))
        for n in range(chunks)
    ]
    return pl.pallas_call(
        partial(adam_kernel, has_partner, chunks),
        grid_spec=pltpu.PrefetchScalarGridSpec(
            num_scalar_prefetch=1,
            grid=(steps,),
            in_specs=[held, flat if has_partner else once, slab, grouped, grouped]
            + [UNREAD] * (len(earlier) + len(deps)),
            out_specs=[grouped, grouped, grouped] + pieces,
        ),
        out_shape=[whole, whole, whole]
        + [jax.ShapeDtypeStruct((rows // chunks, width), LOW)] * chunks,
        input_output_aliases={6 + n: n for n in range(len(earlier))},
        compiler_params=pltpu.CompilerParams(vmem_limit_bytes=VMEM_BYTES),
        cost_estimate=SMALL_COST,
    )(own_block, gradient, partner, master, first, second, *earlier, *deps)


TAG = jax.ShapeDtypeStruct((8, 128), F32)


def outer_kernel(group_count, at_end, whole, back, master, outer, *rest):
    momentum_out, result_out, tag_out = rest[-3:]
    shift = jnp.where(at_end[0] == 1, back[...].astype(F32), whole[...].astype(F32)) / group_count
    momentum, result = outer_step(master[0], shift, outer[0], True)
    momentum_out[0] = momentum
    result_out[0] = result
    tag_out[...] = jnp.zeros_like(tag_out)


def outer_slab(which, chunk, group_count, at_end, whole, back, master, outer, earlier, deps):
    slabs, rows, width = master.shape
    part = whole.shape[0]
    tile = row_tile(part)
    steps = part // tile
    flat = pl.BlockSpec((tile, width), lambda i, at: (i, 0))
    slab = pl.BlockSpec((1, tile, width), lambda i, at: (which, chunk * steps + i, 0))
    result = jax.ShapeDtypeStruct((slabs, rows, width), F32)
    earlier = () if earlier is None else earlier
    return pl.pallas_call(
        partial(outer_kernel, group_count),
        grid_spec=pltpu.PrefetchScalarGridSpec(
            num_scalar_prefetch=1,
            grid=(steps,),
            in_specs=[flat, flat, slab, slab] + [UNREAD] * (len(earlier) + len(deps)),
            out_specs=[slab, slab, pl.BlockSpec(TAG.shape, lambda i, at: (0, 0))],
        ),
        out_shape=[result, result, TAG],
        input_output_aliases={5 + n: n for n in range(len(earlier))},
        compiler_params=pltpu.CompilerParams(vmem_limit_bytes=VMEM_BYTES),
        cost_estimate=SMALL_COST,
    )(at_end, whole, back, master, outer, *earlier, *deps)


class MatrixSteps:
    def __init__(self, chunks, at_end, master, first, second, outer):
        self.chunks = chunks
        self.at_end = at_end.reshape(1)
        self.arrays = (master, first, second)
        self.outer_state = outer
        self.inner_outs = None
        self.outer_outs = None
        self.sums = {}
        self.shifts = {}

    def inner(self, which, gradient, deps, chain=True):
        own, partner, block = gradient
        outs = adam_slab(
            which, self.chunks, block, own, partner, *self.arrays, self.inner_outs, deps
        )
        self.inner_outs = outs[:3]
        if chain:
            self.sums[which] = [group_sum(shift) for shift in outs[3:]]
        else:
            self.shifts[which] = list(outs[3:])
        return outs[3]

    def pairs(self, which):
        return [step[0] for step in self.sums[which]]

    def wholes(self, which):
        return [step[1] for step in self.sums[which]]

    def outer(self, which, tags, also=()):
        for chunk, (_, whole, back) in enumerate(self.sums[which]):
            if chunk < len(also):
                tags = tags + also[chunk]
            *self.outer_outs, tag = outer_slab(
                which,
                chunk,
                lax.axis_size("group"),
                self.at_end,
                whole,
                back,
                self.arrays[0],
                self.outer_state,
                self.outer_outs,
                tags,
            )
            tags = [tag]
        return tags

    def outs(self):
        return (*self.inner_outs, *self.outer_outs)


def place_kernel(core, own, other, *rest):
    out = rest[-1]

    @pl.when(pl.program_id(0) == 0)
    def _():
        out[0, 0] = own[...]

    @pl.when(pl.program_id(0) == 1)
    def _():
        out[0, 0] = other[...]


def place_rows(which, count, core, own, other, earlier, deps=()):
    half, width = own.shape
    held = pl.BlockSpec((half, width), lambda i, at: (0, 0))
    earlier = () if earlier is None else (earlier,)
    return pl.pallas_call(
        place_kernel,
        grid_spec=pltpu.PrefetchScalarGridSpec(
            num_scalar_prefetch=1,
            grid=(2,),
            in_specs=[held, held] + [UNREAD] * (len(earlier) + len(deps)),
            out_specs=pl.BlockSpec(
                (1, 1, half, width), lambda i, at: (0, which, lax.rem(at[0] + i, 2), 0)
            ),
        ),
        out_shape=jax.ShapeDtypeStruct((1, count, 2 * half, width), F32),
        input_output_aliases={3: 0} if earlier else {},
        compiler_params=pltpu.CompilerParams(vmem_limit_bytes=VMEM_BYTES),
        cost_estimate=SMALL_COST,
    )(core, own, other, *earlier, *deps)


def on_device(
    tokens,
    cotangent,
    segments,
    shard_order,
    attention_weights,
    feedforward_weights,
    head_scales,
    hidden_scales,
    residual_rates,
    attention_first,
    feedforward_first,
    heads_first,
    hidden_first,
    rates_first,
    attention_second,
    feedforward_second,
    heads_second,
    hidden_second,
    rates_second,
    attention_outer,
    feedforward_outer,
    heads_outer,
    hidden_outer,
    rates_outer,
):
    micro_count, rows, model_width = tokens.shape[1:]
    half = rows // 2
    ctx_count = lax.axis_size("ctx")
    pair = ctx_count == 2
    group_count = lax.axis_size("group")
    own_rows = attention_weights.shape[1]
    own_units = feedforward_weights.shape[1]
    head_width = own_rows * ctx_count
    head_count = head_width // HEAD_DIM
    units = own_units * ctx_count
    root_head = math.sqrt(HEAD_DIM)
    root_width = math.sqrt(model_width)
    me = lax.axis_index("ctx")
    ctx_first = me == 0
    core_index = lax.rem(lax.axis_index("tensor"), 2).reshape(1)
    core_first = core_index[0] == 0
    even_group = lax.rem(lax.axis_index("group"), 2) == 0
    micros = range(micro_count)
    at_end = lax.axis_index("group")
    at_end = ((at_end == 0) | (at_end == group_count - 1)).astype(jnp.int32)

    attention_low = attention_weights.astype(LOW)
    feed_low = feedforward_weights.astype(LOW)
    small_low = jnp.concatenate(
        [head_scales, hidden_scales[0], hidden_scales[1], residual_rates[0], residual_rates[1]]
    ).astype(LOW)
    own_cols = residual_rates.shape[1]
    if pair:
        part = own_rows // 2
        piece = jnp.where(even_group, attention_low[:3, :part], attention_low[:3, part:])
        triple_across = trade(piece, "ctx", 1)
        triple_other = ordered(even_group, triple_across, trade(triple_across, "group", 1), 1)
        triple_weights = ordered(ctx_first, attention_low[:3], triple_other, 1)
        small_other = trade(small_low, "ctx", 1)
        cuts = [own_rows, own_units, own_units, own_cols, own_cols]
        small_pieces = []
        start = 0
        for which, size in enumerate(cuts):
            mine = small_low[start : start + size].astype(F32)
            theirs = small_other[start : start + size].astype(F32)
            start += size
            if which in (1, 2):
                small_pieces.append(jnp.concatenate([mine, theirs]))
            else:
                small_pieces.append(ordered(ctx_first, mine, theirs, 0))
        scale_heads, scale_up, scale_gate, rate_attention, rate_feed = small_pieces
    else:
        triple_weights = lax.all_gather(attention_low[:3], "ctx", axis=1, tiled=True)
        scale_heads = lax.all_gather(head_scales.astype(LOW), "ctx", axis=0, tiled=True).astype(F32)
        scale_up, scale_gate = lax.all_gather(
            hidden_scales.astype(LOW), "ctx", axis=1, tiled=True
        ).astype(F32)
        rate_attention, rate_feed = lax.all_gather(
            residual_rates.astype(LOW), "ctx", axis=1, tiled=True
        ).astype(F32)
    triple_weights = triple_weights.reshape(3 * head_width, model_width)
    scale_column = scale_heads.reshape(head_width, 1)

    token_halves = tokens[0].reshape(micro_count, 2, half, model_width)
    token_own = jnp.where(core_first, token_halves[:, 0], token_halves[:, 1])
    token_other = jnp.where(core_first, token_halves[:, 1], token_halves[:, 0])
    cotangent_halves = cotangent[0].reshape(micro_count, 2, half, model_width)
    cotangent_own = jnp.where(core_first, cotangent_halves[:, 0], cotangent_halves[:, 1])

    if pair:
        block_ids = jnp.stack([me, 1 - me])
    else:
        block_ids = lax.rem(me + jnp.arange(ctx_count, dtype=jnp.int32), ctx_count)
    table = jnp.arange(ctx_count, dtype=jnp.int32)
    order_of = jnp.sum(
        jnp.where(block_ids[:, None] == table[None, :], shard_order[None, :], 0), axis=1
    )
    local = jnp.arange(rows, dtype=jnp.int32)
    local = jnp.where(core_first, local, lax.rem(local + half, rows))
    place_blocks = order_of[:, None] * rows + local[None, :]
    segment_blocks = segments[0].reshape(micro_count, ctx_count, rows)
    segment_blocks = jnp.sum(
        jnp.where(
            (order_of[:, None] == table[None, :])[None, :, :, None], segment_blocks[:, None], 0
        ),
        axis=2,
    )
    segment_blocks = jnp.where(
        core_first,
        segment_blocks,
        jnp.concatenate([segment_blocks[:, :, half:], segment_blocks[:, :, :half]], axis=2),
    )
    places = [
        (
            segment_blocks[b, 0][None, :],
            place_blocks[0][None, :],
            segment_blocks[b].reshape(ctx_count * rows, 1),
            place_blocks.reshape(ctx_count * rows, 1),
        )
        for b in micros
    ]

    projections, query_low, local_sides = [], [], []
    for b in micros:
        projected, query, key_value = project(
            head_count,
            triple_weights,
            token_own[b],
            token_other[b],
            scale_column,
            projections[-1:],
        )
        projections.append(projected)
        query_low.append(query)
        local_sides.append(key_value)

    def all_sides(b, deps):
        if pair:
            sent = tie(local_sides[b], *deps) if deps else local_sides[b]
            return jnp.stack([local_sides[b], trade(sent, "ctx", 1)])
        return jnp.take(lax.all_gather(local_sides[b], "ctx", axis=0), block_ids, axis=0)

    def across_and_along(source, deps):
        part = source.shape[0] // 2
        piece = tie(jnp.where(even_group, source[:part], source[part:]), *deps)
        across = trade(piece, "ctx", 1)
        return (across, ordered(even_group, across, trade(across, "group", 1), 0))

    arrivals = []
    feed_full = []

    def gather_feed(which, deps):
        across, other = across_and_along(feed_low[which], deps)
        arrivals.append(across)
        feed_full.append(jnp.concatenate([feed_low[which], other], axis=0))

    if pair:
        gather_feed(0, [triple_across])
        _, output_other = across_and_along(attention_low[3], [triple_across])
        output_weights = ordered(ctx_first, attention_low[3], output_other, 0)
    else:
        output_weights = lax.all_gather(attention_low[3], "ctx", axis=0, tiled=True)

    rates_both = jnp.stack([rate_attention, rate_feed])
    scale_up = scale_up.reshape(1, units)
    scale_gate = scale_gate.reshape(1, units)
    summeds, totals, heads_lows, attention_sums, normed_rows = [], [], [], [], []

    def normed_part(b, deps):
        (normed_low,) = rowwise(
            normed_kernel, attention_sums[b], rates_both, [LOW], False, deps
        )
        normed_rows.append((normed_low, trade(normed_low, "tensor", 1)))

    last = micro_count - 1
    key_values = []
    for b in micros:
        if b < last:
            key_values.append(all_sides(b, []))
        if b == last:
            if pair:
                for which in (1, 2):
                    gather_feed(which, totals[:1])
            key_values.append(all_sides(b, totals[-1:]))
        deps = totals[-1:]
        if b == last:
            for n in range(last):
                normed_part(n, deps + arrivals[1:2] * (n == last - 1))
                deps = [normed_rows[-1][0]]
            deps = deps + arrivals[2:]
        summed, total, heads_low = attend(
            head_count, places[b], query_low[b], key_values[b], deps
        )
        summeds.append(summed)
        totals.append(total)
        heads_lows.append(heads_low)
        attention_sums.append((*tensor_sum(*to_rows(heads_low, output_weights)), token_own[b]))

    if not pair:
        feed_full = list(lax.all_gather(feed_low, "ctx", axis=1, tiled=True))
    up_weights, gate_weights, down_weights = feed_full
    ups, gates, hidden_rows, feed_parts = [], [], [], []
    for b in micros:
        if b == last:
            normed_part(b, [feed_parts[-1][1]] if b > 0 else totals[-1:])
        up, gate, hidden, own_part, other_part = feed_forward(
            *normed_rows[b],
            feed_full,
            scale_up,
            scale_gate,
            [totals[-1] if b == 0 else feed_parts[-1][1]],
        )
        ups.append(up)
        gates.append(gate)
        hidden_rows.append(hidden)
        feed_parts.append((own_part, other_part))

    outputs, second_backs, feed_back_rows, feed_rate_terms = [], [], [], []
    up_back_rows, gate_back_rows, hidden_terms, grad_sums = [], [], [], []
    skips, attention_back_rows, attention_rate_terms = [], [], []
    attention_grads = []
    down_grad = None

    def output_part(b, deps):
        output, second_back, feed_back, term = rowwise(
            output_kernel,
            (*attention_sums[b], *tensor_sum(*feed_parts[b]), cotangent_own[b]),
            rates_both,
            [F32, F32, LOW],
            True,
            deps,
        )
        outputs.append(output)
        second_backs.append(second_back)
        feed_rate_terms.append(term)
        feed_back_rows.append((feed_back, trade(feed_back, "tensor", 1)))

    def feed_part_back(b, deps):
        up_low, gate_low, terms, own_part, other_part = feed_backward(
            *feed_back_rows[b], ups[b], gates[b], feed_full, scale_up, scale_gate, deps
        )
        up_back_rows.append(up_low)
        gate_back_rows.append(gate_low)
        hidden_terms.append(terms)
        grad_sums.append(tensor_sum(own_part, other_part))

    def first_part_back(b, deps):
        skip, attention_back, term = rowwise(
            first_back_kernel,
            (*attention_sums[b], second_backs[b], *grad_sums[b]),
            rates_both,
            [F32, LOW],
            True,
            deps,
        )
        skips.append(skip)
        attention_rate_terms.append(term)
        attention_back_rows.append((attention_back, trade(attention_back, "tensor", 1)))

    def attention_part_back(b, deps):
        attention_grads.append(
            attend_back(
                head_count,
                places[b],
                query_low[b],
                key_values[b],
                attention_back_rows[b],
                output_weights,
                summeds[b],
                totals[b],
                deps,
            )
        )

    def to_owner(gradient, in_order):
        if not pair:
            summed_rows = lax.psum_scatter(gradient, "ctx", scatter_dimension=0, tiled=True)
            return (summed_rows, None, jnp.zeros((1,), jnp.int32))
        size = gradient.shape[0] // 2
        other = gradient[size:]
        block = jnp.zeros((1,), jnp.int32)
        if in_order:
            other = jnp.where(ctx_first, gradient[size:], gradient[:size])
            block = me.reshape(1)
        return (gradient, trade(other.astype(LOW), "ctx", 1), block)

    def feed_gradient(lefts, rights, deps):
        if not pair:
            right = jnp.concatenate([side for entry in rights for side in entry], axis=0)
            grad = to_owner(dot(jnp.concatenate(lefts, axis=0), right, (0, 0)), False)
            return (grad, grad[0])
        own, other = weight_grad(lefts, rights, deps)
        return ((own, trade(other, "ctx", 1), jnp.zeros((1,), jnp.int32)), own)

    triples, head_terms, input_sums = [], [], []

    def sides_part_back(b, deps):
        query_grad, own_grad, other_grad = attention_grads[b]
        arrived = None
        if pair:
            arrived = side_arrivals[b]
        else:
            sides = jnp.concatenate([own_grad[None], other_grad], axis=0)
            sides = jnp.take(sides, lax.rem(table - me + ctx_count, ctx_count), axis=0)
            own_grad = lax.psum_scatter(sides, "ctx", scatter_dimension=0)
        triple, terms = sides_back(
            head_count, own_grad, arrived, query_grad, projections[b], scale_column, deps
        )
        triples.append(triple)
        head_terms.append(terms)
        input_sums.append(tensor_sum(*to_rows(triple, triple_weights)))

    tag = feed_parts[-1][1]
    for b in micros:
        output_part(b, [tag])
        if b == last:
            down_grad, tag = feed_gradient(hidden_rows, feed_back_rows, [])
            first_part_back(0, [tag])
            tag = attention_rate_terms[0]
        feed_part_back(b, [tag])
        tag = hidden_terms[b]
    up_grad, tag = feed_gradient(up_back_rows, normed_rows, [tag])
    gate_grad, tag = feed_gradient(gate_back_rows, normed_rows, [tag])
    feed_steps = MatrixSteps(
        2 if own_units % 320 == 0 else 1,
        at_end,
        feedforward_weights,
        feedforward_first,
        feedforward_second,
        feedforward_outer,
    )
    attention_steps = MatrixSteps(
        1,
        at_end,
        attention_weights,
        attention_first,
        attention_second,
        attention_outer,
    )
    side_arrivals = []
    arrived_grads = {0: [down_grad[1]], 1: [up_grad[1]]} if pair else {}
    for b in micros:
        if b > 0:
            first_part_back(b, [tag])
            tag = attention_rate_terms[b]
        attention_part_back(b, [tag] + arrived_grads.get(b, []))
        tag = attention_grads[b][0]
        if pair:
            side_arrivals.append(trade(attention_grads[b][2][0], "ctx", 1))
        if b == last - 1:
            tag = feed_steps.inner(2, down_grad, [tag])
    if pair:
        own, other = triple_grad(me.reshape(1), 1, heads_lows, attention_back_rows, [tag])
        output_grad = (own, trade(other, "ctx", 1), jnp.zeros((1,), jnp.int32))
        output_arrived = [output_grad[1]]
        gate_arrived = [gate_grad[1]]
        tag = own
    else:
        right = jnp.concatenate([side for rows_of in attention_back_rows for side in rows_of], axis=0)
        output_grad = to_owner(dot(jnp.concatenate(heads_lows, axis=1), right, (1, 0)), True)
        output_arrived = []
        gate_arrived = []
    token_sides = [(token_own[b], token_other[b]) for b in micros]
    tag = feed_steps.inner(0, up_grad, [tag])
    tag = feed_steps.inner(
        1, gate_grad, [tag] + feed_steps.pairs(2)[:1] + side_arrivals[:1], False
    )
    for b in micros:
        deps = [tag]
        if b == 0:
            deps += feed_steps.pairs(2) + side_arrivals[1:2]
        elif b < last:
            deps += side_arrivals[-1:]
        else:
            deps += feed_steps.pairs(0)[:1] + feed_steps.wholes(2)[:1] + output_arrived
        sides_part_back(b, deps)
        tag = head_terms[b]
    if pair:
        own, *others = triple_grad(me.reshape(1), 3, triples, token_sides, [tag])
        tag = own
        projection_grads = [
            (own, trade(others[which], "ctx", 1), jnp.full((1,), which, jnp.int32))
            for which in range(3)
        ]
    else:
        triple_all = dot(
            jnp.concatenate(triples, axis=1),
            jnp.concatenate([side for sides in token_sides for side in sides], axis=0),
            (1, 0),
        ).reshape(3, head_width, model_width)
        projection_grads = [to_owner(triple_all[which], True) for which in range(3)]
    tag = attention_steps.inner(3, output_grad, [tag] + feed_steps.wholes(2) + feed_steps.pairs(0), False)

    block_output = None
    for b in micros:
        block_output = place_rows(
            b,
            micro_count,
            core_index,
            outputs[b],
            trade(outputs[b], "tensor", 1),
            block_output,
            [head_terms[0]],
        )

    input_gradient = None

    def place_input(b, deps):
        input_own = added([skips[b], *input_sums[b]], F32)
        return place_rows(
            b,
            micro_count,
            core_index,
            input_own,
            trade(input_own, "tensor", 1),
            input_gradient,
            deps,
        )

    input_gradient = place_input(0, [tag])
    tags = feed_steps.outer(2, [tag])
    tag = attention_steps.inner(0, projection_grads[0], tags, False)
    input_gradient = place_input(1, [tag])
    for which in (1, 2):
        tag = attention_steps.inner(which, projection_grads[which], [tag], False)
    tags = feed_steps.outer(0, [tag])
    for b in micros[2:]:
        input_gradient = place_input(b, [tag])
    rate_terms = jnp.concatenate([sum(attention_rate_terms), sum(feed_rate_terms)], axis=0)
    rate_terms = rate_terms + trade(rate_terms, "tensor", 1)
    head_terms = sum(head_terms).reshape(head_width)
    hidden_terms = sum(hidden_terms)
    if pair:
        heads_own = jnp.where(ctx_first, head_terms[:own_rows], head_terms[own_rows:])
        heads_other = jnp.where(ctx_first, head_terms[own_rows:], head_terms[:own_rows])
        rates_own = jnp.where(ctx_first, rate_terms[:, :own_cols], rate_terms[:, own_cols:])
        rates_other = jnp.where(ctx_first, rate_terms[:, own_cols:], rate_terms[:, :own_cols])
        flat = jnp.concatenate(
            [heads_other, hidden_terms[:, own_units:].reshape(-1), rates_other.reshape(-1)]
        )
        flat = trade(flat, "ctx", 1)
        heads_grad = heads_own + flat[:own_rows]
        hidden_grad = hidden_terms[:, :own_units] + flat[
            own_rows : own_rows + 2 * own_units
        ].reshape(2, own_units)
        rates_grad = rates_own + flat[own_rows + 2 * own_units :].reshape(2, own_cols)
    else:
        heads_grad = lax.psum_scatter(head_terms, "ctx", scatter_dimension=0, tiled=True)
        hidden_grad = lax.psum_scatter(hidden_terms, "ctx", scatter_dimension=1, tiled=True)
        rates_grad = lax.psum_scatter(rate_terms, "ctx", scatter_dimension=1, tiled=True)

    masters = (head_scales, hidden_scales, residual_rates)
    firsts = (heads_first[0], hidden_first[0], rates_first[0])
    seconds = (heads_second[0], hidden_second[0], rates_second[0])
    outers = (heads_outer, hidden_outer, rates_outer)
    small_grads = (heads_grad, hidden_grad, rates_grad)
    small_moments, small_variances, small_shifts = [], [], []
    for which in range(3):
        moment, variance, updated = adam_step(
            masters[which],
            small_grads[which],
            firsts[which],
            seconds[which],
            SCALE_RATE,
            False,
        )
        small_moments.append(moment)
        small_variances.append(variance)
        small_shifts.append((masters[which] - updated).reshape(-1))
    shift_flat = jnp.concatenate(small_shifts)
    flat_size = shift_flat.size
    flat_rows = -(-flat_size // 1024) * 8
    shift_flat = jnp.pad(shift_flat, (0, flat_rows * 128 - flat_size)).reshape(flat_rows, 128)
    feed_shifts = feed_steps.shifts[1]
    attention_shifts = attention_steps.shifts
    *chained, shift_flat = chain_sum(
        [*feed_shifts, *[attention_shifts[which][0] for which in (3, 0, 1, 2)], shift_flat], tags
    )
    shift_flat = shift_flat.reshape(-1)[:flat_size] / group_count
    feed_steps.sums[1] = [(None, total, total) for total in chained[: len(feed_shifts)]]
    for which, total in zip((3, 0, 1, 2), chained[len(feed_shifts) :]):
        attention_steps.sums[which] = [(None, total, total)]
    tags = feed_steps.outer(1, [])
    for which in (3, 0, 1, 2):
        tags = attention_steps.outer(which, tags)
    feed_outs = feed_steps.outs()
    attention_outs = attention_steps.outs()

    small_momenta, small_results = [], []
    start = 0
    for which in range(3):
        size = masters[which].size
        shift = shift_flat[start : start + size].reshape(masters[which].shape)
        start += size
        momentum, result = outer_step(masters[which], shift, outers[which], False)
        small_momenta.append(momentum)
        small_results.append(result)

    return (
        block_output,
        input_gradient,
        attention_outs[0],
        feed_outs[0],
        *[entry[None] for entry in small_grads],
        attention_outs[1],
        feed_outs[1],
        *[entry[None] for entry in small_moments],
        attention_outs[2],
        feed_outs[2],
        *[entry[None] for entry in small_variances],
        attention_outs[3],
        feed_outs[3],
        *small_momenta,
        attention_outs[4],
        feed_outs[4],
        *small_results,
    )


def solution(mesh):
    placed = (
        P("group", None, "ctx", None),
        P("group", None, "ctx", None),
        P("group", None, None),
        P(),
        P(None, ("tensor", "ctx"), None),
        P(None, ("tensor", "ctx"), None),
        P(("tensor", "ctx")),
        P(None, ("tensor", "ctx")),
        P(None, "ctx"),
        P("group", None, ("tensor", "ctx"), None),
        P("group", None, ("tensor", "ctx"), None),
        P("group", ("tensor", "ctx")),
        P("group", None, ("tensor", "ctx")),
        P("group", None, "ctx"),
        P("group", None, ("tensor", "ctx"), None),
        P("group", None, ("tensor", "ctx"), None),
        P("group", ("tensor", "ctx")),
        P("group", None, ("tensor", "ctx")),
        P("group", None, "ctx"),
        P(None, ("tensor", "ctx"), None),
        P(None, ("tensor", "ctx"), None),
        P(("tensor", "ctx")),
        P(None, ("tensor", "ctx")),
        P(None, "ctx"),
    )
    return jax.shard_map(
        on_device,
        mesh=mesh,
        in_specs=placed,
        out_specs=(
            P("group", None, "ctx", None),
            P("group", None, "ctx", None),
            P("group", None, ("tensor", "ctx"), None),
            P("group", None, ("tensor", "ctx"), None),
            P("group", ("tensor", "ctx")),
            P("group", None, ("tensor", "ctx")),
            P("group", None, "ctx"),
            P("group", None, ("tensor", "ctx"), None),
            P("group", None, ("tensor", "ctx"), None),
            P("group", ("tensor", "ctx")),
            P("group", None, ("tensor", "ctx")),
            P("group", None, "ctx"),
            P("group", None, ("tensor", "ctx"), None),
            P("group", None, ("tensor", "ctx"), None),
            P("group", ("tensor", "ctx")),
            P("group", None, ("tensor", "ctx")),
            P("group", None, "ctx"),
            P(None, ("tensor", "ctx"), None),
            P(None, ("tensor", "ctx"), None),
            P(("tensor", "ctx")),
            P(None, ("tensor", "ctx")),
            P(None, "ctx"),
            P(None, ("tensor", "ctx"), None),
            P(None, ("tensor", "ctx"), None),
            P(("tensor", "ctx")),
            P(None, ("tensor", "ctx")),
            P(None, "ctx"),
        ),
        check_vma=False,
    )
```

```python
from functools import partial
import math

import jax
import jax.numpy as jnp
from jax import lax
from jax.experimental import pallas as pl
from jax.experimental.pallas import tpu as pltpu
from jax.sharding import PartitionSpec as P

HEAD_DIM = 64


EPSILON = 1e-06
BETA_ONE = 0.9
BETA_TWO = 0.95
CORR_ONE = 1.0 - 0.9**4
CORR_TWO = 1.0 - 0.95**4
ADAM_EPS = 1e-08
DECAY = 0.1
MATRIX_RATE = 0.02
SCALE_RATE = 0.3
OUTER_RATE = 0.7
OUTER_MOMENTUM = 0.9
MASKED = -1e30
VMEM_BYTES = 40 * 1024 * 1024
LARGE_VMEM_BYTES = 56 * 1024 * 1024
SMALL_VMEM_BYTES = 16 * 1024 * 1024
F32 = jnp.float32
LONG_COST = pl.CostEstimate(flops=10**11, bytes_accessed=10**8, transcendentals=0)
SMALL_COST = pl.CostEstimate(flops=1000, bytes_accessed=1000, transcendentals=0)
LOW = jnp.bfloat16


def unit_rows(values, axis=-1):
    scale = lax.rsqrt(jnp.sum(values * values, axis=axis, keepdims=True) + EPSILON)
    return (values * scale, scale)


def unit_only(values):
    return values * lax.rsqrt(jnp.sum(values * values, axis=-1, keepdims=True) + EPSILON)


def unit_back(unit, scale, upstream, axis=-1):
    return scale * (upstream - unit * jnp.sum(upstream * unit, axis=axis, keepdims=True))


def dot(left, right, contract, out=F32):
    return lax.dot_general(
        left, right, (((contract[0],), (contract[1],)), ((), ())), preferred_element_type=F32
    ).astype(out)


def trade(values, axis, bit):
    count = lax.axis_size(axis)
    return lax.ppermute(values, axis, [(i, i ^ bit) for i in range(count)])


def ordered(first, own, other, axis):
    return jnp.where(
        first,
        jnp.concatenate([own, other], axis=axis),
        jnp.concatenate([other, own], axis=axis),
    )


def split_low(values):
    return lax.optimization_barrier(values.astype(LOW))


def add_low(left, right):
    return left.astype(F32) + right.astype(F32)


def ordered_after(body, count, deps):
    def wrapped(*refs):
        return body(*refs[:count], *refs[count + len(deps) :])

    return wrapped


UNREAD = pl.BlockSpec(memory_space=pl.ANY)
IN_VMEM = pl.BlockSpec(memory_space=pltpu.VMEM)


def tie_kernel(*refs):
    del refs


def tie(values, *deps):
    return pl.pallas_call(
        tie_kernel,
        in_specs=[UNREAD] * (1 + len(deps)),
        out_specs=UNREAD,
        out_shape=jax.ShapeDtypeStruct(values.shape, values.dtype),
        input_output_aliases={0: 0},
    )(values, *deps)


def add_kernel(count, *refs):
    total = refs[0][...].astype(F32)
    for ref in refs[1:count]:
        total = total + ref[...].astype(F32)
    refs[-1][...] = total.astype(refs[-1].dtype)


def added(terms, out, deps=()):
    if len(terms[0].shape) == 1:
        return lax.optimization_barrier(sum(term.astype(F32) for term in terms).astype(out))
    return pl.pallas_call(
        ordered_after(partial(add_kernel, len(terms)), len(terms), deps),
        in_specs=[IN_VMEM] * len(terms) + [UNREAD] * len(deps),
        out_shape=jax.ShapeDtypeStruct(terms[0].shape, out),
        compiler_params=pltpu.CompilerParams(vmem_limit_bytes=SMALL_VMEM_BYTES),
        cost_estimate=SMALL_COST,
    )(*terms, *deps)


def rows_kernel(features, weights, own_out, other_out):
    half = own_out.shape[0]
    other_out[...] = dot(features[:, half:], weights[...], (0, 0), LOW)
    own_out[...] = dot(features[:, :half], weights[...], (0, 0))


def to_rows(features, weights):
    half = features.shape[1] // 2
    width = weights.shape[1]
    return pl.pallas_call(
        rows_kernel,
        in_specs=[IN_VMEM] * 2,
        out_shape=[
            jax.ShapeDtypeStruct((half, width), F32),
            jax.ShapeDtypeStruct((half, width), LOW),
        ],
        compiler_params=pltpu.CompilerParams(vmem_limit_bytes=VMEM_BYTES),
        cost_estimate=SMALL_COST,
    )(features, weights)


def tensor_sum(own_part, other_part):
    pair = added([own_part, trade(other_part, "tensor", 1)], LOW)
    return (pair, trade(pair, "tensor", 2))


def group_sum(values):
    dtype = values.dtype
    pair = added([values, lax.ppermute(values, "group", [(0, 1), (3, 2)])], dtype)
    whole = added([pair, lax.ppermute(pair, "group", [(1, 2), (2, 1)])], dtype)
    back = lax.ppermute(whole, "group", [(1, 0), (2, 3)])
    return (pair, whole, back)


def chain_kernel(count, *refs):
    shifts, outs = refs[:count], refs[count : 2 * count]
    landed = refs[2 * count : 3 * count]
    crossed = refs[3 * count : 4 * count]
    pairs = refs[4 * count : 5 * count]
    sems = refs[5 * count]
    here = lax.axis_index("group")
    at_end = (here == 0) | (here == 3)
    middle = jnp.where(here < 2, 1, 2)
    end = jnp.where(here < 2, 0, 3)
    facing = 3 - middle
    barrier = pltpu.get_barrier_semaphore()

    def remote(source, target, k, step, to):
        return pltpu.make_async_remote_copy(
            src_ref=source,
            dst_ref=target,
            send_sem=sems.at[k, 2 * step],
            recv_sem=sems.at[k, 2 * step + 1],
            device_id={"group": to},
            device_id_type=pl.DeviceIdType.MESH,
        )

    inward = [remote(shifts[k], landed[k], k, 0, middle) for k in range(count)]
    across = [remote(pairs[k], crossed[k], k, 1, facing) for k in range(count)]
    outward = [remote(outs[k], landed[k], k, 2, end) for k in range(count)]

    @pl.when(at_end)
    def _():
        pl.semaphore_signal(
            barrier, inc=1, device_id={"group": middle}, device_id_type=pl.DeviceIdType.MESH
        )
        pl.semaphore_wait(barrier, 1)
        for copy in inward:
            copy.start()
        for k in range(count):
            outward[k].wait_recv()
            outs[k][...] = landed[k][...]
        for copy in inward:
            copy.wait_send()

    @pl.when(jnp.logical_not(at_end))
    def _():
        for to in (end, facing):
            pl.semaphore_signal(
                barrier, inc=1, device_id={"group": to}, device_id_type=pl.DeviceIdType.MESH
            )
        pl.semaphore_wait(barrier, 2)
        for k in range(count + 1):
            if k < count:
                inward[k].wait_recv()
                total = shifts[k][...].astype(F32) + landed[k][...].astype(F32)
                pairs[k][...] = total.astype(pairs[k].dtype)
                across[k].start()
            if k > 0:
                across[k - 1].wait_recv()
                total = pairs[k - 1][...].astype(F32) + crossed[k - 1][...].astype(F32)
                outs[k - 1][...] = total.astype(outs[k - 1].dtype)
                outward[k - 1].start()
        for k in range(count):
            across[k].wait_send()
            outward[k].wait_send()


def chain_sum(shifts, deps):
    count = len(shifts)
    shapes = [jax.ShapeDtypeStruct(shift.shape, shift.dtype) for shift in shifts]
    buffers = [pltpu.VMEM(shift.shape, shift.dtype) for shift in shifts]
    return pl.pallas_call(
        ordered_after(partial(chain_kernel, count), count, deps),
        in_specs=[IN_VMEM] * count + [UNREAD] * len(deps),
        out_specs=[IN_VMEM] * count,
        out_shape=shapes,
        scratch_shapes=buffers * 3 + [pltpu.SemaphoreType.DMA((count, 6))],
        compiler_params=pltpu.CompilerParams(
            collective_id=0, has_side_effects=True, vmem_limit_bytes=VMEM_BYTES
        ),
        cost_estimate=LONG_COST,
    )(*shifts, *deps)


def mask_bias(seg_q, place_q, seg_k, place_k):
    allowed = (seg_k == seg_q) & (place_k <= place_q)
    return jnp.where(allowed, 0.0, MASKED).astype(F32)


def project_kernel(head_count, weights, own, other, scale, projected, query_low, key_value):
    width = head_count * HEAD_DIM
    rows = jnp.concatenate([own[...], other[...]], axis=0)
    projected[...] = dot(weights[...], rows, (1, 1))
    for head in range(head_count):
        cols = pl.ds(head * HEAD_DIM, HEAD_DIM)
        key_cols = pl.ds(width + head * HEAD_DIM, HEAD_DIM)
        head_scale = scale[cols, :]
        query_unit, _ = unit_rows(projected[cols, :], axis=0)
        key_unit, _ = unit_rows(projected[key_cols, :], axis=0)
        query_low[cols, :] = (query_unit * head_scale * math.sqrt(HEAD_DIM)).astype(LOW)
        key_value[cols, :] = (key_unit * head_scale).astype(LOW)
    key_value[width : 2 * width, :] = projected[2 * width : 3 * width, :].astype(LOW)


def project(head_count, weights, own, other, scale, deps=()):
    total, model_width = weights.shape
    width = head_count * HEAD_DIM
    rows = own.shape[0] + other.shape[0]
    return pl.pallas_call(
        ordered_after(partial(project_kernel, head_count), 4, deps),
        in_specs=[IN_VMEM] * 4 + [UNREAD] * len(deps),
        out_shape=[
            jax.ShapeDtypeStruct((total, rows), F32),
            jax.ShapeDtypeStruct((width, rows), LOW),
            jax.ShapeDtypeStruct((2 * width, rows), LOW),
        ],
        compiler_params=pltpu.CompilerParams(vmem_limit_bytes=VMEM_BYTES),
        cost_estimate=SMALL_COST,
    )(weights, own, other, scale, *deps)


def sides_kernel(head_count, has_partner, own, arrived, query_grad, projected, scale, triple, terms):
    width = head_count * HEAD_DIM
    root_head = math.sqrt(HEAD_DIM)

    def side(cols):
        gradient = own[cols, :]
        if has_partner:
            gradient = gradient + arrived[cols, :].astype(F32)
        return gradient

    for head in range(head_count):
        cols = pl.ds(head * HEAD_DIM, HEAD_DIM)
        key_cols = pl.ds(width + head * HEAD_DIM, HEAD_DIM)
        head_scale = scale[cols, :]
        query_unit, query_norm = unit_rows(projected[cols, :], axis=0)
        key_unit, key_norm = unit_rows(projected[key_cols, :], axis=0)
        query_scaled = query_grad[cols, :] * root_head
        key_scaled = side(cols)
        terms[cols, :] = jnp.sum(
            query_scaled * query_unit + key_scaled * key_unit, axis=1, keepdims=True
        )
        triple[cols, :] = unit_back(
            query_unit, query_norm, query_scaled * head_scale, axis=0
        ).astype(LOW)
        triple[key_cols, :] = unit_back(
            key_unit, key_norm, key_scaled * head_scale, axis=0
        ).astype(LOW)
    triple[2 * width : 3 * width, :] = side(pl.ds(width, width)).astype(LOW)


def sides_back(head_count, own, arrived, query_grad, projected, scale, deps=()):
    total, rows = projected.shape
    width = head_count * HEAD_DIM
    has_partner = arrived is not None
    if not has_partner:
        arrived = jnp.zeros((16, rows), LOW)
    return pl.pallas_call(
        ordered_after(partial(sides_kernel, head_count, has_partner), 5, deps),
        in_specs=[IN_VMEM] * 5 + [UNREAD] * len(deps),
        out_shape=[
            jax.ShapeDtypeStruct((total, rows), LOW),
            jax.ShapeDtypeStruct((width, 1), F32),
        ],
        compiler_params=pltpu.CompilerParams(vmem_limit_bytes=VMEM_BYTES),
        cost_estimate=SMALL_COST,
    )(own, arrived, query_grad, projected, scale, *deps)


def triple_grad_kernel(count, parts, own_part, me, *refs):
    lefts, rights = refs[:count], refs[count : 3 * count]
    own_out, other_out = refs[3 * count :]
    right = jnp.concatenate([ref[...] for ref in rights], axis=0)
    rows = lefts[0].shape[0] // parts
    for side in range(2):
        place = me[0] if side == 0 else 1 - me[0]
        left = jnp.concatenate(
            [
                jnp.concatenate(
                    [
                        ref[pl.ds(pl.multiple_of(n * rows + place * own_part, 16), own_part), :]
                        for n in range(parts)
                    ],
                    axis=0,
                )
                for ref in lefts
            ],
            axis=1,
        )
        total = dot(left, right, (1, 0))
        if side == 0:
            own_out[...] = total
        else:
            other_out[...] = total.astype(LOW)


def triple_grad(me, parts, lefts, rights, deps=()):
    count = len(lefts)
    total, rows = lefts[0].shape
    own_part = total // parts // 2
    width = rights[0][0].shape[1]
    return pl.pallas_call(
        ordered_after(partial(triple_grad_kernel, count, parts, own_part), 1 + 3 * count, deps),
        in_specs=[pl.BlockSpec(memory_space=pltpu.SMEM)]
        + [IN_VMEM] * (3 * count)
        + [UNREAD] * len(deps),
        out_shape=[
            jax.ShapeDtypeStruct((parts * own_part, width), F32),
            jax.ShapeDtypeStruct((parts * own_part, width), LOW),
        ],
        compiler_params=pltpu.CompilerParams(vmem_limit_bytes=VMEM_BYTES),
        cost_estimate=SMALL_COST,
    )(me, *lefts, *[side for right in rights for side in right], *deps)


def attend_kernel(
    head_count, seg_q, place_q, seg_k, place_k, query, key_value, summed, total, heads, bias
):
    blocks, _, rows = key_value.shape
    width = head_count * HEAD_DIM
    for j in range(blocks):
        part = pl.ds(j * rows, rows)
        bias[part, :] = mask_bias(seg_q[...], place_q[...], seg_k[part, :], place_k[part, :])
    for head in range(head_count):
        cols = pl.ds(head * HEAD_DIM, HEAD_DIM)
        value_cols = pl.ds(width + head * HEAD_DIM, HEAD_DIM)
        block_query = query[cols, :]
        row_total = jnp.zeros((1, query.shape[1]), F32)
        acc = jnp.zeros((HEAD_DIM, query.shape[1]), F32)
        for j in range(blocks):
            scores = dot(key_value[j, cols, :], block_query, (0, 0))
            raised = jnp.exp(scores + bias[pl.ds(j * rows, rows), :])
            row_total = row_total + jnp.sum(raised, axis=0, keepdims=True)
            acc = acc + dot(key_value[j, value_cols, :], raised.astype(LOW), (1, 0))
        summed[cols, :] = acc
        total[pl.ds(head, 1), :] = row_total
        heads[cols, :] = (acc / row_total).astype(LOW)


def attend(head_count, places, query, key_value, deps=()):
    blocks, _, rows = key_value.shape
    width, count = query.shape
    return pl.pallas_call(
        ordered_after(partial(attend_kernel, head_count), 6, deps),
        in_specs=[IN_VMEM] * 6 + [UNREAD] * len(deps),
        out_shape=(
            jax.ShapeDtypeStruct((width, count), F32),
            jax.ShapeDtypeStruct((head_count, count), F32),
            jax.ShapeDtypeStruct((width, count), LOW),
        ),
        scratch_shapes=[pltpu.VMEM((blocks * rows, count), F32)],
        compiler_params=pltpu.CompilerParams(vmem_limit_bytes=VMEM_BYTES),
        cost_estimate=SMALL_COST,
    )(*places, query, key_value, *deps)


def attend_back_kernel(
    head_count,
    seg_q,
    place_q,
    seg_k,
    place_k,
    query,
    key_value,
    rows_own,
    rows_other,
    weights,
    summed,
    total,
    query_grad,
    own_grad,
    other_grad,
    bias,
    heads_back,
):
    blocks, _, rows = key_value.shape
    rows_back = jnp.concatenate([rows_own[...], rows_other[...]], axis=0)
    heads_back[...] = dot(weights[...], rows_back, (1, 1), LOW)
    width = head_count * HEAD_DIM
    for j in range(blocks):
        part = pl.ds(j * rows, rows)
        bias[part, :] = mask_bias(seg_q[...], place_q[...], seg_k[part, :], place_k[part, :])
    for head in range(head_count):
        cols = pl.ds(head * HEAD_DIM, HEAD_DIM)
        value_cols = pl.ds(width + head * HEAD_DIM, HEAD_DIM)
        block_query = query[cols, :]
        output_back = heads_back[cols, :].astype(F32)
        row_total = total[pl.ds(head, 1), :]
        summed_back = (output_back / row_total).astype(LOW)
        total_back = -jnp.sum(output_back * summed[cols, :], axis=0, keepdims=True) / (
            row_total * row_total
        )
        acc = jnp.zeros((HEAD_DIM, query.shape[1]), F32)
        for j in range(blocks):
            key_part = key_value[j, cols, :]
            scores = dot(key_part, block_query, (0, 0))
            raised = jnp.exp(scores + bias[pl.ds(j * rows, rows), :])
            raised_back = dot(key_value[j, value_cols, :], summed_back, (0, 0))
            score_back = (raised * (raised_back + total_back)).astype(LOW)
            acc = acc + dot(key_part, score_back, (1, 0))
            key_grad = dot(block_query, score_back, (1, 1))
            value_grad = dot(summed_back, raised.astype(LOW), (1, 1))
            if j == 0:
                own_grad[cols, :] = key_grad
                own_grad[value_cols, :] = value_grad
            else:
                other_grad[j - 1, cols, :] = key_grad.astype(other_grad.dtype)
                other_grad[j - 1, value_cols, :] = value_grad.astype(other_grad.dtype)
        query_grad[cols, :] = acc


def attend_back(head_count, places, query, key_value, rows_back, weights, summed, total, deps=()):
    blocks, both, rows = key_value.shape
    width, count = query.shape
    return pl.pallas_call(
        ordered_after(partial(attend_back_kernel, head_count), 11, deps),
        in_specs=[IN_VMEM] * 11 + [UNREAD] * len(deps),
        out_shape=(
            jax.ShapeDtypeStruct((width, count), F32),
            jax.ShapeDtypeStruct((both, rows), F32),
            jax.ShapeDtypeStruct((blocks - 1, both, rows), LOW if blocks == 2 else F32),
        ),
        scratch_shapes=[pltpu.VMEM((blocks * rows, count), F32), pltpu.VMEM((width, count), LOW)],
        compiler_params=pltpu.CompilerParams(vmem_limit_bytes=VMEM_BYTES),
        cost_estimate=SMALL_COST,
    )(*places, query, key_value, *rows_back, weights, summed, total, *deps)


def sigmoid(values):
    return 1.0 / (1.0 + jnp.exp(-values))


def feed_kernel(
    root_width,
    own,
    other,
    up_weights,
    gate_weights,
    down_weights,
    scale_up,
    scale_gate,
    up_out,
    gate_out,
    hidden_out,
    own_out,
    other_out,
    total,
):
    half = own.shape[0]
    rows = jnp.concatenate([own[...], other[...]], axis=0)
    up = dot(rows, up_weights[...], (1, 1))
    gate = dot(rows, gate_weights[...], (1, 1))
    up_out[...] = up
    gate_out[...] = gate
    gate_scaled = gate * scale_gate[...] * root_width
    hidden = (gate_scaled * sigmoid(gate_scaled) * (up * scale_up[...])).astype(LOW)
    hidden_out[...] = hidden
    part = dot(hidden, down_weights[...], (1, 0))
    step = pl.program_id(0)

    @pl.when(step == 0)
    def _():
        total[...] = part

    @pl.when(step > 0)
    def _():
        total[...] += part

    @pl.when(step == pl.num_programs(0) - 1)
    def _():
        own_out[...] = total[:half, :]
        other_out[...] = total[half:, :].astype(LOW)


def feed_forward(own, other, feed_full, scale_up, scale_gate, deps=()):
    half, width = own.shape
    units = feed_full[0].shape[0]
    tile = units
    held = pl.BlockSpec((half, width), lambda i: (0, 0))
    weight = pl.BlockSpec((tile, width), lambda i: (i, 0))
    scale = pl.BlockSpec((1, tile), lambda i: (0, i))
    piece = pl.BlockSpec((2 * half, tile), lambda i: (0, i))
    kept = jax.ShapeDtypeStruct((2 * half, units), F32)
    return pl.pallas_call(
        ordered_after(partial(feed_kernel, math.sqrt(width)), 7, deps),
        grid=(units // tile,),
        in_specs=[held, held, weight, weight, weight, scale, scale] + [UNREAD] * len(deps),
        out_specs=[piece, piece, piece, held, held],
        out_shape=[
            kept,
            kept,
            jax.ShapeDtypeStruct((2 * half, units), LOW),
            jax.ShapeDtypeStruct((half, width), F32),
            jax.ShapeDtypeStruct((half, width), LOW),
        ],
        scratch_shapes=[pltpu.VMEM((2 * half, width), F32)],
        compiler_params=pltpu.CompilerParams(vmem_limit_bytes=LARGE_VMEM_BYTES),
        cost_estimate=SMALL_COST,
    )(own, other, *feed_full, scale_up, scale_gate, *deps)


def feed_back_kernel(
    root_width,
    own,
    other,
    up_ref,
    gate_ref,
    up_weights,
    gate_weights,
    down_weights,
    scale_up,
    scale_gate,
    up_out,
    gate_out,
    terms_out,
    own_out,
    other_out,
    total,
):
    half = own.shape[0]
    rows = jnp.concatenate([own[...], other[...]], axis=0)
    hidden_back = dot(rows, down_weights[...], (1, 1))
    up = up_ref[...]
    gate = gate_ref[...]
    gate_scaled = gate * scale_gate[...] * root_width
    sigmoid_gate = sigmoid(gate_scaled)
    up_back = hidden_back * (gate_scaled * sigmoid_gate)
    gate_back = (
        hidden_back
        * (up * scale_up[...])
        * (sigmoid_gate * (1.0 + gate_scaled * (1.0 - sigmoid_gate)))
    )
    terms_out[...] = jnp.concatenate(
        [
            jnp.sum(up_back * up, axis=0, keepdims=True),
            jnp.sum(gate_back * gate, axis=0, keepdims=True) * root_width,
        ],
        axis=0,
    )
    up_low = (up_back * scale_up[...]).astype(LOW)
    gate_low = (gate_back * scale_gate[...] * root_width).astype(LOW)
    up_out[...] = up_low
    gate_out[...] = gate_low
    part = dot(up_low, up_weights[...], (1, 0)) + dot(gate_low, gate_weights[...], (1, 0))
    step = pl.program_id(0)

    @pl.when(step == 0)
    def _():
        total[...] = part

    @pl.when(step > 0)
    def _():
        total[...] += part

    @pl.when(step == pl.num_programs(0) - 1)
    def _():
        own_out[...] = total[:half, :]
        other_out[...] = total[half:, :].astype(LOW)


def feed_backward(own, other, up, gate, feed_full, scale_up, scale_gate, deps=()):
    half, width = own.shape
    units = feed_full[0].shape[0]
    tile = units
    held = pl.BlockSpec((half, width), lambda i: (0, 0))
    weight = pl.BlockSpec((tile, width), lambda i: (i, 0))
    scale = pl.BlockSpec((1, tile), lambda i: (0, i))
    piece = pl.BlockSpec((2 * half, tile), lambda i: (0, i))
    return pl.pallas_call(
        ordered_after(partial(feed_back_kernel, math.sqrt(width)), 9, deps),
        grid=(units // tile,),
        in_specs=[held, held, piece, piece, weight, weight, weight, scale, scale]
        + [UNREAD] * len(deps),
        out_specs=[piece, piece, pl.BlockSpec((2, tile), lambda i: (0, i)), held, held],
        out_shape=[
            jax.ShapeDtypeStruct((2 * half, units), LOW),
            jax.ShapeDtypeStruct((2 * half, units), LOW),
            jax.ShapeDtypeStruct((2, units), F32),
            jax.ShapeDtypeStruct((half, width), F32),
            jax.ShapeDtypeStruct((half, width), LOW),
        ],
        scratch_shapes=[pltpu.VMEM((2 * half, width), F32)],
        compiler_params=pltpu.CompilerParams(vmem_limit_bytes=LARGE_VMEM_BYTES),
        cost_estimate=SMALL_COST,
    )(own, other, up, gate, *feed_full, scale_up, scale_gate, *deps)


def weight_grad_kernel(count, *refs):
    lefts, rights = refs[:count], refs[count : 3 * count]
    own_out, other_out = refs[3 * count :]
    part = own_out.shape[0]
    right = jnp.concatenate([ref[...] for ref in rights], axis=0)
    for side in range(2):
        left = jnp.concatenate([ref[:, side * part : (side + 1) * part] for ref in lefts], axis=0)
        total = dot(left, right, (0, 0))
        if side == 0:
            own_out[...] = total
        else:
            other_out[...] = total.astype(LOW)


def weight_grad(lefts, rights, deps=()):
    count = len(lefts)
    rows, units = lefts[0].shape
    half, width = rights[0][0].shape
    part = units // 2
    return pl.pallas_call(
        ordered_after(partial(weight_grad_kernel, count), 3 * count, deps),
        in_specs=[IN_VMEM] * (3 * count) + [UNREAD] * len(deps),
        out_shape=[
            jax.ShapeDtypeStruct((part, width), F32),
            jax.ShapeDtypeStruct((part, width), LOW),
        ],
        compiler_params=pltpu.CompilerParams(vmem_limit_bytes=LARGE_VMEM_BYTES),
        cost_estimate=SMALL_COST,
    )(*lefts, *[side for right in rights for side in right], *deps)


def first_part(pair, partner, token, rate):
    attention_unit, attention_norm = unit_rows(add_low(pair[...], partner[...]))
    token_float = token[...].astype(F32)
    after, after_norm = unit_rows(token_float + rate * (attention_unit - token_float))
    return (attention_unit, attention_norm, token_float, after, after_norm)


def normed_kernel(pair, partner, token, rates, normed_out):
    normed_out[...] = first_part(pair, partner, token, rates[0:1, :])[3].astype(LOW)


def output_kernel(
    pair, partner, token, feed_pair, feed_partner, cotangent, rates, output_out, second_out, back_out, term_out
):
    after = first_part(pair, partner, token, rates[0:1, :])[3]
    rate = rates[1:2, :]
    feed_unit, feed_norm = unit_rows(add_low(feed_pair[...], feed_partner[...]))
    output, output_norm = unit_rows(after + rate * (feed_unit - after))
    output_out[...] = output
    second_back = unit_back(output, output_norm, cotangent[...].astype(F32))
    second_out[...] = second_back
    back_out[...] = unit_back(feed_unit, feed_norm, second_back * rate).astype(LOW)
    term = jnp.sum(second_back * (feed_unit - after), axis=0, keepdims=True)

    @pl.when(pl.program_id(0) == 0)
    def _():
        term_out[...] = term

    @pl.when(pl.program_id(0) > 0)
    def _():
        term_out[...] += term


def first_back_kernel(
    pair, partner, token, second, grad_pair, grad_partner, rates, skip_out, back_out, term_out
):
    rate = rates[0:1, :]
    attention_unit, attention_norm, token_float, after, after_norm = first_part(
        pair, partner, token, rate
    )
    after_grad = second[...] * (1.0 - rates[1:2, :]) + add_low(grad_pair[...], grad_partner[...])
    first_back = unit_back(after, after_norm, after_grad)
    skip_out[...] = first_back * (1.0 - rate)
    back_out[...] = unit_back(attention_unit, attention_norm, first_back * rate).astype(LOW)
    term = jnp.sum(first_back * (attention_unit - token_float), axis=0, keepdims=True)

    @pl.when(pl.program_id(0) == 0)
    def _():
        term_out[...] = term

    @pl.when(pl.program_id(0) > 0)
    def _():
        term_out[...] += term


def rowwise(body, arrays, rates, outs, has_term, deps=()):
    half, width = arrays[0].shape
    tile = 128 if half % 128 == 0 else half
    flat = pl.BlockSpec((tile, width), lambda i: (i, 0))
    term = [pl.BlockSpec((1, width), lambda i: (0, 0))] if has_term else []
    term_shape = [jax.ShapeDtypeStruct((1, width), F32)] if has_term else []
    return pl.pallas_call(
        ordered_after(body, len(arrays) + 1, deps),
        grid=(half // tile,),
        in_specs=[flat] * len(arrays)
        + [pl.BlockSpec((2, width), lambda i: (0, 0))]
        + [UNREAD] * len(deps),
        out_specs=[flat] * len(outs) + term,
        out_shape=[jax.ShapeDtypeStruct((half, width), kind) for kind in outs] + term_shape,
        compiler_params=pltpu.CompilerParams(vmem_limit_bytes=VMEM_BYTES),
        cost_estimate=SMALL_COST,
    )(*arrays, rates, *deps)


def adam_step(master, gradient, first_state, second_state, step_rate, is_matrix):
    moment = BETA_ONE * first_state + (1.0 - BETA_ONE) * gradient
    variance = BETA_TWO * second_state + (1.0 - BETA_TWO) * gradient * gradient
    update = moment / CORR_ONE / (jnp.sqrt(variance / CORR_TWO) + ADAM_EPS)
    updated = master - step_rate * (update + DECAY * master)
    if is_matrix:
        updated = unit_only(updated)
    return (moment, variance, updated)


def outer_step(master, shift, outer_state, is_matrix):
    momentum = OUTER_MOMENTUM * outer_state + shift
    result = master - OUTER_RATE * (shift + OUTER_MOMENTUM * momentum)
    if is_matrix:
        result = unit_only(result)
    return (momentum, result)


def row_tile(rows):
    for size in (160, 128):
        if rows % size == 0:
            return size
    return rows


def adam_kernel(has_partner, chunks, offset, own, partner, master, first, second, *rest):
    del offset
    gradient_out, moment_out, variance_out = rest[-3 - chunks : -chunks]
    gradient = own[...]
    if has_partner:
        gradient = gradient + partner[...].astype(F32)
    moment, variance, updated = adam_step(
        master[0], gradient, first[0, 0], second[0, 0], MATRIX_RATE, True
    )
    gradient_out[0, 0] = gradient
    moment_out[0, 0] = moment
    variance_out[0, 0] = variance
    shift = (master[0] - updated).astype(LOW)
    each = pl.num_programs(0) // chunks
    for n in range(chunks):

        @pl.when(pl.program_id(0) // each == n)
        def _(n=n):
            rest[n - chunks][...] = shift


def adam_slab(which, chunks, own_block, gradient, partner, master, first, second, earlier, deps=()):
    slabs, rows, width = master.shape
    tile = row_tile(rows)
    steps = rows // tile
    each = steps // chunks
    has_partner = partner is not None
    if not has_partner:
        partner = jnp.zeros((tile, width), LOW)
    flat = pl.BlockSpec((tile, width), lambda i, at: (i, 0))
    held = pl.BlockSpec((tile, width), lambda i, at: (at[0] * steps + i, 0))
    partner_spec = flat if not has_partner or partner.shape[0] == rows else held
    once = pl.BlockSpec((tile, width), lambda i, at: (0, 0))
    slab = pl.BlockSpec((1, tile, width), lambda i, at: (which, i, 0))
    grouped = pl.BlockSpec((1, 1, tile, width), lambda i, at: (0, which, i, 0))
    whole = jax.ShapeDtypeStruct((1, slabs, rows, width), F32)
    earlier = () if earlier is None else earlier
    pieces = [
        pl.BlockSpec((tile, width), lambda i, at, n=n: (jnp.clip(i - n * each, 0, each - 1), 0))
        for n in range(chunks)
    ]
    return pl.pallas_call(
        partial(adam_kernel, has_partner, chunks),
        grid_spec=pltpu.PrefetchScalarGridSpec(
            num_scalar_prefetch=1,
            grid=(steps,),
            in_specs=[held, partner_spec if has_partner else once, slab, grouped, grouped]
            + [UNREAD] * (len(earlier) + len(deps)),
            out_specs=[grouped, grouped, grouped] + pieces,
        ),
        out_shape=[whole, whole, whole]
        + [jax.ShapeDtypeStruct((rows // chunks, width), LOW)] * chunks,
        input_output_aliases={6 + n: n for n in range(len(earlier))},
        compiler_params=pltpu.CompilerParams(vmem_limit_bytes=VMEM_BYTES),
        cost_estimate=SMALL_COST,
    )(own_block, gradient, partner, master, first, second, *earlier, *deps)


TAG = jax.ShapeDtypeStruct((8, 128), F32)


def outer_kernel(group_count, at_end, whole, back, master, outer, *rest):
    momentum_out, result_out, tag_out = rest[-3:]
    shift = jnp.where(at_end[0] == 1, back[...].astype(F32), whole[...].astype(F32)) / group_count
    momentum, result = outer_step(master[0], shift, outer[0], True)
    momentum_out[0] = momentum
    result_out[0] = result
    tag_out[...] = jnp.zeros_like(tag_out)


def outer_slab(which, chunk, group_count, at_end, whole, back, master, outer, earlier, deps):
    slabs, rows, width = master.shape
    part = whole.shape[0]
    tile = row_tile(part)
    steps = part // tile
    flat = pl.BlockSpec((tile, width), lambda i, at: (i, 0))
    slab = pl.BlockSpec((1, tile, width), lambda i, at: (which, chunk * steps + i, 0))
    result = jax.ShapeDtypeStruct((slabs, rows, width), F32)
    earlier = () if earlier is None else earlier
    return pl.pallas_call(
        partial(outer_kernel, group_count),
        grid_spec=pltpu.PrefetchScalarGridSpec(
            num_scalar_prefetch=1,
            grid=(steps,),
            in_specs=[flat, flat, slab, slab] + [UNREAD] * (len(earlier) + len(deps)),
            out_specs=[slab, slab, pl.BlockSpec(TAG.shape, lambda i, at: (0, 0))],
        ),
        out_shape=[result, result, TAG],
        input_output_aliases={5 + n: n for n in range(len(earlier))},
        compiler_params=pltpu.CompilerParams(vmem_limit_bytes=VMEM_BYTES),
        cost_estimate=SMALL_COST,
    )(at_end, whole, back, master, outer, *earlier, *deps)


class MatrixSteps:
    def __init__(self, chunks, late_chunks, at_end, master, first, second, outer):
        self.chunks = chunks
        self.late_chunks = late_chunks
        self.at_end = at_end.reshape(1)
        self.arrays = (master, first, second)
        self.outer_state = outer
        self.inner_outs = None
        self.outer_outs = None
        self.sums = {}
        self.shifts = {}

    def inner(self, which, gradient, deps, chain=True):
        own, partner, block = gradient
        chunks = self.chunks if chain else self.late_chunks
        outs = adam_slab(which, chunks, block, own, partner, *self.arrays, self.inner_outs, deps)
        self.inner_outs = outs[:3]
        if chain:
            self.sums[which] = [group_sum(shift) for shift in outs[3:]]
        else:
            self.shifts[which] = list(outs[3:])
        return outs[3]

    def pairs(self, which):
        return [step[0] for step in self.sums[which]]

    def wholes(self, which):
        return [step[1] for step in self.sums[which]]

    def outer(self, which, tags, also=()):
        for chunk, (_, whole, back) in enumerate(self.sums[which]):
            if chunk < len(also):
                tags = tags + also[chunk]
            *self.outer_outs, tag = outer_slab(
                which,
                chunk,
                lax.axis_size("group"),
                self.at_end,
                whole,
                back,
                self.arrays[0],
                self.outer_state,
                self.outer_outs,
                tags,
            )
            tags = [tag]
        return tags

    def outs(self):
        return (*self.inner_outs, *self.outer_outs)


def place_kernel(core, own, other, *rest):
    out = rest[-1]

    @pl.when(pl.program_id(0) == 0)
    def _():
        out[0, 0] = own[...]

    @pl.when(pl.program_id(0) == 1)
    def _():
        out[0, 0] = other[...]


def place_rows(which, count, core, own, other, earlier, deps=()):
    half, width = own.shape
    held = pl.BlockSpec((half, width), lambda i, at: (0, 0))
    earlier = () if earlier is None else (earlier,)
    return pl.pallas_call(
        place_kernel,
        grid_spec=pltpu.PrefetchScalarGridSpec(
            num_scalar_prefetch=1,
            grid=(2,),
            in_specs=[held, held] + [UNREAD] * (len(earlier) + len(deps)),
            out_specs=pl.BlockSpec(
                (1, 1, half, width), lambda i, at: (0, which, lax.rem(at[0] + i, 2), 0)
            ),
        ),
        out_shape=jax.ShapeDtypeStruct((1, count, 2 * half, width), F32),
        input_output_aliases={3: 0} if earlier else {},
        compiler_params=pltpu.CompilerParams(vmem_limit_bytes=VMEM_BYTES),
        cost_estimate=SMALL_COST,
    )(core, own, other, *earlier, *deps)


def on_device(
    tokens,
    cotangent,
    segments,
    shard_order,
    attention_weights,
    feedforward_weights,
    head_scales,
    hidden_scales,
    residual_rates,
    attention_first,
    feedforward_first,
    heads_first,
    hidden_first,
    rates_first,
    attention_second,
    feedforward_second,
    heads_second,
    hidden_second,
    rates_second,
    attention_outer,
    feedforward_outer,
    heads_outer,
    hidden_outer,
    rates_outer,
):
    micro_count, rows, model_width = tokens.shape[1:]
    half = rows // 2
    ctx_count = lax.axis_size("ctx")
    pair = ctx_count == 2
    group_count = lax.axis_size("group")
    own_rows = attention_weights.shape[1]
    own_units = feedforward_weights.shape[1]
    head_width = own_rows * ctx_count
    head_count = head_width // HEAD_DIM
    units = own_units * ctx_count
    root_head = math.sqrt(HEAD_DIM)
    root_width = math.sqrt(model_width)
    me = lax.axis_index("ctx")
    ctx_first = me == 0
    core_index = lax.rem(lax.axis_index("tensor"), 2).reshape(1)
    core_first = core_index[0] == 0
    even_group = lax.rem(lax.axis_index("group"), 2) == 0
    micros = range(micro_count)
    at_end = lax.axis_index("group")
    at_end = ((at_end == 0) | (at_end == group_count - 1)).astype(jnp.int32)

    attention_low = attention_weights.astype(LOW)
    feed_low = feedforward_weights.astype(LOW)
    small_low = jnp.concatenate(
        [head_scales, hidden_scales[0], hidden_scales[1], residual_rates[0], residual_rates[1]]
    ).astype(LOW)
    own_cols = residual_rates.shape[1]
    if pair:
        part = own_rows // 2
        piece = jnp.where(even_group, attention_low[:3, :part], attention_low[:3, part:])
        triple_across = trade(piece, "ctx", 1)
        triple_other = ordered(even_group, triple_across, trade(triple_across, "group", 1), 1)
        triple_weights = ordered(ctx_first, attention_low[:3], triple_other, 1)
        small_other = trade(small_low, "ctx", 1)
        cuts = [own_rows, own_units, own_units, own_cols, own_cols]
        small_pieces = []
        start = 0
        for which, size in enumerate(cuts):
            mine = small_low[start : start + size].astype(F32)
            theirs = small_other[start : start + size].astype(F32)
            start += size
            if which in (1, 2):
                small_pieces.append(jnp.concatenate([mine, theirs]))
            else:
                small_pieces.append(ordered(ctx_first, mine, theirs, 0))
        scale_heads, scale_up, scale_gate, rate_attention, rate_feed = small_pieces
    else:
        triple_weights = lax.all_gather(attention_low[:3], "ctx", axis=1, tiled=True)
        scale_heads = lax.all_gather(head_scales.astype(LOW), "ctx", axis=0, tiled=True).astype(F32)
        scale_up, scale_gate = lax.all_gather(
            hidden_scales.astype(LOW), "ctx", axis=1, tiled=True
        ).astype(F32)
        rate_attention, rate_feed = lax.all_gather(
            residual_rates.astype(LOW), "ctx", axis=1, tiled=True
        ).astype(F32)
    triple_weights = triple_weights.reshape(3 * head_width, model_width)
    scale_column = scale_heads.reshape(head_width, 1)

    token_halves = tokens[0].reshape(micro_count, 2, half, model_width)
    token_own = jnp.where(core_first, token_halves[:, 0], token_halves[:, 1])
    token_other = jnp.where(core_first, token_halves[:, 1], token_halves[:, 0])
    cotangent_halves = cotangent[0].reshape(micro_count, 2, half, model_width)
    cotangent_own = jnp.where(core_first, cotangent_halves[:, 0], cotangent_halves[:, 1])

    if pair:
        block_ids = jnp.stack([me, 1 - me])
    else:
        block_ids = lax.rem(me + jnp.arange(ctx_count, dtype=jnp.int32), ctx_count)
    table = jnp.arange(ctx_count, dtype=jnp.int32)
    order_of = jnp.sum(
        jnp.where(block_ids[:, None] == table[None, :], shard_order[None, :], 0), axis=1
    )
    local = jnp.arange(rows, dtype=jnp.int32)
    local = jnp.where(core_first, local, lax.rem(local + half, rows))
    place_blocks = order_of[:, None] * rows + local[None, :]
    segment_blocks = segments[0].reshape(micro_count, ctx_count, rows)
    segment_blocks = jnp.sum(
        jnp.where(
            (order_of[:, None] == table[None, :])[None, :, :, None], segment_blocks[:, None], 0
        ),
        axis=2,
    )
    segment_blocks = jnp.where(
        core_first,
        segment_blocks,
        jnp.concatenate([segment_blocks[:, :, half:], segment_blocks[:, :, :half]], axis=2),
    )
    places = [
        (
            segment_blocks[b, 0][None, :],
            place_blocks[0][None, :],
            segment_blocks[b].reshape(ctx_count * rows, 1),
            place_blocks.reshape(ctx_count * rows, 1),
        )
        for b in micros
    ]

    projections, query_low, local_sides = [], [], []
    for b in micros:
        projected, query, key_value = project(
            head_count,
            triple_weights,
            token_own[b],
            token_other[b],
            scale_column,
            projections[-1:],
        )
        projections.append(projected)
        query_low.append(query)
        local_sides.append(key_value)

    def all_sides(b, deps):
        if pair:
            sent = tie(local_sides[b], *deps) if deps else local_sides[b]
            return jnp.stack([local_sides[b], trade(sent, "ctx", 1)])
        return jnp.take(lax.all_gather(local_sides[b], "ctx", axis=0), block_ids, axis=0)

    def across_and_along(source, deps):
        part = source.shape[0] // 2
        piece = tie(jnp.where(even_group, source[:part], source[part:]), *deps)
        across = trade(piece, "ctx", 1)
        return (across, ordered(even_group, across, trade(across, "group", 1), 0))

    arrivals = []
    feed_full = []

    def gather_feed(which, deps):
        across, other = across_and_along(feed_low[which], deps)
        arrivals.append(across)
        feed_full.append(jnp.concatenate([feed_low[which], other], axis=0))

    if pair:
        gather_feed(0, [triple_across])
        _, output_other = across_and_along(attention_low[3], [triple_across])
        output_weights = ordered(ctx_first, attention_low[3], output_other, 0)
    else:
        output_weights = lax.all_gather(attention_low[3], "ctx", axis=0, tiled=True)

    rates_both = jnp.stack([rate_attention, rate_feed])
    scale_up = scale_up.reshape(1, units)
    scale_gate = scale_gate.reshape(1, units)
    summeds, totals, heads_lows, attention_sums, normed_rows = [], [], [], [], []

    def normed_part(b, deps):
        (normed_low,) = rowwise(
            normed_kernel, attention_sums[b], rates_both, [LOW], False, deps
        )
        normed_rows.append((normed_low, trade(normed_low, "tensor", 1)))

    last = micro_count - 1
    key_values = []
    for b in micros:
        if b < last:
            key_values.append(all_sides(b, []))
        if b == last:
            if pair:
                for which in (1, 2):
                    gather_feed(which, totals[:1])
            key_values.append(all_sides(b, totals[-1:]))
        deps = totals[-1:]
        if b == last:
            for n in range(last):
                normed_part(n, deps + arrivals[1:2] * (n == last - 1))
                deps = [normed_rows[-1][0]]
            deps = deps + arrivals[2:]
        summed, total, heads_low = attend(
            head_count, places[b], query_low[b], key_values[b], deps
        )
        summeds.append(summed)
        totals.append(total)
        heads_lows.append(heads_low)
        attention_sums.append((*tensor_sum(*to_rows(heads_low, output_weights)), token_own[b]))

    if not pair:
        feed_full = list(lax.all_gather(feed_low, "ctx", axis=1, tiled=True))
    up_weights, gate_weights, down_weights = feed_full
    ups, gates, hidden_rows, feed_parts = [], [], [], []
    for b in micros:
        if b == last:
            normed_part(b, [feed_parts[-1][1]] if b > 0 else totals[-1:])
        up, gate, hidden, own_part, other_part = feed_forward(
            *normed_rows[b],
            feed_full,
            scale_up,
            scale_gate,
            [totals[-1] if b == 0 else feed_parts[-1][1]],
        )
        ups.append(up)
        gates.append(gate)
        hidden_rows.append(hidden)
        feed_parts.append((own_part, other_part))

    outputs, second_backs, feed_back_rows, feed_rate_terms = [], [], [], []
    up_back_rows, gate_back_rows, hidden_terms, grad_sums = [], [], [], []
    skips, attention_back_rows, attention_rate_terms = [], [], []
    attention_grads = []
    down_grad = None

    def output_part(b, deps):
        output, second_back, feed_back, term = rowwise(
            output_kernel,
            (*attention_sums[b], *tensor_sum(*feed_parts[b]), cotangent_own[b]),
            rates_both,
            [F32, F32, LOW],
            True,
            deps,
        )
        outputs.append(output)
        second_backs.append(second_back)
        feed_rate_terms.append(term)
        feed_back_rows.append((feed_back, trade(feed_back, "tensor", 1)))

    def feed_part_back(b, deps):
        up_low, gate_low, terms, own_part, other_part = feed_backward(
            *feed_back_rows[b], ups[b], gates[b], feed_full, scale_up, scale_gate, deps
        )
        up_back_rows.append(up_low)
        gate_back_rows.append(gate_low)
        hidden_terms.append(terms)
        grad_sums.append(tensor_sum(own_part, other_part))

    def first_part_back(b, deps):
        skip, attention_back, term = rowwise(
            first_back_kernel,
            (*attention_sums[b], second_backs[b], *grad_sums[b]),
            rates_both,
            [F32, LOW],
            True,
            deps,
        )
        skips.append(skip)
        attention_rate_terms.append(term)
        attention_back_rows.append((attention_back, trade(attention_back, "tensor", 1)))

    def attention_part_back(b, deps):
        attention_grads.append(
            attend_back(
                head_count,
                places[b],
                query_low[b],
                key_values[b],
                attention_back_rows[b],
                output_weights,
                summeds[b],
                totals[b],
                deps,
            )
        )

    def to_owner(gradient, in_order):
        if not pair:
            summed_rows = lax.psum_scatter(gradient, "ctx", scatter_dimension=0, tiled=True)
            return (summed_rows, None, jnp.zeros((1,), jnp.int32))
        size = gradient.shape[0] // 2
        other = gradient[size:]
        block = jnp.zeros((1,), jnp.int32)
        if in_order:
            other = jnp.where(ctx_first, gradient[size:], gradient[:size])
            block = me.reshape(1)
        return (gradient, trade(other.astype(LOW), "ctx", 1), block)

    def feed_gradient(lefts, rights, deps):
        if not pair:
            right = jnp.concatenate([side for entry in rights for side in entry], axis=0)
            grad = to_owner(dot(jnp.concatenate(lefts, axis=0), right, (0, 0)), False)
            return (grad, grad[0])
        own, other = weight_grad(lefts, rights, deps)
        return ((own, trade(other, "ctx", 1), jnp.zeros((1,), jnp.int32)), own)

    triples, head_terms, input_sums = [], [], []

    def sides_part_back(b, deps):
        query_grad, own_grad, other_grad = attention_grads[b]
        arrived = None
        if pair:
            arrived = side_arrivals[b]
        else:
            sides = jnp.concatenate([own_grad[None], other_grad], axis=0)
            sides = jnp.take(sides, lax.rem(table - me + ctx_count, ctx_count), axis=0)
            own_grad = lax.psum_scatter(sides, "ctx", scatter_dimension=0)
        triple, terms = sides_back(
            head_count, own_grad, arrived, query_grad, projections[b], scale_column, deps
        )
        triples.append(triple)
        head_terms.append(terms)
        input_sums.append(tensor_sum(*to_rows(triple, triple_weights)))

    tag = feed_parts[-1][1]
    for b in micros:
        output_part(b, [tag])
        if b == last:
            down_grad, tag = feed_gradient(hidden_rows, feed_back_rows, [])
            first_part_back(0, [tag])
            tag = attention_rate_terms[0]
        feed_part_back(b, [tag])
        tag = hidden_terms[b]
    up_grad, tag = feed_gradient(up_back_rows, normed_rows, [tag])
    gate_grad, tag = feed_gradient(gate_back_rows, normed_rows, [tag])
    feed_steps = MatrixSteps(
        2 if own_units % 320 == 0 else 1,
        4 if own_units % 640 == 0 else 1,
        at_end,
        feedforward_weights,
        feedforward_first,
        feedforward_second,
        feedforward_outer,
    )
    attention_steps = MatrixSteps(
        1,
        1,
        at_end,
        attention_weights,
        attention_first,
        attention_second,
        attention_outer,
    )
    side_arrivals = []
    arrived_grads = {0: [down_grad[1]], 1: [up_grad[1]]} if pair else {}
    for b in micros:
        if b > 0:
            first_part_back(b, [tag])
            tag = attention_rate_terms[b]
        attention_part_back(b, [tag] + arrived_grads.get(b, []))
        tag = attention_grads[b][0]
        if pair:
            side_arrivals.append(trade(attention_grads[b][2][0], "ctx", 1))
        if b == last - 1:
            tag = feed_steps.inner(2, down_grad, [tag])
    if pair:
        own, other = triple_grad(me.reshape(1), 1, heads_lows, attention_back_rows, [tag])
        output_grad = (own, trade(other, "ctx", 1), jnp.zeros((1,), jnp.int32))
        output_arrived = [output_grad[1]]
        gate_arrived = [gate_grad[1]]
        tag = own
    else:
        right = jnp.concatenate([side for rows_of in attention_back_rows for side in rows_of], axis=0)
        output_grad = to_owner(dot(jnp.concatenate(heads_lows, axis=1), right, (1, 0)), True)
        output_arrived = []
        gate_arrived = []
    token_sides = [(token_own[b], token_other[b]) for b in micros]
    tag = feed_steps.inner(0, up_grad, [tag], False)
    tag = feed_steps.inner(
        1, gate_grad, [tag] + feed_steps.pairs(2)[:1] + side_arrivals[:1], False
    )
    for b in micros:
        deps = [tag]
        if b == 0:
            deps += feed_steps.pairs(2) + side_arrivals[1:2]
        elif b < last:
            deps += side_arrivals[-1:]
        else:
            deps += feed_steps.wholes(2)[:1] + output_arrived
        sides_part_back(b, deps)
        tag = head_terms[b]
    if pair:
        own, other = triple_grad(me.reshape(1), 3, triples, token_sides, [tag])
        tag = own
        arrived = trade(other, "ctx", 1)
        projection_grads = [
            (own, arrived, jnp.full((1,), which, jnp.int32)) for which in range(3)
        ]
    else:
        triple_all = dot(
            jnp.concatenate(triples, axis=1),
            jnp.concatenate([side for sides in token_sides for side in sides], axis=0),
            (1, 0),
        ).reshape(3, head_width, model_width)
        projection_grads = [to_owner(triple_all[which], True) for which in range(3)]
    tag = attention_steps.inner(3, output_grad, [tag] + feed_steps.wholes(2), False)

    block_output = None
    for b in micros:
        block_output = place_rows(
            b,
            micro_count,
            core_index,
            outputs[b],
            trade(outputs[b], "tensor", 1),
            block_output,
            [head_terms[0]],
        )

    input_gradient = None

    def place_input(b, deps):
        input_own = added([skips[b], *input_sums[b]], F32, deps)
        return place_rows(
            b,
            micro_count,
            core_index,
            input_own,
            trade(input_own, "tensor", 1),
            input_gradient,
            deps,
        )

    for which in range(3):
        tag = attention_steps.inner(which, projection_grads[which], [tag], False)
    tags = [tag]
    rate_terms = jnp.concatenate([sum(attention_rate_terms), sum(feed_rate_terms)], axis=0)
    rate_terms = rate_terms + trade(rate_terms, "tensor", 1)
    head_terms = sum(head_terms).reshape(head_width)
    hidden_terms = sum(hidden_terms)
    if pair:
        heads_own = jnp.where(ctx_first, head_terms[:own_rows], head_terms[own_rows:])
        heads_other = jnp.where(ctx_first, head_terms[own_rows:], head_terms[:own_rows])
        rates_own = jnp.where(ctx_first, rate_terms[:, :own_cols], rate_terms[:, own_cols:])
        rates_other = jnp.where(ctx_first, rate_terms[:, own_cols:], rate_terms[:, :own_cols])
        flat = jnp.concatenate(
            [heads_other, hidden_terms[:, own_units:].reshape(-1), rates_other.reshape(-1)]
        )
        flat = trade(flat, "ctx", 1)
        heads_grad = heads_own + flat[:own_rows]
        hidden_grad = hidden_terms[:, :own_units] + flat[
            own_rows : own_rows + 2 * own_units
        ].reshape(2, own_units)
        rates_grad = rates_own + flat[own_rows + 2 * own_units :].reshape(2, own_cols)
    else:
        heads_grad = lax.psum_scatter(head_terms, "ctx", scatter_dimension=0, tiled=True)
        hidden_grad = lax.psum_scatter(hidden_terms, "ctx", scatter_dimension=1, tiled=True)
        rates_grad = lax.psum_scatter(rate_terms, "ctx", scatter_dimension=1, tiled=True)

    masters = (head_scales, hidden_scales, residual_rates)
    firsts = (heads_first[0], hidden_first[0], rates_first[0])
    seconds = (heads_second[0], hidden_second[0], rates_second[0])
    outers = (heads_outer, hidden_outer, rates_outer)
    small_grads = (heads_grad, hidden_grad, rates_grad)
    small_moments, small_variances, small_shifts = [], [], []
    for which in range(3):
        moment, variance, updated = adam_step(
            masters[which],
            small_grads[which],
            firsts[which],
            seconds[which],
            SCALE_RATE,
            False,
        )
        small_moments.append(moment)
        small_variances.append(variance)
        small_shifts.append((masters[which] - updated).reshape(-1))
    shift_flat = jnp.concatenate(small_shifts)
    flat_size = shift_flat.size
    flat_rows = -(-flat_size // 1024) * 8
    shift_flat = jnp.pad(shift_flat, (0, flat_rows * 128 - flat_size)).reshape(flat_rows, 128)
    feed_shifts = feed_steps.shifts[0] + feed_steps.shifts[1]
    attention_shifts = attention_steps.shifts
    *chained, shift_flat = chain_sum(
        [*feed_shifts, *[attention_shifts[which][0] for which in (3, 0, 1, 2)], shift_flat], tags
    )
    shift_flat = shift_flat.reshape(-1)[:flat_size] / group_count
    for which in (0, 1):
        start = which * (len(feed_shifts) // 2)
        feed_steps.sums[which] = [
            (None, total, total) for total in chained[start : start + len(feed_shifts) // 2]
        ]
    for which, total in zip((3, 0, 1, 2), chained[len(feed_shifts) :]):
        attention_steps.sums[which] = [(None, total, total)]
    tags = [chained[0]]
    for which in (2, 0, 1):
        tags = feed_steps.outer(which, tags)
    for which in (3, 0, 1, 2):
        tags = attention_steps.outer(which, tags)
    for b in micros:
        input_gradient = place_input(b, [chained[0]])
    feed_outs = feed_steps.outs()
    attention_outs = attention_steps.outs()

    small_momenta, small_results = [], []
    start = 0
    for which in range(3):
        size = masters[which].size
        shift = shift_flat[start : start + size].reshape(masters[which].shape)
        start += size
        momentum, result = outer_step(masters[which], shift, outers[which], False)
        small_momenta.append(momentum)
        small_results.append(result)

    return (
        block_output,
        input_gradient,
        attention_outs[0],
        feed_outs[0],
        *[entry[None] for entry in small_grads],
        attention_outs[1],
        feed_outs[1],
        *[entry[None] for entry in small_moments],
        attention_outs[2],
        feed_outs[2],
        *[entry[None] for entry in small_variances],
        attention_outs[3],
        feed_outs[3],
        *small_momenta,
        attention_outs[4],
        feed_outs[4],
        *small_results,
    )


def solution(mesh):
    placed = (
        P("group", None, "ctx", None),
        P("group", None, "ctx", None),
        P("group", None, None),
        P(),
        P(None, ("tensor", "ctx"), None),
        P(None, ("tensor", "ctx"), None),
        P(("tensor", "ctx")),
        P(None, ("tensor", "ctx")),
        P(None, "ctx"),
        P("group", None, ("tensor", "ctx"), None),
        P("group", None, ("tensor", "ctx"), None),
        P("group", ("tensor", "ctx")),
        P("group", None, ("tensor", "ctx")),
        P("group", None, "ctx"),
        P("group", None, ("tensor", "ctx"), None),
        P("group", None, ("tensor", "ctx"), None),
        P("group", ("tensor", "ctx")),
        P("group", None, ("tensor", "ctx")),
        P("group", None, "ctx"),
        P(None, ("tensor", "ctx"), None),
        P(None, ("tensor", "ctx"), None),
        P(("tensor", "ctx")),
        P(None, ("tensor", "ctx")),
        P(None, "ctx"),
    )
    return jax.shard_map(
        on_device,
        mesh=mesh,
        in_specs=placed,
        out_specs=(
            P("group", None, "ctx", None),
            P("group", None, "ctx", None),
            P("group", None, ("tensor", "ctx"), None),
            P("group", None, ("tensor", "ctx"), None),
            P("group", ("tensor", "ctx")),
            P("group", None, ("tensor", "ctx")),
            P("group", None, "ctx"),
            P("group", None, ("tensor", "ctx"), None),
            P("group", None, ("tensor", "ctx"), None),
            P("group", ("tensor", "ctx")),
            P("group", None, ("tensor", "ctx")),
            P("group", None, "ctx"),
            P("group", None, ("tensor", "ctx"), None),
            P("group", None, ("tensor", "ctx"), None),
            P("group", ("tensor", "ctx")),
            P("group", None, ("tensor", "ctx")),
            P("group", None, "ctx"),
            P(None, ("tensor", "ctx"), None),
            P(None, ("tensor", "ctx"), None),
            P(("tensor", "ctx")),
            P(None, ("tensor", "ctx")),
            P(None, "ctx"),
            P(None, ("tensor", "ctx"), None),
            P(None, ("tensor", "ctx"), None),
            P(("tensor", "ctx")),
            P(None, ("tensor", "ctx")),
            P(None, "ctx"),
        ),
        check_vma=False,
    )
```
